128 devices in a mesh: seq: 32 (over z, y, core), head: 4 (over x).
Axes of the slice: x: 4, y: 4, z: 4, core: 2. Of those that a mesh axis runs over, the one named last changes fastest.
Arguments:
- hidden_in: bfloat16 [8192, 1024], P('seq'), may hold values from -6 to 6
- cotangent: bfloat16 [8192, 1024], P('seq'), may hold values from -6 to 6
- log_decay: float32 [8192, 24], P('seq', 'head'), may hold values from -2 to 0, as said below
- norm_gain: float32 [1024], replicated, may hold values from 0.25 to 1.75
- query_weight: bfloat16 [1024, 512], P(None, 'head'), may hold values from -0.1875 to 0.1875
- keyvalue_weight: bfloat16 [2, 1024, 128], replicated, may hold values from -0.1875 to 0.1875
- attention_output: bfloat16 [512, 1024], P('head'), may hold values from -2 to 2
- mixer_weight: bfloat16 [2, 1024, 1536], P(None, None, 'head'), may hold values from -0.1875 to 0.1875
- state_weight: bfloat16 [1024, 256], replicated, may hold values from -0.1875 to 0.1875
- kernel_mixer: float32 [4, 1536], P(None, 'head'), may hold values from -3 to 3
- kernel_state: float32 [4, 256], replicated, may hold values from -3 to 3
- bias_mixer: float32 [1536], P('head'), may hold values from -3 to 3
- bias_state: float32 [256], replicated, may hold values from -3 to 3
- skip_gain: float32 [24], P('head'), may hold values from 0.5 to 1.5
- mixer_gain: float32 [1536], P('head'), may hold values from 0.25 to 1.75
- mixer_output: bfloat16 [1536, 1024], P('head'), may hold values from -0.15625 to 0.15625
- second_gain: float32 [1024], replicated, may hold values from 0.25 to 1.75
- gate_up: bfloat16 [2, 1024, 2048], P(None, None, 'head'), may hold values from -0.1875 to 0.1875
- down_weight: bfloat16 [2048, 1024], P('head'), may hold values from -0.125 to 0.125
Outputs:
- block_out: float32 [8192, 1024], P('seq', 'head')
- input_grads: float32 [8192, 1024], P('seq', 'head')
- gain_grads: float32 [1024], replicated
- query_grads: float32 [1024, 512], P(None, 'head')
- keyvalue_grads: float32 [2, 1024, 128], replicated
- attention_grads: float32 [512, 1024], P('head')
- mixer_grads: float32 [2, 1024, 1536], P(None, None, 'head')
- state_grads: float32 [1024, 256], replicated
- mixkernel_grads: float32 [4, 1536], P(None, 'head')
- statekernel_grads: float32 [4, 256], replicated
- mixbias_grads: float32 [1536], P('head')
- statebias_grads: float32 [256], replicated
- skip_grads: float32 [24], P('head')
- mixgain_grads: float32 [1536], P('head')
- mixout_grads: float32 [1536, 1024], P('head')
- second_grads: float32 [1024], replicated
- gateup_grads: float32 [2, 1024, 2048], P(None, None, 'head')
- down_grads: float32 [2048, 1024], P('head')
The draws below stay inside these ranges and needn't reach their ends.
Inputs may be any that keep to these rules, and one draw needn't show every extreme that they name: `log_decay`: strictly negative; per token and Mamba head.
All inputs are finite; a program needn't handle non-finite values.
Results may differ from the reference program's by a relative error of at most 0.03.
Values may be sent and summed in bfloat16 or wider, within the bound.
A program may use at most 128 MiB of HBM per device.

```python
import jax
import jax.numpy as jnp
from jax import lax

D = 1024
FF = 2048
AH = 8
KVH = 2
HD = 64
MAMBA_HEADS = 24
MP = 64
NS = 128
KC = 4
LEN_DEV = 256
SEQUENCE_TOKENS = 8192


def draw_log_decay(key, part):
    key = jax.random.fold_in(key, 7)
    random_subkeys = jax.random.split(key, 7)
    fast_share = 0.4
    slow_top = 0.8
    fast_mask = jax.random.uniform(random_subkeys[0], (MAMBA_HEADS,)) < fast_share
    slow_rate = jnp.exp(jax.random.uniform(random_subkeys[1], (MAMBA_HEADS,), minval=jnp.log(0.1), maxval=jnp.log(slow_top))) / SEQUENCE_TOKENS
    fast_rate = jax.random.uniform(random_subkeys[2], (MAMBA_HEADS,), minval=1.0 / 50.0, maxval=1.0 / 30.0)
    baseline_rate = jnp.where(fast_mask, fast_rate, slow_rate)
    blocks = SEQUENCE_TOKENS // LEN_DEV
    block_multiplier = jnp.exp(jax.random.uniform(random_subkeys[3], (blocks, MAMBA_HEADS), minval=jnp.log(0.5), maxval=jnp.log(1.5)))
    block_multiplier = jnp.repeat(block_multiplier, LEN_DEV, axis=0)
    jitter_level = jax.random.uniform(random_subkeys[4], (SEQUENCE_TOKENS, MAMBA_HEADS), minval=0.5, maxval=1.5)
    spike_position = jax.random.randint(random_subkeys[5], (3, MAMBA_HEADS), 0, SEQUENCE_TOKENS)
    amplitude_values = jax.random.uniform(random_subkeys[6], (3, MAMBA_HEADS), minval=0.22, maxval=0.5)
    spike_hits = jnp.arange(SEQUENCE_TOKENS)[:, None, None] == spike_position[None]
    spike_value = jnp.sum(jnp.where(spike_hits, amplitude_values[None], 0.0), axis=1)
    return (-(baseline_rate[None, :] * block_multiplier * jitter_level + spike_value)).astype(jnp.float32)


def block_levels(own_key, shape, shards, smallest, largest):
    def one(position, shards_of):
        heights = jax.random.uniform(jax.random.fold_in(jax.random.fold_in(own_key, 6), position), (shards_of,), jnp.float32, smallest / len(shards), largest / len(shards))
        return jnp.repeat(jnp.exp(heights), shape[position] // shards_of).reshape((-1,) + (1,) * (len(shape) - position - 1))

    level = one(*shards[0])
    for cut in shards[1:]:
        level = level * one(*cut)
    return level


def centred(own_key, extent, width, limit, cuts=(), held_as=jnp.bfloat16):
    level = block_levels(own_key, extent, cuts, -0.22, 0.18) if cuts else 1.0
    entries = jax.random.normal(own_key, extent, jnp.float32) * width * level
    return jnp.minimum(jnp.maximum(entries, -limit), limit).astype(held_as)


def setup_inputs(seed: int = 0) -> dict:
    seeds = jax.random.split(jax.random.key(seed), 20)
    return {
        "hidden_in": centred(seeds[0], (SEQUENCE_TOKENS, D), 1.0, 6.0, ((0, 32),)),
        "cotangent": centred(seeds[1], (SEQUENCE_TOKENS, D), 1.0, 6.0, ((0, 32),)),
        "log_decay": draw_log_decay(jax.random.fold_in(seeds[19], 71), 0),
        "norm_gain": jnp.clip(1.0 + 0.15 * jax.random.normal(seeds[3], (D,), jnp.float32), 0.25, 1.75),
        "query_weight": centred(seeds[4], (D, AH * HD), D ** -0.5, 0.1875, ((1, 4),)),
        "keyvalue_weight": centred(seeds[5], (2, D, KVH * HD), D ** -0.5, 0.1875),
        "attention_output": centred(seeds[6], (AH * HD, D), (AH * HD // 64) ** -0.5, 2.0, ((0, 4),)),
        "mixer_weight": centred(seeds[7], (2, D, MAMBA_HEADS * MP), D ** -0.5, 0.1875, ((2, 4),)),
        "state_weight": centred(seeds[8], (D, 2 * NS), D ** -0.5, 0.1875),
        "kernel_mixer": centred(seeds[9], (KC, MAMBA_HEADS * MP), KC ** -0.5, 3.0, ((1, 4),), jnp.float32),
        "kernel_state": centred(seeds[10], (KC, 2 * NS), KC ** -0.5, 3.0, (), jnp.float32),
        "bias_mixer": centred(seeds[11], (MAMBA_HEADS * MP,), 0.5, 3.0, ((0, 4),), jnp.float32),
        "bias_state": centred(seeds[12], (2 * NS,), 0.5, 3.0, (), jnp.float32),
        "skip_gain": jnp.clip(0.5 + 1.0 * jax.random.uniform(seeds[13], (MAMBA_HEADS,), jnp.float32) ** block_levels(seeds[13], (MAMBA_HEADS,), ((0, 4),), -0.2, 0.2), 0.5, 1.5),
        "mixer_gain": jnp.clip(1.0 + 0.15 * jax.random.normal(seeds[14], (MAMBA_HEADS * MP,), jnp.float32), 0.25, 1.75),
        "mixer_output": centred(seeds[15], (MAMBA_HEADS * MP, D), (MAMBA_HEADS * MP) ** -0.5, 0.15625, ((0, 4),)),
        "second_gain": jnp.clip(1.0 + 0.15 * jax.random.normal(seeds[16], (D,), jnp.float32), 0.25, 1.75),
        "gate_up": centred(seeds[17], (2, D, FF), D ** -0.5, 0.1875, ((2, 4),)),
        "down_weight": centred(seeds[18], (FF, D), FF ** -0.5, 0.125, ((0, 4),)),
    }


HIGHEST = lax.Precision.HIGHEST
EPSILON = 1e-05

@jax.custom_vjp
def low(v):
    return lax.optimization_barrier(v.astype(jnp.bfloat16)).astype(jnp.float32)

@jax.custom_vjp
def low_back(v):
    return v

def low_keep(v):
    return (low(v), None)

def low_pass(kept, grad):
    return (grad,)

def back_keep(v):
    return (v, None)

def back_low(kept, grad):
    return (low(grad),)
low.defvjp(low_keep, low_pass)
low_back.defvjp(back_keep, back_low)

def exact_dot(left, right):
    return jnp.dot(left, right, precision=HIGHEST, preferred_element_type=jnp.float32)

def rms_scale(values):
    return lax.rsqrt(lax.optimization_barrier(jnp.mean(values * values, axis=-1, keepdims=True)) + EPSILON)

def causal_conv(signal, kernel, offset):
    kernel_width = kernel.shape[0]
    padded = jnp.concatenate([jnp.zeros((kernel_width - 1, signal.shape[1]), jnp.float32), signal], axis=0)
    summed = offset[None, :] + jnp.zeros_like(signal)
    for k in range(kernel_width):
        summed = summed + kernel[k][None, :] * padded[k:k + signal.shape[0]]
    return summed

def attention(queries, key_rows, values):
    length = queries.shape[0]
    group_size = AH // KVH
    key_all = jnp.repeat(key_rows, group_size, axis=1)
    value_all = jnp.repeat(values, group_size, axis=1)
    block_rows = min(512, length)
    score_scale = HD ** (-0.5)
    key_pos = jnp.arange(length).astype(jnp.int32)

    def one_block(first_row):
        query_rows = lax.dynamic_slice_in_dim(queries, first_row, block_rows, 0)
        scores = jnp.einsum('qhd,khd->hqk', query_rows, key_all, precision=HIGHEST) * score_scale
        query_pos = first_row + jnp.arange(block_rows).astype(jnp.int32)
        visible = key_pos[None, :] <= query_pos[:, None]
        scores = low_back(jnp.where(visible[None], scores, -1e+30))
        row_max = lax.optimization_barrier(jnp.max(scores, axis=2, keepdims=True))
        weights = jnp.exp(scores - row_max)
        prob_rows = low(weights / lax.optimization_barrier(jnp.sum(weights, axis=2, keepdims=True)))
        return jnp.einsum('hqk,khd->qhd', prob_rows, value_all, precision=HIGHEST)
    starts = (jnp.arange(length // block_rows) * block_rows).astype(jnp.int32)
    blocks = lax.map(jax.checkpoint(one_block), starts)
    return blocks.reshape(length, AH * HD)

def state_space(scaled_in, b_rows, c_rows, log_decay):
    length = scaled_in.shape[0]
    count = length // LEN_DEV
    pieces = (scaled_in.reshape(count, LEN_DEV, MAMBA_HEADS, MP), b_rows.reshape(count, LEN_DEV, NS), c_rows.reshape(count, LEN_DEV, NS), log_decay.reshape(count, LEN_DEV, MAMBA_HEADS))
    lower_mask = jnp.tril(jnp.ones((LEN_DEV, LEN_DEV), dtype=bool))

    def one_block(carry_state, piece):
        block_in, block_b, block_c, block_log = piece
        cum_log = jnp.cumsum(block_log, axis=0)
        gram_mat = exact_dot(block_c, block_b.T)
        diff = cum_log.T[:, :, None] - cum_log.T[:, None, :]
        decay_mat = jnp.where(lower_mask[None], jnp.exp(jnp.where(lower_mask[None], diff, 0.0)), 0.0)
        block_out = jnp.einsum('hts,shp->thp', gram_mat[None] * decay_mat, block_in, precision=HIGHEST)
        block_out = block_out + jnp.exp(cum_log)[:, :, None] * jnp.einsum('tn,hnp->thp', block_c, carry_state, precision=HIGHEST)
        tail_decay = jnp.exp(cum_log[-1][None, :] - cum_log)
        carry_state = jnp.exp(cum_log[-1])[:, None, None] * carry_state + jnp.einsum('sn,shp->hnp', block_b, block_in * tail_decay[:, :, None], precision=HIGHEST)
        return (carry_state, block_out)
    initial = jnp.zeros((MAMBA_HEADS, NS, MP), jnp.float32)
    _, outputs = lax.scan(jax.checkpoint(one_block), initial, pieces)
    return outputs.reshape(length, MAMBA_HEADS, MP)

def forward(hidden, norm_gain, query_weight, keyvalue_weight, attention_output, mixer_weight, state_weight, kernel_mixer, kernel_state, bias_mixer, bias_state, skip_gain, mixer_gain, mixer_output, second_gain, gate_up, down_weight, log_decay):
    length = hidden.shape[0]
    normed = low(hidden * rms_scale(hidden) * norm_gain)
    queries = low(low_back(exact_dot(normed, query_weight))).reshape(length, AH, HD)
    key_rows = low(exact_dot(normed, keyvalue_weight[0])).reshape(length, KVH, HD)
    values = low(exact_dot(normed, keyvalue_weight[1])).reshape(length, KVH, HD)
    attended = low(low_back(attention(queries, key_rows, values)))
    attn_branch = low_back(exact_dot(attended, attention_output))
    gate_z = low_back(exact_dot(normed, mixer_weight[0]))
    raw_mixer = low_back(exact_dot(normed, mixer_weight[1]))
    raw_state = exact_dot(normed, state_weight)
    mixer_in = low(jax.nn.silu(causal_conv(raw_mixer, kernel_mixer, bias_mixer))).reshape(length, MAMBA_HEADS, MP)
    state_in = low(jax.nn.silu(causal_conv(raw_state, kernel_state, bias_state)))
    step_size = -log_decay
    ssd_out = state_space(mixer_in * step_size[:, :, None], state_in[:, :NS], state_in[:, NS:], log_decay)
    ssd_out = ssd_out + skip_gain[None, :, None] * mixer_in
    mixed = ssd_out.reshape(length, MAMBA_HEADS * MP) * jax.nn.silu(gate_z)
    gated = low(mixed * rms_scale(mixed) * mixer_gain)
    mamba_branch = low_back(exact_dot(gated, mixer_output))
    residual = hidden + attn_branch + mamba_branch
    second_normed = low(residual * rms_scale(residual) * second_gain)
    gate_pre = low_back(exact_dot(second_normed, gate_up[0]))
    up_pre = low_back(exact_dot(second_normed, gate_up[1]))
    activation = low(jax.nn.silu(gate_pre) * up_pre)
    return residual + low_back(exact_dot(activation, down_weight))

def reference(hidden_in, cotangent, log_decay, norm_gain, query_weight, keyvalue_weight, attention_output, mixer_weight, state_weight, kernel_mixer, kernel_state, bias_mixer, bias_state, skip_gain, mixer_gain, mixer_output, second_gain, gate_up, down_weight):
    inputs_f = (hidden_in.astype(jnp.float32), norm_gain, query_weight.astype(jnp.float32), keyvalue_weight.astype(jnp.float32), attention_output.astype(jnp.float32), mixer_weight.astype(jnp.float32), state_weight.astype(jnp.float32), kernel_mixer, kernel_state, bias_mixer, bias_state, skip_gain, mixer_gain, mixer_output.astype(jnp.float32), second_gain, gate_up.astype(jnp.float32), down_weight.astype(jnp.float32))

    def wrapped(*arrays):
        return forward(*arrays, log_decay)
    block_out, pullback = jax.vjp(wrapped, *inputs_f)
    gradients = pullback(cotangent.astype(jnp.float32))
    return (block_out, gradients[0], gradients[1], gradients[2], gradients[3], gradients[4], gradients[5], gradients[6], gradients[7], gradients[8], gradients[9], gradients[10], gradients[11], gradients[12], gradients[13], gradients[14], gradients[15], gradients[16])
```

```python
import functools

import jax
import jax.numpy as jnp
from jax import lax
from jax.experimental import pallas as pl
from jax.experimental.pallas import tpu as pltpu
from jax.sharding import PartitionSpec as P

D = 1024
FF = 2048
AH = 8
KVH = 2
HD = 64
MAMBA_HEADS = 24
MP = 64
NS = 128
KC = 4
EPSILON = 1e-05
SEQ = 32
HEADS = 4
ROWS = 256
MW = 384
CW = 640
HMH = 6
HIGHEST = lax.Precision.HIGHEST
MESH = pl.DeviceIdType.MESH
F32 = jnp.float32
BF16 = jnp.bfloat16
VMEM_LIMIT = 50 * 1024 * 1024


def nn(a, b):
    return jnp.dot(a, b, preferred_element_type=F32)


def nt(a, b):
    return lax.dot_general(a, b, (((1,), (1,)), ((), ())), preferred_element_type=F32)


def tn(a, b):
    return lax.dot_general(a, b, (((0,), (0,)), ((), ())), preferred_element_type=F32)


def exact(a, b, dims):
    return lax.dot_general(
        a, b, (dims, ((), ())), precision=HIGHEST, preferred_element_type=F32
    )


def sigmoid(v):
    return 1.0 / (1.0 + jnp.exp(-v))


def shape(dims, kind):
    return jax.ShapeDtypeStruct(dims, kind)


def seq_bits(s):
    core, y, z = s % 2, (s // 2) % 4, s // 8
    return {
        "c": core,
        "ya": (y + y // 2) % 2,
        "yb": y // 2,
        "za": (z + z // 2) % 2,
        "zb": z // 2,
    }


SEQ_PATHS = (
    ("c", "ya", "yb", "za", "zb"),
    ("c", "yb", "ya", "zb", "za"),
    ("c", "za", "zb", "ya", "yb"),
    ("c", "zb", "za", "yb", "ya"),
)
HEAD_PATHS = (("xa", "xb"), ("xb", "xa"))


def position(bits, path):
    at = 0
    for name in path:
        at = at * 2 + bits[name]
    return at


def block_position(s, p):
    return position(seq_bits(s), SEQ_PATHS[p])


def head_position(h, p):
    bits = {"xa": (h + h // 2) % 2, "xb": h // 2}
    return position(bits, HEAD_PATHS[p])


class Links:
    def __init__(self, send_sem, recv_sem):
        s, h = lax.axis_index("seq"), lax.axis_index("head")
        self.s, self.h = s, h
        core, y, z = s % 2, (s // 2) % 4, s // 8
        self.bits = seq_bits(s)
        self.bits["xa"] = (h + h // 2) % 2
        self.bits["xb"] = h // 2
        self.partner = {
            "c": (s + 1 - 2 * core, h),
            "ya": (s + 2 * (1 - 2 * (y % 2)), h),
            "yb": (s + 2 * (3 - 2 * y), h),
            "za": (s + 8 * (1 - 2 * (z % 2)), h),
            "zb": (s + 8 * (3 - 2 * z), h),
            "xa": (s, h + 1 - 2 * (h % 2)),
            "xb": (s, 3 - h),
            "x1": (s, (h + 1) % HEADS),
            "x2": (s, (h + 2) % HEADS),
            "x3": (s, (h + 3) % HEADS),
            "next": ((s + 1) % SEQ, h),
            "prev": ((s + SEQ - 1) % SEQ, h),
        }
        self.send_sem, self.recv_sem, self.used = send_sem, recv_sem, 0

    def barrier(self, names):
        semaphore = pltpu.get_barrier_semaphore()
        for name in names:
            pl.semaphore_signal(
                semaphore, inc=1, device_id=self.partner[name], device_id_type=MESH
            )
        pl.semaphore_wait(semaphore, len(names))

    def send(self, src, dst, name):
        k = self.used
        self.used += 1
        copy = pltpu.make_async_remote_copy(
            src_ref=src,
            dst_ref=dst,
            send_sem=self.send_sem.at[k],
            recv_sem=self.recv_sem.at[k],
            device_id=self.partner[name],
            device_id_type=MESH,
        )
        copy.start()
        return copy


SEQ_NAMES = ("c", "ya", "yb", "za", "zb")


def rows_at(start, count, unit=16):
    return pl.ds(pl.multiple_of(start, unit), count)


class Reduce:
    def __init__(self, links, path, rows, src, src_base, work, recv, out, base):
        self.links, self.path, self.rows = links, path, rows
        self.src, self.src_base = src, src_base
        self.work, self.recv, self.out, self.base = work, recv, out, base
        self.start = 0
        self.copy = None

    def begin(self, step):
        name = self.path[step]
        half = self.rows >> (step + 1)
        bit = self.links.bits[name]
        away = self.start + (1 - bit) * half
        ref, at = (self.src, self.src_base) if step == 0 else (self.work, self.base)
        landing = self.base + self.rows - (self.rows >> step)
        self.copy = self.links.send(
            ref.at[rows_at(at + away, half)], self.recv.at[pl.ds(landing, half)], name
        )

    def finish(self, step):
        name = self.path[step]
        half = self.rows >> (step + 1)
        keep = self.start + self.links.bits[name] * half
        ref, at = (self.src, self.src_base) if step == 0 else (self.work, self.base)
        landing = self.base + self.rows - (self.rows >> step)
        last = step == len(self.path) - 1
        target, offset = (self.out, self.base) if last and self.out is not None else (self.work, self.base)
        self.copy.wait()
        chunk = min(half, 32)

        def add(i, carry):
            own = ref[rows_at(at + keep + i * chunk, chunk)].astype(F32)
            other = self.recv[rows_at(landing + i * chunk, chunk)].astype(F32)
            target[rows_at(offset + keep + i * chunk, chunk)] = (own + other).astype(BF16)
            return carry

        lax.fori_loop(0, half // chunk, add, 0)
        self.start = keep

    def send_back(self, step, columns=None):
        name = self.path[step]
        size = self.rows >> (step + 1)
        at = rows_at(self.base + self.start, size, min(size, 16))
        ref = self.out.at[at] if columns is None else self.out.at[at, pl.ds(0, columns)]
        self.copy = self.links.send(ref, ref, name)

    def wait_back(self, step):
        size = self.rows >> (step + 1)
        self.copy.wait()
        self.start = self.start - self.links.bits[self.path[step]] * size


def reduce_all(jobs):
    for job in jobs:
        job.begin(0)
    for step in range(max(len(job.path) for job in jobs)):
        for job in jobs:
            if step < len(job.path):
                job.finish(step)
                if step + 1 < len(job.path):
                    job.begin(step + 1)


def gather_all(jobs, columns=None):
    columns = columns or [None] * len(jobs)
    for job, width in zip(jobs, columns):
        job.send_back(len(job.path) - 1, width)
    for step in range(max(len(job.path) for job in jobs) - 1, -1, -1):
        for job, width in zip(jobs, columns):
            if step < len(job.path):
                job.wait_back(step)
                if step:
                    job.send_back(step - 1, width)


def call(body, outs, args, scratch=(), collective=None, smem=0, copies=0, cost=None):
    vm = pl.BlockSpec(memory_space=pltpu.VMEM)
    scratch = list(scratch)
    if copies:
        scratch += [pltpu.SemaphoreType.DMA((copies,)), pltpu.SemaphoreType.DMA((copies,))]
    if collective is None:
        params = pltpu.CompilerParams(vmem_limit_bytes=VMEM_LIMIT)
    else:
        params = pltpu.CompilerParams(
            vmem_limit_bytes=VMEM_LIMIT, collective_id=collective, has_side_effects=True
        )
    in_specs = [pl.BlockSpec(memory_space=pltpu.SMEM)] * smem + [vm] * (len(args) - smem)
    return pl.pallas_call(
        body,
        out_shape=tuple(outs),
        in_specs=in_specs,
        out_specs=tuple(vm for _ in outs),
        scratch_shapes=scratch,
        compiler_params=params,
    )(*args)


class Gather:
    def __init__(self, links, path, piece, out, base):
        self.links, self.path, self.piece, self.out, self.base = links, path, piece, out, base
        self.start = position(links.bits, path) * piece
        self.rows = piece << len(path)

    send_back = Reduce.send_back
    wait_back = Reduce.wait_back


def gather_rows(links, src, out, paths=SEQ_PATHS):
    piece = src.shape[0] // len(paths)
    jobs = []
    for p, path in enumerate(paths):
        job = Gather(links, path, piece, out, p * (piece << len(path)))
        own = rows_at(job.base + job.start, piece, 8 if piece == 8 else 16)
        out[own] = src[pl.ds(p * piece, piece)]
        jobs.append(job)
    return jobs


def keyval_kernel(kv, edge, logs, kv_all, edge_in, logs_all, send_sem, recv_sem):
    links = Links(send_sem, recv_sem)
    jobs = gather_rows(links, kv, kv_all) + gather_rows(links, logs, logs_all, SEQ_PATHS[:1])
    links.barrier(SEQ_NAMES + ("next", "prev"))
    edge_copy = links.send(edge, edge_in, "next")
    gather_all(jobs)
    edge_copy.wait()


def state_kernel(state, state_all, send_sem, recv_sem):
    links = Links(send_sem, recv_sem)
    jobs = gather_rows(links, state, state_all)
    links.barrier(SEQ_NAMES)
    gather_all(jobs)


def sums_kernel(part, total, slots, send_sem, recv_sem):
    links = Links(send_sem, recv_sem)
    slots[links.h] = part[...]
    links.barrier(("x1", "x2", "x3"))
    copies = [links.send(part, slots.at[links.h], name) for name in ("x1", "x2", "x3")]
    for copy in copies:
        copy.wait()
    total[...] = (slots[0] + slots[1]) + (slots[2] + slots[3])


def head_sum_kernel(part, total, work, recv, send_sem, recv_sem):
    links = Links(send_sem, recv_sem)
    links.barrier(("xa", "xb"))
    jobs = [
        Reduce(links, path, 128, part, 128 * p, work, recv, total, 128 * p)
        for p, path in enumerate(HEAD_PATHS)
    ]
    reduce_all(jobs)
    gather_all(jobs)


def own_rows(job, count):
    return job.work[rows_at(job.base + job.start, count)]


def second_sum_kernel(part, wide, total, share, work, recv, wide_work, wide_recv, send_sem, recv_sem):
    links = Links(send_sem, recv_sem)
    links.barrier(("xa", "xb"))
    sums = [
        Reduce(links, path, 128, part, 128 * p, work, recv, total, 128 * p)
        for p, path in enumerate(HEAD_PATHS)
    ]
    shares = [
        Reduce(links, path, 512, wide, 512 * p, wide_work, wide_recv, None, 512 * p)
        for p, path in enumerate(HEAD_PATHS)
    ]
    reduce_all(sums + shares)
    gather_all(sums)
    for p, job in enumerate(shares):
        share[pl.ds(128 * p, 128)] = own_rows(job, 128)


def pair_kernel(pairs, edge, own, edge_in, work, recv, send_sem, recv_sem):
    links = Links(send_sem, recv_sem)
    links.barrier(SEQ_NAMES + ("next", "prev"))
    edge_copy = links.send(edge, edge_in, "prev")
    jobs = [
        Reduce(links, path, 2048, pairs, 2048 * p, work, recv, None, 2048 * p)
        for p, path in enumerate(SEQ_PATHS)
    ]
    reduce_all(jobs)
    for p, job in enumerate(jobs):
        own[pl.ds(64 * p, 64)] = own_rows(job, 64)
    edge_copy.wait()


def final_kernel(
    xf, xb, ms, wide, small,
    x_out, ms_out, share, small_out,
    x_work, x_recv, ms_work, ms_recv, wide_work, wide_recv, head_slots, small_y, small_z, small_x,
    small_work, small_recv, send_sem, recv_sem,
):
    links = Links(send_sem, recv_sem)
    links.barrier(SEQ_NAMES + ("xa", "xb", "x1", "x2", "x3"))
    x_jobs = [
        Reduce(
            links, path, 512, xf if p < 3 else xb, 512 * p if p < 3 else 0,
            x_work, x_recv, x_out, 512 * p,
        )
        for p, path in enumerate(SEQ_PATHS)
    ]
    ms_jobs = [
        Reduce(links, path, 512, ms, 512 * p, ms_work, ms_recv, None, 512 * p)
        for p, path in enumerate(SEQ_PATHS)
    ]
    shares = [
        Reduce(links, path, 512, wide, 512 * p, wide_work, wide_recv, None, 512 * p)
        for p, path in enumerate(HEAD_PATHS)
    ]
    small_work[0] = small[...]
    small_steps = ("c", "ya", "yb", "za", "zb")
    reduce_all(shares)
    for p, job in enumerate(shares):
        share[pl.ds(128 * p, 128)] = own_rows(job, 128)
    for step, name in enumerate(small_steps):
        copy = links.send(small_work.at[step], small_recv.at[step], name)
        copy.wait()
        small_work[step + 1] = small_work[step] + small_recv[step]
    small_x[links.h] = small_work[5]
    small_copies = [links.send(small_work.at[5], small_x.at[links.h], n) for n in ("x1", "x2", "x3")]
    reduce_all(x_jobs + ms_jobs)
    head_copies = []
    for p, job in enumerate(ms_jobs):
        at = rows_at(job.base + job.start, 16)
        if p < 2:
            piece = ms_work[at, pl.ds(384, 256)]
        else:
            piece = jnp.concatenate([ms_work[at, pl.ds(512, 128)]] * 2, axis=1)
        head_slots[links.h, pl.ds(16 * p, 16)] = piece
    slot = head_slots.at[links.h]
    head_copies = [links.send(slot, slot, n) for n in ("x1", "x2", "x3")]
    for copy in small_copies:
        copy.wait()
    total = (small_x[0] + small_x[1]) + (small_x[2] + small_x[3])
    row = lax.broadcasted_iota(jnp.int32, (8, 1024), 0)
    small_out[...] = jnp.where(row < 4, total, small_work[5])
    for copy in head_copies:
        copy.wait()
    for p, job in enumerate(ms_jobs):
        job.out = ms_out
        at = rows_at(job.base + job.start, 16)
        parts = [head_slots[k, pl.ds(16 * p, 16)].astype(F32) for k in range(HEADS)]
        if p < 2:
            ms_out[at, pl.ds(0, 384)] = ms_work[at, pl.ds(0, 384)]
            ms_out[at, pl.ds(384, 256)] = ((parts[0] + parts[1]) + (parts[2] + parts[3])).astype(BF16)
        else:
            ms_out[at, pl.ds(0, 512)] = ms_work[at, pl.ds(0, 512)]
            ms_out[at, pl.ds(512, 128)] = (parts[0] + parts[1])[:, :128].astype(BF16)
            ms_out[at, pl.ds(640, 128)] = (parts[2] + parts[3])[:, :128].astype(BF16)
    gather_all(x_jobs + ms_jobs, [None] * 4 + [640, 640, None, None])


def project_kernel(x_ref, gain, wq, wkv, wm, ws, normed, q, kv, gz, raw):
    x = x_ref[...].astype(F32)
    r1 = lax.rsqrt(jnp.mean(x * x, axis=1, keepdims=True) + EPSILON)
    n = (x * r1 * gain[...]).astype(BF16)
    normed[...] = n
    q[...] = nn(n, wq[...]).astype(BF16)
    kv[...] = nn(n, wkv[...]).astype(BF16)
    gz[...] = nn(n, wm[0])
    raw[:, pl.ds(0, MW)] = nn(n, wm[1])
    raw[:, pl.ds(MW, 256)] = nn(n, ws[...])


def widen(values):
    lane = lax.broadcasted_iota(jnp.int32, (8, MW), 1)
    row = lax.broadcasted_iota(jnp.int32, (8, MW), 0)
    spread = jnp.where((lane >= row * MP) & (lane < row * MP + MP), 1.0, 0.0)
    return exact(values, spread, ((1,), (0,)))


def decay_terms(step_ref, cum_ref):
    cum = cum_ref[...]
    step_x = widen(step_ref[...])
    cum_x = widen(cum)
    enter_x = jnp.exp(cum_x)
    tail_x = jnp.exp(cum_x[ROWS - 1 : ROWS, :] - cum_x)
    return step_x, enter_x, tail_x


def conv_kernel(idx, raw, edge, taps, bias, step, cum, pre, post, state, ext):
    keep = jnp.where(idx[0] > 0, 1.0, 0.0)
    ext[pl.ds(0, 8)] = edge[...] * keep
    ext[pl.ds(8, ROWS)] = raw[...]
    for c in range(5):
        lanes = pl.ds(128 * c, 128)
        total = bias[:, lanes] + taps[pl.ds(0, 1), lanes] * ext[pl.ds(5, ROWS), lanes]
        for k in range(1, KC):
            total = total + taps[pl.ds(k, 1), lanes] * ext[pl.ds(5 + k, ROWS), lanes]
        pre[:, lanes] = total
        post[:, lanes] = (total * sigmoid(total)).astype(BF16)
    step_x, _, tail_x = decay_terms(step, cum)
    tail_in = (post[:, pl.ds(0, MW)].astype(F32) * step_x * tail_x).astype(BF16)
    state[...] = tn(tail_in, post[:, pl.ds(MW, NS)]).astype(BF16)


def chain(idx, gathered, logs, total, forward):
    s = idx[0]
    total[...] = jnp.zeros_like(total)

    def hop(i, run):
        j = s - 1 - i if forward else s + 1 + i
        weight = jnp.exp(run)
        for seg in range(12):
            p, off = seg // 3, (seg % 3) * 32
            at = rows_at(p * 3072 + block_position(j, p) * 96 + off, 32)
            h = seg // 2
            total[pl.ds(32 * seg, 32)] += weight[h : h + 1, :] * gathered[at].astype(F32)
        return run + logs[rows_at(block_position(j, 0) * 8, 8, 8)]

    lax.fori_loop(0, s if forward else SEQ - 1 - s, hop, jnp.zeros((8, 128), F32))


def lower_mask():
    t = lax.broadcasted_iota(jnp.int32, (ROWS, ROWS), 0)
    u = lax.broadcasted_iota(jnp.int32, (ROWS, ROWS), 1)
    return u <= t


def decay_of(cum, cum_t, h, mask):
    diff = cum[:, h : h + 1] - cum_t[h : h + 1, :]
    return jnp.exp(jnp.where(mask, diff, -1e30))


def row_sums(values):
    return exact(jnp.ones((8, values.shape[1]), F32), values, ((1,), (1,)))


def column_of(rows):
    return exact(rows, jnp.full((8, 128), 0.125, F32), ((0,), (0,)))[:, 0:1]


def ssd_kernel(
    idx, post, step, cum_ref, cumt_ref, skip, gz, gathered, logs, ssd, mixed, squares, state, total
):
    chain(idx, gathered, logs, total, True)
    state[...] = total[...].astype(BF16)
    step_x, enter_x, _ = decay_terms(step, cum_ref)
    mixer_in = post[:, pl.ds(0, MW)].astype(F32)
    scaled = (mixer_in * step_x).astype(BF16)
    b, c = post[:, pl.ds(MW, NS)], post[:, pl.ds(MW + NS, NS)]
    gram = nt(c, b)
    mask = lower_mask()
    cum, cum_t = cum_ref[...], cumt_ref[...]
    left = lax.broadcasted_iota(jnp.int32, (ROWS, 128), 1) < MP
    carried = enter_x * nt(c, state[...]) + skip[...] * mixer_in
    for pair in range(3):
        lanes = slice(128 * pair, 128 * pair + 128)
        first = nn((gram * decay_of(cum, cum_t, 2 * pair, mask)).astype(BF16), scaled[:, lanes])
        second = nn((gram * decay_of(cum, cum_t, 2 * pair + 1, mask)).astype(BF16), scaled[:, lanes])
        ssd[:, pl.ds(128 * pair, 128)] = jnp.where(left, first, second) + carried[:, lanes]
    z = gz[...]
    m = ssd[...] * (z * sigmoid(z))
    mixed[...] = m
    squares[...] = row_sums(m * m)


def outputs_kernel(mixed, squares, mgain, wmo, attended, wao, gated, part):
    scale = lax.rsqrt(column_of(squares[...]) / (MAMBA_HEADS * MP) + EPSILON)
    g = (mixed[...] * scale * mgain[...]).astype(BF16)
    gated[...] = g
    for c in range(2):
        lanes = pl.ds(512 * c, 512)
        part[:, lanes] = (nn(attended[...], wao[:, lanes]) + nn(g, wmo[:, lanes])).astype(BF16)


def load_block(kv_all, j):
    return jnp.concatenate(
        [kv_all[rows_at(2048 * p + block_position(j, p) * 64, 64)] for p in range(4)], axis=0
    )


def causal(block):
    key = lax.broadcasted_iota(jnp.int32, block.shape, 0)
    query = lax.broadcasted_iota(jnp.int32, block.shape, 1)
    query = jnp.where(query >= ROWS, query - ROWS, query)
    return jnp.where(key <= query, block, -1e30)


def stacked_queries(q):
    q = q.astype(F32) * (HD ** -0.5)
    left = lax.broadcasted_iota(jnp.int32, (ROWS, 128), 1) < HD
    first = jnp.where(left, q, 0.0)
    second = jnp.where(left, pltpu.roll(q, HD, 1), 0.0)
    return jnp.concatenate([first, second], axis=0).astype(BF16)


def attend_kernel(idx, q, kv_all, attended, attended_f, totals, qp, acc):
    s = idx[0]
    qp[...] = stacked_queries(q[...])
    block = load_block(kv_all, s)
    scores = causal(nt(block, qp[...]))
    high = jnp.max(scores, axis=0, keepdims=True)
    weights = jnp.exp(scores - high)
    acc[...] = tn(block, weights.astype(BF16))

    def hop(j, running):
        high, total = running
        block = load_block(kv_all, j)
        scores = nt(block, qp[...])
        new = jnp.maximum(high, jnp.max(scores, axis=0, keepdims=True))
        fade = jnp.exp(high - new)
        weights = jnp.exp(scores - new)
        acc[...] = acc[...] * fade + tn(block, weights.astype(BF16))
        return new, total * fade + jnp.sum(weights, axis=0, keepdims=True)

    high, total = lax.fori_loop(0, s, hop, (high, jnp.sum(weights, axis=0, keepdims=True)))
    out = acc[pl.ds(HD, HD)] / total
    out = jnp.concatenate([out[:, :ROWS], out[:, ROWS:]], axis=0).T
    attended_f[...] = out
    attended[...] = out.astype(BF16)
    totals[...] = jnp.broadcast_to(high + jnp.log(total), totals.shape)


def attend_back_kernel(idx, q, kv_all, d_att, attended_f, totals, d_q, pairs, qp, dop, acc):
    s = idx[0]
    qp[...] = stacked_queries(q[...])
    d_out = d_att[...].astype(F32)
    left = lax.broadcasted_iota(jnp.int32, (ROWS, 128), 1) < HD
    first = jnp.where(left, 0.0, pltpu.roll(d_out, HD, 1))
    second = jnp.where(left, 0.0, d_out)
    dop[...] = jnp.concatenate([first, second], axis=0).astype(BF16)
    product = (d_out * attended_f[...]).T
    delta = jnp.concatenate(
        [
            jnp.sum(product[:HD], axis=0, keepdims=True),
            jnp.sum(product[HD:], axis=0, keepdims=True),
        ],
        axis=1,
    )
    total = totals[pl.ds(0, 1)]
    pairs[...] = jnp.zeros_like(pairs)

    def step(j, masked):
        block = load_block(kv_all, j)
        scores = nt(block, qp[...])
        if masked:
            scores = causal(scores)
        probs = jnp.exp(scores - total)
        d_probs = nt(block, dop[...])
        d_scores = (probs * (d_probs - delta)).astype(BF16)
        d_pair = (nn(d_scores, qp[...]) + nn(probs.astype(BF16), dop[...])).astype(BF16)
        for p in range(4):
            at = rows_at(2048 * p + block_position(j, p) * 64, 64)
            pairs[at] = d_pair[64 * p : 64 * p + 64]
        return tn(block, d_scores)

    acc[...] = step(s, True)

    def hop(j, carry):
        acc[...] += step(j, False)
        return carry

    lax.fori_loop(0, s, hop, 0)
    out = acc[pl.ds(0, HD)] * (HD ** -0.5)
    d_q[...] = jnp.concatenate([out[:, :ROWS], out[:, ROWS:]], axis=0).T.astype(BF16)


def put_wide(wide, values):
    for j in range(HEADS):
        for p in range(2):
            at = 512 * p + int(head_position(j, p)) * 128
            wide[pl.ds(at, 128)] = values[128 * p : 128 * p + 128, 256 * j : 256 * j + 256].astype(BF16)


def feed_kernel(x_ref, summed, cot_ref, gain, gu, dw, wide, back, xf, second_part, sn, out_acc, d_acc):
    residual = x_ref[...].astype(F32) + summed[...].astype(F32)
    r2 = lax.rsqrt(jnp.mean(residual * residual, axis=1, keepdims=True) + EPSILON)
    sn[...] = (residual * r2 * gain[...]).astype(BF16)
    out_acc[...] = jnp.zeros_like(out_acc)
    d_acc[...] = jnp.zeros_like(d_acc)

    def part(c, carry):
        cols = pl.ds(pl.multiple_of(c * 256, 256), 256)
        high = pl.ds(pl.multiple_of(c * 256 + 512, 256), 256)
        wg, wu, wd = gu[0, :, cols], gu[1, :, cols], dw[cols]
        gate, up = nn(sn[...], wg), nn(sn[...], wu)
        sig = sigmoid(gate)
        act_gate = gate * sig
        act = (act_gate * up).astype(BF16)
        out_acc[...] += nn(act, wd)
        xf[cols] = tn(act, cot_ref[...]).astype(BF16)
        d_act = nt(cot_ref[...], wd)
        d_gate = (d_act * up * (sig * (1.0 + gate * (1.0 - sig)))).astype(BF16)
        d_up = (d_act * act_gate).astype(BF16)
        xf[pl.ds(512, 1024), cols] = tn(sn[...], d_gate).astype(BF16)
        xf[pl.ds(512, 1024), high] = tn(sn[...], d_up).astype(BF16)
        d_acc[...] += nt(d_gate, wg) + nt(d_up, wu)
        return carry

    lax.fori_loop(0, 2, part, 0)
    put_wide(wide, out_acc[...])
    d_second = d_acc[...]
    residual = x_ref[...].astype(F32) + summed[...].astype(F32)
    second_part[...] = jnp.broadcast_to(
        jnp.sum(d_second * residual * r2, axis=0, keepdims=True), second_part.shape
    )
    weighted = d_second * gain[...]
    inner = jnp.sum(weighted * residual, axis=1, keepdims=True)
    back[...] = (r2 * weighted - residual * (r2 * r2 * r2 / D * inner)).astype(BF16)


def lower_kernel(cot, d_sum, gated, attended, wmo, wao, mixed, squares, mgain, xb, d_att, d_gated, mixgain, inner):
    low = (cot[...].astype(F32) + d_sum[...].astype(F32)).astype(BF16)
    for c in range(2):
        lanes = slice(512 * c, 512 * c + 512)
        xb[pl.ds(0, MW), pl.ds(512 * c, 512)] = tn(gated[...], low[:, lanes]).astype(BF16)
        xb[pl.ds(MW, 128), pl.ds(512 * c, 512)] = tn(attended[...], low[:, lanes]).astype(BF16)
    d_att[...] = nt(low, wao[...]).astype(BF16)
    dg = nt(low, wmo[...])
    d_gated[...] = dg
    scale = lax.rsqrt(column_of(squares[...]) / (MAMBA_HEADS * MP) + EPSILON)
    product = dg * mixed[...]
    mixgain[...] = jnp.broadcast_to(jnp.sum(product * scale, axis=0, keepdims=True), mixgain.shape)
    inner[...] = row_sums(product * mgain[...])


def ssd_back_kernel(
    d_gated, mixed, squares, inner, mgain, gz, ssd, post, step, cum_ref, cumt_ref, state,
    d_z, d_ssd, skip_part, d_scaled, d_bc, grad_state,
):
    scale = lax.rsqrt(column_of(squares[...]) / (MAMBA_HEADS * MP) + EPSILON)
    inner_col = column_of(inner[...])
    d_mixed = scale * (d_gated[...] * mgain[...]) - mixed[...] * (
        scale * scale * scale / (MAMBA_HEADS * MP) * inner_col
    )
    z = gz[...]
    sig = sigmoid(z)
    ds = d_mixed * (z * sig)
    d_ssd[...] = ds
    d_z[...] = (d_mixed * ssd[...] * (sig * (1.0 + z * (1.0 - sig)))).astype(BF16)
    step_x, enter_x, _ = decay_terms(step, cum_ref)
    mixer_in = post[:, pl.ds(0, MW)].astype(F32)
    skip_part[...] = jnp.broadcast_to(jnp.sum(ds * mixer_in, axis=0, keepdims=True), skip_part.shape)
    scaled = (mixer_in * step_x).astype(BF16)
    b, c = post[:, pl.ds(MW, NS)], post[:, pl.ds(MW + NS, NS)]
    gram = nt(c, b)
    mask = lower_mask()
    cum, cum_t = cum_ref[...], cumt_ref[...]
    left = lax.broadcasted_iota(jnp.int32, (ROWS, 128), 1) < MP
    low = ds.astype(BF16)
    d_gram = jnp.zeros((ROWS, ROWS), F32)
    for pair in range(3):
        lanes = slice(128 * pair, 128 * pair + 128)
        halves = []
        for k in range(2):
            decay = decay_of(cum, cum_t, 2 * pair + k, mask)
            here = left if k == 0 else jnp.logical_not(left)
            mine = jnp.where(here, ds[:, lanes], 0.0).astype(BF16)
            halves.append(tn((gram * decay).astype(BF16), low[:, lanes]))
            d_gram = d_gram + decay * nt(mine, scaled[:, lanes])
        d_scaled[:, pl.ds(128 * pair, 128)] = jnp.where(left, halves[0], halves[1])
    entered = (ds * enter_x).astype(BF16)
    grad_state[...] = tn(entered, c).astype(BF16)
    d_gram = d_gram.astype(BF16)
    d_bc[:, pl.ds(0, NS)] = tn(d_gram, c)
    d_bc[:, pl.ds(NS, NS)] = nn(d_gram, b) + nn(entered, state[...])


def conv_back_kernel(
    idx, gathered, logs, d_ssd, d_scaled, d_bc, skip, step, cum, post, pre, raw, edge,
    d_pre, kernel_grads, total, ext,
):
    chain(idx, gathered, logs, total, False)
    leaving = total[...].astype(BF16)
    step_x, _, tail_x = decay_terms(step, cum)
    b = post[:, pl.ds(MW, NS)]
    mixer_in = post[:, pl.ds(0, MW)].astype(F32)
    tail_in = (mixer_in * step_x * tail_x).astype(BF16)
    scaled_grad = d_scaled[...] + tail_x * nt(b, leaving)
    d_pre[:, pl.ds(0, MW)] = skip[...] * d_ssd[...] + scaled_grad * step_x
    d_pre[:, pl.ds(MW, NS)] = d_bc[:, pl.ds(0, NS)] + nn(tail_in, leaving)
    d_pre[:, pl.ds(MW + NS, NS)] = d_bc[:, pl.ds(NS, NS)]
    keep = jnp.where(idx[0] > 0, 1.0, 0.0)
    ext[pl.ds(0, 8)] = edge[...] * keep
    ext[pl.ds(8, ROWS)] = raw[...]
    for c in range(5):
        lanes = pl.ds(128 * c, 128)
        v = pre[:, lanes]
        sig = sigmoid(v)
        dp = d_pre[:, lanes] * (sig * (1.0 + v * (1.0 - sig)))
        d_pre[:, lanes] = dp
        rows = [jnp.sum(dp * ext[pl.ds(5 + k, ROWS), lanes], axis=0, keepdims=True) for k in range(KC)]
        rows.append(jnp.sum(dp, axis=0, keepdims=True))
        rows.append(jnp.zeros((3, 128), F32))
        kernel_grads[:, lanes] = jnp.concatenate(rows, axis=0)


def input_back_kernel(
    idx, d_pre, edge, taps, d_z, d_q, pair, normed, x_ref, gain, wm, ws, wq, wkv,
    ms, wide, first_part, ext, d_all, acc,
):
    keep = jnp.where(idx[0] < SEQ - 1, 1.0, 0.0)
    ext[pl.ds(0, ROWS)] = d_pre[...]
    ext[pl.ds(ROWS, 8)] = edge[...] * keep
    d_all[:, pl.ds(0, MW)] = d_z[...]
    for c in range(5):
        lanes = pl.ds(128 * c, 128)
        total = taps[pl.ds(0, 1), lanes] * ext[pl.ds(3, ROWS), lanes]
        for k in range(1, KC):
            total = total + taps[pl.ds(k, 1), lanes] * ext[pl.ds(3 - k, ROWS), lanes]
        to = 640 + 128 * c if c < 3 else 384 + 128 * (c - 3)
        d_all[:, pl.ds(to, 128)] = total.astype(BF16)
    d_all[:, pl.ds(1024, 128)] = d_q[...]
    d_all[:, pl.ds(1152, 128)] = pair[...]

    def part(i, carry):
        rows = pl.ds(pl.multiple_of(i * 256, 256), 256)
        late = pl.ds(pl.multiple_of(i * 256 + 1024, 256), 256)
        mine = normed[:, rows]
        ms[rows] = tn(mine, d_all[:, pl.ds(0, 640)]).astype(BF16)
        ms[late] = tn(mine, d_all[:, pl.ds(640, 640)]).astype(BF16)
        total = nt(d_all[:, pl.ds(0, 384)], wm[0, rows]) + nt(d_all[:, pl.ds(640, 384)], wm[1, rows])
        total = total + nt(d_all[:, pl.ds(384, 256)], ws[rows])
        total = total + nt(d_all[:, pl.ds(1024, 128)], wq[rows])
        total = total + nt(d_all[:, pl.ds(1152, 128)], wkv[rows])
        acc[:, rows] = total
        return carry

    lax.fori_loop(0, 4, part, 0)
    x = x_ref[...].astype(F32)
    r1 = lax.rsqrt(jnp.mean(x * x, axis=1, keepdims=True) + EPSILON)
    d_normed = acc[...]
    first_part[...] = jnp.broadcast_to(
        jnp.sum(d_normed * x * r1, axis=0, keepdims=True), first_part.shape
    )
    weighted = d_normed * gain[...]
    inner = jnp.sum(weighted * x, axis=1, keepdims=True)
    put_wide(wide, r1 * weighted - x * (r1 * r1 * r1 / D * inner))


def on_device(
    hidden_in, cotangent, log_decay, norm_gain, query_weight, keyvalue_weight, attention_output,
    mixer_weight, state_weight, kernel_mixer, kernel_state, bias_mixer, bias_state, skip_gain,
    mixer_gain, mixer_output, second_gain, gate_up, down_weight,
):
    s, h = lax.axis_index("seq"), lax.axis_index("head")
    idx = jnp.stack([s, h]).astype(jnp.int32)
    shared = h * (AH // HEADS) // (AH // KVH)
    pair_weight = lax.dynamic_slice_in_dim(keyvalue_weight, shared * HD, HD, 2)
    wkv = jnp.concatenate([pair_weight[0], pair_weight[1]], axis=1)
    gain1 = norm_gain.reshape(1, D)
    gain2 = second_gain.reshape(1, D)
    mgain = mixer_gain.reshape(1, MW)
    skip = jnp.repeat(skip_gain, MP).reshape(1, MW)
    taps = jnp.pad(jnp.concatenate([kernel_mixer, kernel_state], axis=1), ((0, 4), (0, 0)))
    bias = jnp.concatenate([bias_mixer, bias_state]).reshape(1, CW)
    decay = jnp.pad(log_decay, ((0, 0), (0, 2)))
    step = -decay
    cum = jnp.cumsum(decay, axis=0)
    cum_t = cum.T
    logs = jnp.broadcast_to(cum[ROWS - 1][:, None], (8, 128))

    normed, q, kv, gz, raw = call(
        project_kernel,
        [
            shape((ROWS, D), BF16), shape((ROWS, 128), BF16), shape((ROWS, 128), BF16),
            shape((ROWS, MW), F32), shape((ROWS, CW), F32),
        ],
        (hidden_in, gain1, query_weight, wkv, mixer_weight, state_weight),
    )
    kv_all, edge, logs_all = call(
        keyval_kernel,
        [shape((8192, 128), BF16), shape((8, CW), F32), shape((256, 128), F32)],
        (kv, raw[ROWS - 8 :], logs),
        collective=1, copies=26,
    )
    pre, post, local_state = call(
        conv_kernel,
        [shape((ROWS, CW), F32), shape((ROWS, CW), BF16), shape((MW, NS), BF16)],
        (idx, raw, edge, taps, bias, step, cum),
        scratch=[pltpu.VMEM((ROWS + 8, CW), F32)], smem=1,
    )
    (states,) = call(
        state_kernel, [shape((12288, NS), BF16)], (local_state,), collective=2, copies=20
    )
    attended, attended_f, totals = call(
        attend_kernel,
        [shape((ROWS, 128), BF16), shape((ROWS, 128), F32), shape((8, 512), F32)],
        (idx, q, kv_all),
        scratch=[pltpu.VMEM((512, 128), BF16), pltpu.VMEM((128, 512), F32)], smem=1,
    )
    ssd, mixed, squares, state = call(
        ssd_kernel,
        [shape((ROWS, MW), F32), shape((ROWS, MW), F32), shape((8, ROWS), F32), shape((MW, NS), BF16)],
        (idx, post, step, cum, cum_t, skip, gz, states, logs_all),
        scratch=[pltpu.VMEM((MW, NS), F32)], smem=1,
    )
    (squares,) = call(
        sums_kernel, [shape((8, ROWS), F32)], (squares,),
        scratch=[pltpu.VMEM((HEADS, 8, ROWS), F32)], collective=3, copies=3,
    )
    gated, part = call(
        outputs_kernel,
        [shape((ROWS, MW), BF16), shape((ROWS, D), BF16)],
        (mixed, squares, mgain, mixer_output, attended, attention_output),
    )
    (summed,) = call(
        head_sum_kernel, [shape((ROWS, D), BF16)], (part,),
        scratch=[pltpu.VMEM((ROWS, D), BF16)] * 2, collective=4, copies=8,
    )
    wide, back, xf, second_part = call(
        feed_kernel,
        [
            shape((1024, 256), BF16), shape((ROWS, D), BF16), shape((1536, D), BF16),
            shape((8, D), F32),
        ],
        (hidden_in, summed, cotangent, gain2, gate_up, down_weight),
        scratch=[pltpu.VMEM((ROWS, D), BF16), pltpu.VMEM((ROWS, D), F32), pltpu.VMEM((ROWS, D), F32)],
    )
    d_sum, out_share = call(
        second_sum_kernel,
        [shape((ROWS, D), BF16), shape((ROWS, 256), BF16)],
        (back, wide),
        scratch=[pltpu.VMEM((ROWS, D), BF16)] * 2 + [pltpu.VMEM((1024, 256), BF16)] * 2,
        collective=5, copies=12,
    )
    xb, d_att, d_gated, mixgain, inner = call(
        lower_kernel,
        [
            shape((512, D), BF16), shape((ROWS, 128), BF16), shape((ROWS, MW), F32),
            shape((8, MW), F32), shape((8, ROWS), F32),
        ],
        (cotangent, d_sum, gated, attended, mixer_output, attention_output, mixed, squares, mgain),
    )
    (inner,) = call(
        sums_kernel, [shape((8, ROWS), F32)], (inner,),
        scratch=[pltpu.VMEM((HEADS, 8, ROWS), F32)], collective=3, copies=3,
    )
    d_z, d_ssd, skip_part, d_scaled, d_bc, grad_state = call(
        ssd_back_kernel,
        [
            shape((ROWS, MW), BF16), shape((ROWS, MW), F32), shape((8, MW), F32),
            shape((ROWS, MW), F32), shape((ROWS, 256), F32), shape((MW, NS), BF16),
        ],
        (d_gated, mixed, squares, inner, mgain, gz, ssd, post, step, cum, cum_t, state),
    )
    (grad_states,) = call(
        state_kernel, [shape((12288, NS), BF16)], (grad_state,), collective=2, copies=20
    )
    d_pre, kernel_grads = call(
        conv_back_kernel,
        [shape((ROWS, CW), F32), shape((8, CW), F32)],
        (idx, grad_states, logs_all, d_ssd, d_scaled, d_bc, skip, step, cum, post, pre, raw, edge),
        scratch=[pltpu.VMEM((MW, NS), F32), pltpu.VMEM((ROWS + 8, CW), F32)], smem=1,
    )
    d_q, pairs = call(
        attend_back_kernel,
        [shape((ROWS, 128), BF16), shape((8192, 128), BF16)],
        (idx, q, kv_all, d_att, attended_f, totals),
        scratch=[
            pltpu.VMEM((512, 128), BF16), pltpu.VMEM((512, 128), BF16), pltpu.VMEM((128, 512), F32),
        ],
        smem=1,
    )
    pair, edge_back = call(
        pair_kernel,
        [shape((ROWS, 128), BF16), shape((8, CW), F32)],
        (pairs, d_pre[:8]),
        scratch=[pltpu.VMEM((8192, 128), BF16)] * 2, collective=6, copies=21,
    )
    ms, back_wide, first_part = call(
        input_back_kernel,
        [shape((2048, CW), BF16), shape((1024, 256), BF16), shape((8, D), F32)],
        (
            idx, d_pre, edge_back, taps, d_z, d_q, pair, normed, hidden_in, gain1, mixer_weight,
            state_weight, query_weight, wkv,
        ),
        scratch=[
            pltpu.VMEM((ROWS + 8, CW), F32), pltpu.VMEM((ROWS, 1280), BF16), pltpu.VMEM((ROWS, D), F32),
        ],
        smem=1,
    )
    blank = jnp.zeros((256,), F32)
    small = jnp.stack(
        [
            first_part[0],
            second_part[0],
            kernel_grads[:KC, MW:].reshape(-1),
            jnp.concatenate([kernel_grads[KC, MW:], blank, blank, blank]),
            jnp.concatenate([kernel_grads[0, :MW], kernel_grads[KC, :MW], blank]),
            jnp.concatenate([kernel_grads[1, :MW], mixgain[0], blank]),
            jnp.concatenate([kernel_grads[2, :MW], skip_part[0], blank]),
            jnp.concatenate([kernel_grads[3, :MW], blank, blank, blank[:128]]),
        ]
    )
    x_out, ms_out, in_share, small = call(
        final_kernel,
        [
            shape((2048, D), BF16), shape((2048, 768), BF16), shape((ROWS, 256), BF16),
            shape((8, D), F32),
        ],
        (xf, xb, ms, back_wide, small),
        scratch=[
            pltpu.VMEM((2048, D), BF16), pltpu.VMEM((2048, D), BF16),
            pltpu.VMEM((2048, CW), BF16), pltpu.VMEM((2048, CW), BF16),
            pltpu.VMEM((1024, 256), BF16), pltpu.VMEM((1024, 256), BF16),
            pltpu.VMEM((HEADS, 64, 256), BF16),
            pltpu.VMEM((8, 128), F32), pltpu.VMEM((8, 128), F32),
            pltpu.VMEM((HEADS, 8, D), F32),
            pltpu.VMEM((6, 8, D), F32), pltpu.VMEM((5, 8, D), F32),
        ],
        collective=7, copies=100,
    )

    def columns(values):
        return lax.dynamic_slice_in_dim(values, h * 256, 256, 1).astype(F32)

    block_out = columns(hidden_in) + columns(summed) + out_share.astype(F32)
    input_grads = columns(cotangent) + columns(d_sum) + in_share.astype(F32)
    x_f = x_out
    gateup = x_f[512:1536]
    head, tail = ms_out[:1024], ms_out[1024:]
    gateup_grads = jnp.stack([gateup[:, :512], gateup[:, 512:]]).astype(F32)
    mixer_grads = jnp.stack([head[:, :MW], tail[:, :MW]]).astype(F32)
    keys = jnp.concatenate([tail[:, 512:576], tail[:, 640:704]], axis=1)
    values = jnp.concatenate([tail[:, 576:640], tail[:, 704:768]], axis=1)
    return (
        block_out,
        input_grads,
        small[0],
        tail[:, MW:512].astype(F32),
        jnp.stack([keys, values]).astype(F32),
        x_f[1920:].astype(F32),
        mixer_grads,
        head[:, MW:640].astype(F32),
        small[4:8, :MW],
        small[2].reshape(KC, 256),
        small[4, MW : 2 * MW],
        small[3, :256],
        jnp.sum(small[6, MW : 2 * MW].reshape(HMH, MP), axis=1),
        small[5, MW : 2 * MW],
        x_f[1536:1920].astype(F32),
        small[1],
        gateup_grads,
        x_f[:512].astype(F32),
    )


def solution(mesh):
    return jax.shard_map(
        on_device,
        mesh=mesh,
        in_specs=(
            P("seq", None), P("seq", None), P("seq", "head"), P(), P(None, "head"), P(),
            P("head", None), P(None, None, "head"), P(), P(None, "head"), P(), P("head"), P(),
            P("head"), P("head"), P("head", None), P(), P(None, None, "head"), P("head", None),
        ),
        out_specs=(
            P("seq", "head"), P("seq", "head"), P(), P(None, "head"), P(), P("head", None),
            P(None, None, "head"), P(), P(None, "head"), P(), P("head"), P(), P("head"), P("head"),
            P("head", None), P(), P(None, None, "head"), P("head", None),
        ),
        check_vma=False,
    )
```

```python
import functools

import jax
import jax.numpy as jnp
from jax import lax
from jax.experimental import pallas as pl
from jax.experimental.pallas import tpu as pltpu
from jax.sharding import PartitionSpec as P

D = 1024
FF = 2048
AH = 8
KVH = 2
HD = 64
MAMBA_HEADS = 24
MP = 64
NS = 128
KC = 4
EPSILON = 1e-05
SEQ = 32
HEADS = 4
ROWS = 256
MW = 384
CW = 640
HMH = 6
HIGHEST = lax.Precision.HIGHEST
MESH = pl.DeviceIdType.MESH
F32 = jnp.float32
BF16 = jnp.bfloat16
VMEM_LIMIT = 50 * 1024 * 1024


def nn(a, b):
    return jnp.dot(a, b, preferred_element_type=F32)


def nt(a, b):
    return lax.dot_general(a, b, (((1,), (1,)), ((), ())), preferred_element_type=F32)


def tn(a, b):
    return lax.dot_general(a, b, (((0,), (0,)), ((), ())), preferred_element_type=F32)


def exact(a, b, dims):
    return lax.dot_general(
        a, b, (dims, ((), ())), precision=HIGHEST, preferred_element_type=F32
    )


def sigmoid(v):
    return 1.0 / (1.0 + jnp.exp(-v))


def shape(dims, kind):
    return jax.ShapeDtypeStruct(dims, kind)


def seq_bits(s):
    core, y, z = s % 2, (s // 2) % 4, s // 8
    return {
        "c": core,
        "ya": (y + y // 2) % 2,
        "yb": y // 2,
        "za": (z + z // 2) % 2,
        "zb": z // 2,
    }


SEQ_PATHS = (
    ("c", "ya", "yb", "za", "zb"),
    ("c", "yb", "ya", "zb", "za"),
    ("c", "za", "zb", "ya", "yb"),
    ("c", "zb", "za", "yb", "ya"),
)
HEAD_PATHS = (("xa", "xb"), ("xb", "xa"))


def position(bits, path):
    at = 0
    for name in path:
        at = at * 2 + bits[name]
    return at


def block_position(s, p):
    return position(seq_bits(s), SEQ_PATHS[p])


def head_position(h, p):
    bits = {"xa": (h + h // 2) % 2, "xb": h // 2}
    return position(bits, HEAD_PATHS[p])


class Links:
    def __init__(self, send_sem, recv_sem):
        s, h = lax.axis_index("seq"), lax.axis_index("head")
        self.s, self.h = s, h
        core, y, z = s % 2, (s // 2) % 4, s // 8
        self.bits = seq_bits(s)
        self.bits["xa"] = (h + h // 2) % 2
        self.bits["xb"] = h // 2
        self.partner = {
            "c": (s + 1 - 2 * core, h),
            "ya": (s + 2 * (1 - 2 * (y % 2)), h),
            "yb": (s + 2 * (3 - 2 * y), h),
            "za": (s + 8 * (1 - 2 * (z % 2)), h),
            "zb": (s + 8 * (3 - 2 * z), h),
            "xa": (s, h + 1 - 2 * (h % 2)),
            "xb": (s, 3 - h),
            "x1": (s, (h + 1) % HEADS),
            "x2": (s, (h + 2) % HEADS),
            "x3": (s, (h + 3) % HEADS),
            "next": ((s + 1) % SEQ, h),
            "prev": ((s + SEQ - 1) % SEQ, h),
        }
        self.send_sem, self.recv_sem, self.used = send_sem, recv_sem, 0

    def greet(self, names):
        semaphore = pltpu.get_barrier_semaphore()
        for name in names:
            pl.semaphore_signal(
                semaphore, inc=1, device_id=self.partner[name], device_id_type=MESH
            )

    def met(self, names):
        pl.semaphore_wait(pltpu.get_barrier_semaphore(), len(names))

    def barrier(self, names):
        self.greet(names)
        self.met(names)

    def send(self, src, dst, name):
        k = self.used
        self.used += 1
        copy = pltpu.make_async_remote_copy(
            src_ref=src,
            dst_ref=dst,
            send_sem=self.send_sem.at[k],
            recv_sem=self.recv_sem.at[k],
            device_id=self.partner[name],
            device_id_type=MESH,
        )
        copy.start()
        return copy


DONE = object()
SEQ_NAMES = ("c", "ya", "yb", "za", "zb")


def rows_at(start, count, unit=16):
    return pl.ds(pl.multiple_of(start, unit), count)


class Reduce:
    def __init__(self, links, path, rows, src, src_base, work, recv, out, base):
        self.links, self.path, self.rows = links, path, rows
        self.src, self.src_base = src, src_base
        self.work, self.recv, self.out, self.base = work, recv, out, base
        self.start = 0
        self.copy = None

    def begin(self, step):
        name = self.path[step]
        half = self.rows >> (step + 1)
        bit = self.links.bits[name]
        away = self.start + (1 - bit) * half
        ref, at = (self.src, self.src_base) if step == 0 else (self.work, self.base)
        landing = self.base + self.rows - (self.rows >> step)
        self.copy = self.links.send(
            ref.at[rows_at(at + away, half)], self.recv.at[pl.ds(landing, half)], name
        )

    def finish(self, step):
        name = self.path[step]
        half = self.rows >> (step + 1)
        keep = self.start + self.links.bits[name] * half
        ref, at = (self.src, self.src_base) if step == 0 else (self.work, self.base)
        landing = self.base + self.rows - (self.rows >> step)
        last = step == len(self.path) - 1
        target, offset = (self.out, self.base) if last and self.out is not None else (self.work, self.base)
        self.copy.wait()
        chunk = min(half, 32)

        def add(i, carry):
            own = ref[rows_at(at + keep + i * chunk, chunk)].astype(F32)
            other = self.recv[rows_at(landing + i * chunk, chunk)].astype(F32)
            target[rows_at(offset + keep + i * chunk, chunk)] = (own + other).astype(BF16)
            return carry

        lax.fori_loop(0, half // chunk, add, 0)
        self.start = keep

    def send_back(self, step, columns=None):
        name = self.path[step]
        size = self.rows >> (step + 1)
        at = rows_at(self.base + self.start, size, min(size, 16))
        ref = self.out.at[at] if columns is None else self.out.at[at, pl.ds(0, columns)]
        self.copy = self.links.send(ref, ref, name)

    def wait_back(self, step):
        size = self.rows >> (step + 1)
        self.copy.wait()
        self.start = self.start - self.links.bits[self.path[step]] * size


def reduce_steps(jobs):
    for job in jobs:
        job.begin(0)
    for step in range(max(len(job.path) for job in jobs)):
        yield
        for job in jobs:
            if step < len(job.path):
                job.finish(step)
                if step + 1 < len(job.path):
                    job.begin(step + 1)


def gather_steps(jobs, columns=None):
    columns = columns or [None] * len(jobs)
    for job, width in zip(jobs, columns):
        job.send_back(len(job.path) - 1, width)
    for step in range(max(len(job.path) for job in jobs) - 1, -1, -1):
        yield
        for job, width in zip(jobs, columns):
            if step < len(job.path):
                job.wait_back(step)
                if step:
                    job.send_back(step - 1, width)


def finish(*runs):
    runs = list(runs)
    while runs:
        for run in list(runs):
            if next(run, DONE) is DONE:
                runs.remove(run)


def advance(*runs):
    for run in runs:
        next(run, DONE)


def reduce_all(jobs):
    finish(reduce_steps(jobs))


def gather_all(jobs, columns=None):
    finish(gather_steps(jobs, columns))


def call(body, outs, args, scratch=(), collective=None, smem=0, copies=0, cost=None):
    vm = pl.BlockSpec(memory_space=pltpu.VMEM)
    scratch = list(scratch)
    if copies:
        scratch += [pltpu.SemaphoreType.DMA((copies,)), pltpu.SemaphoreType.DMA((copies,))]
    if collective is None:
        params = pltpu.CompilerParams(vmem_limit_bytes=VMEM_LIMIT)
    else:
        params = pltpu.CompilerParams(
            vmem_limit_bytes=VMEM_LIMIT, collective_id=collective, has_side_effects=True
        )
    in_specs = [pl.BlockSpec(memory_space=pltpu.SMEM)] * smem + [vm] * (len(args) - smem)
    return pl.pallas_call(
        body,
        out_shape=tuple(outs),
        in_specs=in_specs,
        out_specs=tuple(vm for _ in outs),
        scratch_shapes=scratch,
        compiler_params=params,
    )(*args)


class Gather:
    def __init__(self, links, path, piece, out, base):
        self.links, self.path, self.piece, self.out, self.base = links, path, piece, out, base
        self.start = position(links.bits, path) * piece
        self.rows = piece << len(path)

    send_back = Reduce.send_back
    wait_back = Reduce.wait_back


def gather_rows(links, src, out, paths=SEQ_PATHS):
    piece = src.shape[0] // len(paths)
    jobs = []
    for p, path in enumerate(paths):
        job = Gather(links, path, piece, out, p * (piece << len(path)))
        own = rows_at(job.base + job.start, piece, 8 if piece == 8 else 16)
        out[own] = src[pl.ds(p * piece, piece)]
        jobs.append(job)
    return jobs


def state_kernel(state, state_all, send_sem, recv_sem):
    links = Links(send_sem, recv_sem)
    jobs = gather_rows(links, state, state_all)
    links.barrier(SEQ_NAMES)
    gather_all(jobs)


def sums_kernel(part, total, slots, send_sem, recv_sem):
    links = Links(send_sem, recv_sem)
    slots[links.h] = part[...]
    links.barrier(("x1", "x2", "x3"))
    copies = [links.send(part, slots.at[links.h], name) for name in ("x1", "x2", "x3")]
    for copy in copies:
        copy.wait()
    total[...] = (slots[0] + slots[1]) + (slots[2] + slots[3])


def own_rows(job, count):
    return job.work[rows_at(job.base + job.start, count)]


def second_sum_kernel(part, wide, total, share, work, recv, wide_work, wide_recv, send_sem, recv_sem):
    links = Links(send_sem, recv_sem)
    links.barrier(("xa", "xb"))
    sums = [
        Reduce(links, path, 128, part, 128 * p, work, recv, total, 128 * p)
        for p, path in enumerate(HEAD_PATHS)
    ]
    shares = [
        Reduce(links, path, 512, wide, 512 * p, wide_work, wide_recv, None, 512 * p)
        for p, path in enumerate(HEAD_PATHS)
    ]
    reduce_all(sums + shares)
    gather_all(sums)
    for p, job in enumerate(shares):
        share[pl.ds(128 * p, 128)] = own_rows(job, 128)


def pair_kernel(pairs, edge, own, edge_in, work, recv, send_sem, recv_sem):
    links = Links(send_sem, recv_sem)
    links.barrier(SEQ_NAMES + ("next", "prev"))
    edge_copy = links.send(edge, edge_in, "prev")
    jobs = [
        Reduce(links, path, 2048, pairs, 2048 * p, work, recv, None, 2048 * p)
        for p, path in enumerate(SEQ_PATHS)
    ]
    reduce_all(jobs)
    for p, job in enumerate(jobs):
        own[pl.ds(64 * p, 64)] = own_rows(job, 64)
    edge_copy.wait()


def final_kernel(
    xf, xb, ms, wide, small,
    x_out, ms_out, share, small_out,
    x_work, x_recv, ms_work, ms_recv, wide_work, wide_recv, head_slots, small_x,
    small_work, small_recv, send_sem, recv_sem,
):
    links = Links(send_sem, recv_sem)
    links.barrier(SEQ_NAMES + ("xa", "xb", "x1", "x2", "x3"))
    x_jobs = [
        Reduce(
            links, path, 512, xf if p < 3 else xb, 512 * p if p < 3 else 0,
            x_work, x_recv, x_out, 512 * p,
        )
        for p, path in enumerate(SEQ_PATHS)
    ]
    ms_jobs = [
        Reduce(links, path, 512, ms, 512 * p, ms_work, ms_recv, None, 512 * p)
        for p, path in enumerate(SEQ_PATHS)
    ]
    shares = [
        Reduce(links, path, 512, wide, 512 * p, wide_work, wide_recv, None, 512 * p)
        for p, path in enumerate(HEAD_PATHS)
    ]
    small_work[0] = small[...]

    def vectors():
        for step, name in enumerate(SEQ_NAMES):
            copy = links.send(small_work.at[step], small_recv.at[step], name)
            yield
            copy.wait()
            small_work[step + 1] = small_work[step] + small_recv[step]
        small_x[links.h] = small_work[5]
        copies = [links.send(small_work.at[5], small_x.at[links.h], n) for n in ("x1", "x2", "x3")]
        yield
        for copy in copies:
            copy.wait()
        total = (small_x[0] + small_x[1]) + (small_x[2] + small_x[3])
        row = lax.broadcasted_iota(jnp.int32, (8, 1024), 0)
        small_out[...] = jnp.where(row < 4, total, small_work[5])

    finish(reduce_steps(x_jobs + ms_jobs), reduce_steps(shares), vectors())
    for p, job in enumerate(shares):
        share[pl.ds(128 * p, 128)] = own_rows(job, 128)
    for p, job in enumerate(ms_jobs):
        at = rows_at(job.base + job.start, 16)
        if p < 2:
            piece = ms_work[at, pl.ds(384, 256)]
        else:
            piece = jnp.concatenate([ms_work[at, pl.ds(512, 128)]] * 2, axis=1)
        head_slots[links.h, pl.ds(16 * p, 16)] = piece
    slot = head_slots.at[links.h]
    head_copies = [links.send(slot, slot, n) for n in ("x1", "x2", "x3")]
    for copy in head_copies:
        copy.wait()
    for p, job in enumerate(ms_jobs):
        job.out = ms_out
        at = rows_at(job.base + job.start, 16)
        parts = [head_slots[k, pl.ds(16 * p, 16)].astype(F32) for k in range(HEADS)]
        if p < 2:
            ms_out[at, pl.ds(0, 384)] = ms_work[at, pl.ds(0, 384)]
            ms_out[at, pl.ds(384, 256)] = ((parts[0] + parts[1]) + (parts[2] + parts[3])).astype(BF16)
        else:
            ms_out[at, pl.ds(0, 512)] = ms_work[at, pl.ds(0, 512)]
            ms_out[at, pl.ds(512, 128)] = (parts[0] + parts[1])[:, :128].astype(BF16)
            ms_out[at, pl.ds(640, 128)] = (parts[2] + parts[3])[:, :128].astype(BF16)
    gather_all(x_jobs + ms_jobs, [None] * 4 + [640, 640, None, None])


def widen(values):
    lane = lax.broadcasted_iota(jnp.int32, (8, MW), 1)
    row = lax.broadcasted_iota(jnp.int32, (8, MW), 0)
    spread = jnp.where((lane >= row * MP) & (lane < row * MP + MP), 1.0, 0.0)
    return exact(values, spread, ((1,), (0,)))


def decay_terms(step_ref, cum_ref):
    cum = cum_ref[...]
    step_x = widen(step_ref[...])
    cum_x = widen(cum)
    enter_x = jnp.exp(cum_x)
    tail_x = jnp.exp(cum_x[ROWS - 1 : ROWS, :] - cum_x)
    return step_x, enter_x, tail_x


def conv_forward(ext, taps, bias, pre, post):
    for c in range(5):
        lanes = pl.ds(128 * c, 128)
        total = bias[:, lanes] + taps[pl.ds(0, 1), lanes] * ext[pl.ds(13, ROWS), lanes]
        for k in range(1, KC):
            total = total + taps[pl.ds(k, 1), lanes] * ext[pl.ds(13 + k, ROWS), lanes]
        pre[:, lanes] = total
        post[:, lanes] = (total * sigmoid(total)).astype(BF16)


def chain(s, gathered, logs, total, forward):
    total[...] = jnp.zeros_like(total)

    def hop(i, run):
        j = s - 1 - i if forward else s + 1 + i
        weight = jnp.exp(run)
        for seg in range(12):
            p, off = seg // 3, (seg % 3) * 32
            at = rows_at(p * 3072 + block_position(j, p) * 96 + off, 32)
            h = seg // 2
            total[pl.ds(32 * seg, 32)] += weight[h : h + 1, :] * gathered[at].astype(F32)
        return run + logs[rows_at(block_position(j, 0) * 8, 8, 8)]

    lax.fori_loop(0, s if forward else SEQ - 1 - s, hop, jnp.zeros((8, 128), F32))


def lower_mask():
    t = lax.broadcasted_iota(jnp.int32, (ROWS, ROWS), 0)
    u = lax.broadcasted_iota(jnp.int32, (ROWS, ROWS), 1)
    return u <= t


def decay_of(cum, cum_t, h, mask):
    diff = cum[:, h : h + 1] - cum_t[h : h + 1, :]
    return jnp.exp(jnp.where(mask, diff, -1e30))


def row_sums(values):
    return exact(jnp.ones((8, values.shape[1]), F32), values, ((1,), (1,)))


def column_of(rows):
    return exact(rows, jnp.full((8, 128), 0.125, F32), ((0,), (0,)))[:, 0:1]


def ssd_forward(post, step_x, enter_x, cum_ref, cumt_ref, skip, gz, state, ssd, mixed, squares):
    mixer_in = post[:, pl.ds(0, MW)].astype(F32)
    scaled = (mixer_in * step_x).astype(BF16)
    b, c = post[:, pl.ds(MW, NS)], post[:, pl.ds(MW + NS, NS)]
    gram = nt(c, b)
    mask = lower_mask()
    cum, cum_t = cum_ref[...], cumt_ref[...]
    left = lax.broadcasted_iota(jnp.int32, (ROWS, 128), 1) < MP
    carried = enter_x * nt(c, state[...]) + skip[...] * mixer_in
    for pair in range(3):
        lanes = slice(128 * pair, 128 * pair + 128)
        first = nn((gram * decay_of(cum, cum_t, 2 * pair, mask)).astype(BF16), scaled[:, lanes])
        second = nn((gram * decay_of(cum, cum_t, 2 * pair + 1, mask)).astype(BF16), scaled[:, lanes])
        ssd[:, pl.ds(128 * pair, 128)] = jnp.where(left, first, second) + carried[:, lanes]
    z = gz[...]
    m = ssd[...] * (z * sigmoid(z))
    mixed[...] = m
    squares[...] = row_sums(m * m)


def load_block(kv_all, j):
    return jnp.concatenate(
        [kv_all[rows_at(2048 * p + block_position(j, p) * 64, 64)] for p in range(4)], axis=0
    )


def causal(block):
    key = lax.broadcasted_iota(jnp.int32, block.shape, 0)
    query = lax.broadcasted_iota(jnp.int32, block.shape, 1)
    query = jnp.where(query >= ROWS, query - ROWS, query)
    return jnp.where(key <= query, block, -1e30)


def stacked_queries(q):
    q = q.astype(F32) * (HD ** -0.5)
    left = lax.broadcasted_iota(jnp.int32, (ROWS, 128), 1) < HD
    first = jnp.where(left, q, 0.0)
    second = jnp.where(left, pltpu.roll(q, HD, 1), 0.0)
    return jnp.concatenate([first, second], axis=0).astype(BF16)


FORWARD_NAMES = SEQ_NAMES + ("next", "prev", "x1", "x2", "x3")


def forward_kernel(
    x_ref, gain, wq, wkv, wm, ws, taps, bias, step, cum_ref, cumt_ref, logs, skip, mgain, wmo, wao,
    normed, q, kv_all, logs_all, gz, ext, pre, post, attended, attended_f, totals, ssd, mixed,
    squares, state, gated, summed,
    kv, x_edge, edge_normed, local, states, chained, qp, acc, own_squares, slots, proj, part, work,
    recv, send_sem, recv_sem,
):
    links = Links(send_sem, recv_sem)
    s = links.s
    links.greet(FORWARD_NAMES)

    def normalise(rows):
        x = rows.astype(F32)
        r1 = lax.rsqrt(jnp.mean(x * x, axis=1, keepdims=True) + EPSILON)
        return (x * r1 * gain[...]).astype(BF16)

    n = normalise(x_ref[...])
    normed[...] = n
    kv[...] = nn(n, wkv[...]).astype(BF16)
    q[...] = nn(n, wq[...]).astype(BF16)
    key_jobs = gather_rows(links, kv, kv_all) + gather_rows(links, logs, logs_all, SEQ_PATHS[:1])
    links.met(FORWARD_NAMES)
    edge_copy = links.send(x_ref.at[pl.ds(ROWS - 16, 16)], x_edge, "next")
    keys = gather_steps(key_jobs)
    advance(keys)
    gz[...] = nn(normed[...], wm[0])
    advance(keys)
    ext[pl.ds(16, ROWS), pl.ds(0, MW)] = nn(normed[...], wm[1])
    ext[pl.ds(16, ROWS), pl.ds(MW, 256)] = nn(normed[...], ws[...])
    edge_copy.wait()
    advance(keys)
    keep = jnp.where(s > 0, 1.0, 0.0)
    edge_normed[...] = normalise(x_edge[...])
    ext[pl.ds(0, 16), pl.ds(0, MW)] = nn(edge_normed[...], wm[1]) * keep
    ext[pl.ds(0, 16), pl.ds(MW, 256)] = nn(edge_normed[...], ws[...]) * keep
    conv_forward(ext, taps, bias, pre, post)
    advance(keys)
    step_x, enter_x, tail_x = decay_terms(step, cum_ref)
    tail_in = (post[:, pl.ds(0, MW)].astype(F32) * step_x * tail_x).astype(BF16)
    local[...] = tn(tail_in, post[:, pl.ds(MW, NS)]).astype(BF16)
    entering = gather_steps(gather_rows(links, local, states))
    advance(entering, keys)

    qp[...] = stacked_queries(q[...])
    scores = causal(nt(kv[...], qp[...]))
    high = jnp.max(scores, axis=0, keepdims=True)
    weights = jnp.exp(scores - high)
    acc[...] = tn(kv[...], weights.astype(BF16))
    advance(entering)
    finish(keys)

    def hop(j, running):
        high, total = running
        block = load_block(kv_all, j)
        scores = nt(block, qp[...])
        new = jnp.maximum(high, jnp.max(scores, axis=0, keepdims=True))
        fade = jnp.exp(high - new)
        weights = jnp.exp(scores - new)
        acc[...] = acc[...] * fade + tn(block, weights.astype(BF16))
        return new, total * fade + jnp.sum(weights, axis=0, keepdims=True)

    running = (high, jnp.sum(weights, axis=0, keepdims=True))
    for turn in range(4):
        running = lax.fori_loop((s * turn) // 4, (s * (turn + 1)) // 4, hop, running)
        advance(entering)
    high, total = running
    out = acc[pl.ds(HD, HD)] / total
    out = jnp.concatenate([out[:, :ROWS], out[:, ROWS:]], axis=0).T
    attended_f[...] = out
    attended[...] = out.astype(BF16)
    totals[...] = jnp.broadcast_to(high + jnp.log(total), totals.shape)
    finish(entering)

    chain(s, states, logs_all, chained, True)
    state[...] = chained[...].astype(BF16)
    ssd_forward(post, step_x, enter_x, cum_ref, cumt_ref, skip, gz, state, ssd, mixed, own_squares)
    slots[links.h] = own_squares[...]
    copies = [links.send(own_squares, slots.at[links.h], name) for name in ("x1", "x2", "x3")]
    for c in range(2):
        lanes = pl.ds(512 * c, 512)
        proj[:, lanes] = nn(attended[...], wao[:, lanes])
    for copy in copies:
        copy.wait()
    squares[...] = (slots[0] + slots[1]) + (slots[2] + slots[3])
    scale = lax.rsqrt(column_of(squares[...]) / (MAMBA_HEADS * MP) + EPSILON)
    gated[...] = (mixed[...] * scale * mgain[...]).astype(BF16)
    for c in range(2):
        lanes = pl.ds(512 * c, 512)
        part[:, lanes] = (proj[:, lanes] + nn(gated[...], wmo[:, lanes])).astype(BF16)
    jobs = [
        Reduce(links, path, 128, part, 128 * p, work, recv, summed, 128 * p)
        for p, path in enumerate(HEAD_PATHS)
    ]
    reduce_all(jobs)
    gather_all(jobs)


def attend_back_kernel(idx, q, kv_all, d_att, attended_f, totals, d_q, pairs, qp, dop, acc):
    s = idx[0]
    qp[...] = stacked_queries(q[...])
    d_out = d_att[...].astype(F32)
    left = lax.broadcasted_iota(jnp.int32, (ROWS, 128), 1) < HD
    first = jnp.where(left, 0.0, pltpu.roll(d_out, HD, 1))
    second = jnp.where(left, 0.0, d_out)
    dop[...] = jnp.concatenate([first, second], axis=0).astype(BF16)
    product = (d_out * attended_f[...]).T
    delta = jnp.concatenate(
        [
            jnp.sum(product[:HD], axis=0, keepdims=True),
            jnp.sum(product[HD:], axis=0, keepdims=True),
        ],
        axis=1,
    )
    total = totals[pl.ds(0, 1)]
    pairs[...] = jnp.zeros_like(pairs)

    def step(j, masked):
        block = load_block(kv_all, j)
        scores = nt(block, qp[...])
        if masked:
            scores = causal(scores)
        probs = jnp.exp(scores - total)
        d_probs = nt(block, dop[...])
        d_scores = (probs * (d_probs - delta)).astype(BF16)
        d_pair = (nn(d_scores, qp[...]) + nn(probs.astype(BF16), dop[...])).astype(BF16)
        for p in range(4):
            at = rows_at(2048 * p + block_position(j, p) * 64, 64)
            pairs[at] = d_pair[64 * p : 64 * p + 64]
        return tn(block, d_scores)

    acc[...] = step(s, True)

    def hop(j, carry):
        acc[...] += step(j, False)
        return carry

    lax.fori_loop(0, s, hop, 0)
    out = acc[pl.ds(0, HD)] * (HD ** -0.5)
    d_q[...] = jnp.concatenate([out[:, :ROWS], out[:, ROWS:]], axis=0).T.astype(BF16)


def put_wide(wide, values):
    for j in range(HEADS):
        for p in range(2):
            at = 512 * p + int(head_position(j, p)) * 128
            wide[pl.ds(at, 128)] = values[128 * p : 128 * p + 128, 256 * j : 256 * j + 256].astype(BF16)


def feed_kernel(x_ref, summed, cot_ref, gain, gu, dw, wide, back, xf, second_part, sn, out_acc, d_acc):
    residual = x_ref[...].astype(F32) + summed[...].astype(F32)
    r2 = lax.rsqrt(jnp.mean(residual * residual, axis=1, keepdims=True) + EPSILON)
    sn[...] = (residual * r2 * gain[...]).astype(BF16)
    out_acc[...] = jnp.zeros_like(out_acc)
    d_acc[...] = jnp.zeros_like(d_acc)

    def part(c, carry):
        cols = pl.ds(pl.multiple_of(c * 256, 256), 256)
        high = pl.ds(pl.multiple_of(c * 256 + 512, 256), 256)
        wg, wu, wd = gu[0, :, cols], gu[1, :, cols], dw[cols]
        gate, up = nn(sn[...], wg), nn(sn[...], wu)
        sig = sigmoid(gate)
        act_gate = gate * sig
        act = (act_gate * up).astype(BF16)
        out_acc[...] += nn(act, wd)
        xf[cols] = tn(act, cot_ref[...]).astype(BF16)
        d_act = nt(cot_ref[...], wd)
        d_gate = (d_act * up * (sig * (1.0 + gate * (1.0 - sig)))).astype(BF16)
        d_up = (d_act * act_gate).astype(BF16)
        xf[pl.ds(512, 1024), cols] = tn(sn[...], d_gate).astype(BF16)
        xf[pl.ds(512, 1024), high] = tn(sn[...], d_up).astype(BF16)
        d_acc[...] += nt(d_gate, wg) + nt(d_up, wu)
        return carry

    lax.fori_loop(0, 2, part, 0)
    put_wide(wide, out_acc[...])
    d_second = d_acc[...]
    residual = x_ref[...].astype(F32) + summed[...].astype(F32)
    second_part[...] = jnp.broadcast_to(
        jnp.sum(d_second * residual * r2, axis=0, keepdims=True), second_part.shape
    )
    weighted = d_second * gain[...]
    inner = jnp.sum(weighted * residual, axis=1, keepdims=True)
    back[...] = (r2 * weighted - residual * (r2 * r2 * r2 / D * inner)).astype(BF16)


def lower_kernel(cot, d_sum, gated, attended, wmo, wao, mixed, squares, mgain, xb, d_att, d_gated, mixgain, inner):
    low = (cot[...].astype(F32) + d_sum[...].astype(F32)).astype(BF16)
    for c in range(2):
        lanes = slice(512 * c, 512 * c + 512)
        xb[pl.ds(0, MW), pl.ds(512 * c, 512)] = tn(gated[...], low[:, lanes]).astype(BF16)
        xb[pl.ds(MW, 128), pl.ds(512 * c, 512)] = tn(attended[...], low[:, lanes]).astype(BF16)
    d_att[...] = nt(low, wao[...]).astype(BF16)
    dg = nt(low, wmo[...])
    d_gated[...] = dg
    scale = lax.rsqrt(column_of(squares[...]) / (MAMBA_HEADS * MP) + EPSILON)
    product = dg * mixed[...]
    mixgain[...] = jnp.broadcast_to(jnp.sum(product * scale, axis=0, keepdims=True), mixgain.shape)
    inner[...] = row_sums(product * mgain[...])


def ssd_back_kernel(
    d_gated, mixed, squares, inner, mgain, gz, ssd, post, step, cum_ref, cumt_ref, state,
    d_z, d_ssd, skip_part, d_scaled, d_bc, grad_state,
):
    scale = lax.rsqrt(column_of(squares[...]) / (MAMBA_HEADS * MP) + EPSILON)
    inner_col = column_of(inner[...])
    d_mixed = scale * (d_gated[...] * mgain[...]) - mixed[...] * (
        scale * scale * scale / (MAMBA_HEADS * MP) * inner_col
    )
    z = gz[...]
    sig = sigmoid(z)
    ds = d_mixed * (z * sig)
    d_ssd[...] = ds
    d_z[...] = (d_mixed * ssd[...] * (sig * (1.0 + z * (1.0 - sig)))).astype(BF16)
    step_x, enter_x, _ = decay_terms(step, cum_ref)
    mixer_in = post[:, pl.ds(0, MW)].astype(F32)
    skip_part[...] = jnp.broadcast_to(jnp.sum(ds * mixer_in, axis=0, keepdims=True), skip_part.shape)
    scaled = (mixer_in * step_x).astype(BF16)
    b, c = post[:, pl.ds(MW, NS)], post[:, pl.ds(MW + NS, NS)]
    gram = nt(c, b)
    mask = lower_mask()
    cum, cum_t = cum_ref[...], cumt_ref[...]
    left = lax.broadcasted_iota(jnp.int32, (ROWS, 128), 1) < MP
    low = ds.astype(BF16)
    d_gram = jnp.zeros((ROWS, ROWS), F32)
    for pair in range(3):
        lanes = slice(128 * pair, 128 * pair + 128)
        halves = []
        for k in range(2):
            decay = decay_of(cum, cum_t, 2 * pair + k, mask)
            here = left if k == 0 else jnp.logical_not(left)
            mine = jnp.where(here, ds[:, lanes], 0.0).astype(BF16)
            halves.append(tn((gram * decay).astype(BF16), low[:, lanes]))
            d_gram = d_gram + decay * nt(mine, scaled[:, lanes])
        d_scaled[:, pl.ds(128 * pair, 128)] = jnp.where(left, halves[0], halves[1])
    entered = (ds * enter_x).astype(BF16)
    grad_state[...] = tn(entered, c).astype(BF16)
    d_gram = d_gram.astype(BF16)
    d_bc[:, pl.ds(0, NS)] = tn(d_gram, c)
    d_bc[:, pl.ds(NS, NS)] = nn(d_gram, b) + nn(entered, state[...])


def conv_back_kernel(
    idx, gathered, logs, d_ssd, d_scaled, d_bc, skip, step, cum, post, pre, ext,
    d_pre, kernel_grads, total,
):
    chain(idx[0], gathered, logs, total, False)
    leaving = total[...].astype(BF16)
    step_x, _, tail_x = decay_terms(step, cum)
    b = post[:, pl.ds(MW, NS)]
    mixer_in = post[:, pl.ds(0, MW)].astype(F32)
    tail_in = (mixer_in * step_x * tail_x).astype(BF16)
    scaled_grad = d_scaled[...] + tail_x * nt(b, leaving)
    d_pre[:, pl.ds(0, MW)] = skip[...] * d_ssd[...] + scaled_grad * step_x
    d_pre[:, pl.ds(MW, NS)] = d_bc[:, pl.ds(0, NS)] + nn(tail_in, leaving)
    d_pre[:, pl.ds(MW + NS, NS)] = d_bc[:, pl.ds(NS, NS)]
    for c in range(5):
        lanes = pl.ds(128 * c, 128)
        v = pre[:, lanes]
        sig = sigmoid(v)
        dp = d_pre[:, lanes] * (sig * (1.0 + v * (1.0 - sig)))
        d_pre[:, lanes] = dp
        rows = [jnp.sum(dp * ext[pl.ds(13 + k, ROWS), lanes], axis=0, keepdims=True) for k in range(KC)]
        rows.append(jnp.sum(dp, axis=0, keepdims=True))
        rows.append(jnp.zeros((3, 128), F32))
        kernel_grads[:, lanes] = jnp.concatenate(rows, axis=0)


def input_back_kernel(
    idx, d_pre, edge, taps, d_z, d_q, pair, normed, x_ref, gain, wm, ws, wq, wkv,
    ms, wide, first_part, ext, d_all, acc,
):
    keep = jnp.where(idx[0] < SEQ - 1, 1.0, 0.0)
    ext[pl.ds(0, ROWS)] = d_pre[...]
    ext[pl.ds(ROWS, 8)] = edge[...] * keep
    d_all[:, pl.ds(0, MW)] = d_z[...]
    for c in range(5):
        lanes = pl.ds(128 * c, 128)
        total = taps[pl.ds(0, 1), lanes] * ext[pl.ds(3, ROWS), lanes]
        for k in range(1, KC):
            total = total + taps[pl.ds(k, 1), lanes] * ext[pl.ds(3 - k, ROWS), lanes]
        to = 640 + 128 * c if c < 3 else 384 + 128 * (c - 3)
        d_all[:, pl.ds(to, 128)] = total.astype(BF16)
    d_all[:, pl.ds(1024, 128)] = d_q[...]
    d_all[:, pl.ds(1152, 128)] = pair[...]

    def part(i, carry):
        rows = pl.ds(pl.multiple_of(i * 256, 256), 256)
        late = pl.ds(pl.multiple_of(i * 256 + 1024, 256), 256)
        mine = normed[:, rows]
        ms[rows] = tn(mine, d_all[:, pl.ds(0, 640)]).astype(BF16)
        ms[late] = tn(mine, d_all[:, pl.ds(640, 640)]).astype(BF16)
        total = nt(d_all[:, pl.ds(0, 384)], wm[0, rows]) + nt(d_all[:, pl.ds(640, 384)], wm[1, rows])
        total = total + nt(d_all[:, pl.ds(384, 256)], ws[rows])
        total = total + nt(d_all[:, pl.ds(1024, 128)], wq[rows])
        total = total + nt(d_all[:, pl.ds(1152, 128)], wkv[rows])
        acc[:, rows] = total
        return carry

    lax.fori_loop(0, 4, part, 0)
    x = x_ref[...].astype(F32)
    r1 = lax.rsqrt(jnp.mean(x * x, axis=1, keepdims=True) + EPSILON)
    d_normed = acc[...]
    first_part[...] = jnp.broadcast_to(
        jnp.sum(d_normed * x * r1, axis=0, keepdims=True), first_part.shape
    )
    weighted = d_normed * gain[...]
    inner = jnp.sum(weighted * x, axis=1, keepdims=True)
    put_wide(wide, r1 * weighted - x * (r1 * r1 * r1 / D * inner))


def widths_kernel(
    down_in, gateup_in, mixout_in, attn_in, head, tail,
    down, gateup, mixout, attn, mixer, query, keyval, state,
):
    down[...] = down_in[...].astype(F32)
    gateup[0] = gateup_in[:, pl.ds(0, 512)].astype(F32)
    gateup[1] = gateup_in[:, pl.ds(512, 512)].astype(F32)
    mixout[...] = mixout_in[...].astype(F32)
    attn[...] = attn_in[...].astype(F32)
    mixer[0] = head[:, pl.ds(0, MW)].astype(F32)
    mixer[1] = tail[:, pl.ds(0, MW)].astype(F32)
    state[...] = head[:, pl.ds(MW, 256)].astype(F32)
    query[...] = tail[:, pl.ds(MW, 128)].astype(F32)
    first, second = tail[:, pl.ds(512, 128)].astype(F32), tail[:, pl.ds(640, 128)].astype(F32)
    left = lax.broadcasted_iota(jnp.int32, first.shape, 1) < HD
    keyval[0] = jnp.where(left, first, pltpu.roll(second, HD, 1))
    keyval[1] = jnp.where(left, pltpu.roll(first, HD, 1), second)


def widened(x_out, ms_out):
    def rows(count, width, offset=0):
        return pl.BlockSpec((count, width), lambda i: (i + offset, 0))

    def halves(count, width):
        return pl.BlockSpec((2, count, width), lambda i: (0, i, 0))

    return pl.pallas_call(
        widths_kernel,
        grid=(4,),
        out_shape=(
            shape((512, D), F32), shape((2, D, 512), F32), shape((MW, D), F32), shape((128, D), F32),
            shape((2, D, MW), F32), shape((D, 128), F32), shape((2, D, 128), F32), shape((D, 256), F32),
        ),
        in_specs=[
            rows(128, D), rows(256, D, 2), rows(96, D, 16), rows(32, D, 60),
            rows(256, 768), rows(256, 768, 4),
        ],
        out_specs=(
            rows(128, D), halves(256, 512), rows(96, D), rows(32, D),
            halves(256, MW), rows(256, 128), halves(256, 128), rows(256, 256),
        ),
        compiler_params=pltpu.CompilerParams(vmem_limit_bytes=VMEM_LIMIT),
    )(x_out, x_out, x_out, x_out, ms_out, ms_out)


def on_device(
    hidden_in, cotangent, log_decay, norm_gain, query_weight, keyvalue_weight, attention_output,
    mixer_weight, state_weight, kernel_mixer, kernel_state, bias_mixer, bias_state, skip_gain,
    mixer_gain, mixer_output, second_gain, gate_up, down_weight,
):
    s, h = lax.axis_index("seq"), lax.axis_index("head")
    idx = jnp.stack([s, h]).astype(jnp.int32)
    shared = h * (AH // HEADS) // (AH // KVH)
    pair_weight = lax.dynamic_slice_in_dim(keyvalue_weight, shared * HD, HD, 2)
    wkv = jnp.concatenate([pair_weight[0], pair_weight[1]], axis=1)
    gain1 = norm_gain.reshape(1, D)
    gain2 = second_gain.reshape(1, D)
    mgain = mixer_gain.reshape(1, MW)
    skip = jnp.repeat(skip_gain, MP).reshape(1, MW)
    taps = jnp.pad(jnp.concatenate([kernel_mixer, kernel_state], axis=1), ((0, 4), (0, 0)))
    bias = jnp.concatenate([bias_mixer, bias_state]).reshape(1, CW)
    decay = jnp.pad(log_decay, ((0, 0), (0, 2)))
    step = -decay
    cum = jnp.cumsum(decay, axis=0)
    cum_t = cum.T
    logs = jnp.broadcast_to(cum[ROWS - 1][:, None], (8, 128))

    (
        normed, q, kv_all, logs_all, gz, ext, pre, post, attended, attended_f, totals, ssd, mixed,
        squares, state, gated, summed,
    ) = call(
        forward_kernel,
        [
            shape((ROWS, D), BF16), shape((ROWS, 128), BF16), shape((8192, 128), BF16),
            shape((256, 128), F32), shape((ROWS, MW), F32), shape((ROWS + 16, CW), F32),
            shape((ROWS, CW), F32), shape((ROWS, CW), BF16), shape((ROWS, 128), BF16),
            shape((ROWS, 128), F32), shape((8, 512), F32), shape((ROWS, MW), F32),
            shape((ROWS, MW), F32), shape((8, ROWS), F32), shape((MW, NS), BF16),
            shape((ROWS, MW), BF16), shape((ROWS, D), BF16),
        ],
        (
            hidden_in, gain1, query_weight, wkv, mixer_weight, state_weight, taps, bias, step, cum,
            cum_t, logs, skip, mgain, mixer_output, attention_output,
        ),
        scratch=[
            pltpu.VMEM((ROWS, 128), BF16), pltpu.VMEM((16, D), BF16), pltpu.VMEM((16, D), BF16),
            pltpu.VMEM((MW, NS), BF16), pltpu.VMEM((12288, NS), BF16), pltpu.VMEM((MW, NS), F32),
            pltpu.VMEM((512, 128), BF16), pltpu.VMEM((128, 512), F32), pltpu.VMEM((8, ROWS), F32),
            pltpu.VMEM((HEADS, 8, ROWS), F32), pltpu.VMEM((ROWS, D), F32),
            pltpu.VMEM((ROWS, D), BF16), pltpu.VMEM((ROWS, D), BF16), pltpu.VMEM((ROWS, D), BF16),
        ],
        collective=1, copies=60,
    )
    wide, back, xf, second_part = call(
        feed_kernel,
        [
            shape((1024, 256), BF16), shape((ROWS, D), BF16), shape((1536, D), BF16),
            shape((8, D), F32),
        ],
        (hidden_in, summed, cotangent, gain2, gate_up, down_weight),
        scratch=[pltpu.VMEM((ROWS, D), BF16), pltpu.VMEM((ROWS, D), F32), pltpu.VMEM((ROWS, D), F32)],
    )
    d_sum, out_share = call(
        second_sum_kernel,
        [shape((ROWS, D), BF16), shape((ROWS, 256), BF16)],
        (back, wide),
        scratch=[pltpu.VMEM((ROWS, D), BF16)] * 2 + [pltpu.VMEM((1024, 256), BF16)] * 2,
        collective=5, copies=12,
    )
    xb, d_att, d_gated, mixgain, inner = call(
        lower_kernel,
        [
            shape((512, D), BF16), shape((ROWS, 128), BF16), shape((ROWS, MW), F32),
            shape((8, MW), F32), shape((8, ROWS), F32),
        ],
        (cotangent, d_sum, gated, attended, mixer_output, attention_output, mixed, squares, mgain),
    )
    (inner,) = call(
        sums_kernel, [shape((8, ROWS), F32)], (inner,),
        scratch=[pltpu.VMEM((HEADS, 8, ROWS), F32)], collective=3, copies=3,
    )
    d_z, d_ssd, skip_part, d_scaled, d_bc, grad_state = call(
        ssd_back_kernel,
        [
            shape((ROWS, MW), BF16), shape((ROWS, MW), F32), shape((8, MW), F32),
            shape((ROWS, MW), F32), shape((ROWS, 256), F32), shape((MW, NS), BF16),
        ],
        (d_gated, mixed, squares, inner, mgain, gz, ssd, post, step, cum, cum_t, state),
    )
    (grad_states,) = call(
        state_kernel, [shape((12288, NS), BF16)], (grad_state,), collective=2, copies=20
    )
    d_pre, kernel_grads = call(
        conv_back_kernel,
        [shape((ROWS, CW), F32), shape((8, CW), F32)],
        (idx, grad_states, logs_all, d_ssd, d_scaled, d_bc, skip, step, cum, post, pre, ext),
        scratch=[pltpu.VMEM((MW, NS), F32)], smem=1,
    )
    d_q, pairs = call(
        attend_back_kernel,
        [shape((ROWS, 128), BF16), shape((8192, 128), BF16)],
        (idx, q, kv_all, d_att, attended_f, totals),
        scratch=[
            pltpu.VMEM((512, 128), BF16), pltpu.VMEM((512, 128), BF16), pltpu.VMEM((128, 512), F32),
        ],
        smem=1,
    )
    pair, edge_back = call(
        pair_kernel,
        [shape((ROWS, 128), BF16), shape((8, CW), F32)],
        (pairs, d_pre[:8]),
        scratch=[pltpu.VMEM((8192, 128), BF16)] * 2, collective=6, copies=21,
    )
    ms, back_wide, first_part = call(
        input_back_kernel,
        [shape((2048, CW), BF16), shape((1024, 256), BF16), shape((8, D), F32)],
        (
            idx, d_pre, edge_back, taps, d_z, d_q, pair, normed, hidden_in, gain1, mixer_weight,
            state_weight, query_weight, wkv,
        ),
        scratch=[
            pltpu.VMEM((ROWS + 8, CW), F32), pltpu.VMEM((ROWS, 1280), BF16), pltpu.VMEM((ROWS, D), F32),
        ],
        smem=1,
    )
    blank = jnp.zeros((256,), F32)
    small = jnp.stack(
        [
            first_part[0],
            second_part[0],
            kernel_grads[:KC, MW:].reshape(-1),
            jnp.concatenate([kernel_grads[KC, MW:], blank, blank, blank]),
            jnp.concatenate([kernel_grads[0, :MW], kernel_grads[KC, :MW], blank]),
            jnp.concatenate([kernel_grads[1, :MW], mixgain[0], blank]),
            jnp.concatenate([kernel_grads[2, :MW], skip_part[0], blank]),
            jnp.concatenate([kernel_grads[3, :MW], blank, blank, blank[:128]]),
        ]
    )
    x_out, ms_out, in_share, small = call(
        final_kernel,
        [
            shape((2048, D), BF16), shape((2048, 768), BF16), shape((ROWS, 256), BF16),
            shape((8, D), F32),
        ],
        (xf, xb, ms, back_wide, small),
        scratch=[
            pltpu.VMEM((2048, D), BF16), pltpu.VMEM((2048, D), BF16),
            pltpu.VMEM((2048, CW), BF16), pltpu.VMEM((2048, CW), BF16),
            pltpu.VMEM((1024, 256), BF16), pltpu.VMEM((1024, 256), BF16),
            pltpu.VMEM((HEADS, 64, 256), BF16),
            pltpu.VMEM((HEADS, 8, D), F32),
            pltpu.VMEM((6, 8, D), F32), pltpu.VMEM((5, 8, D), F32),
        ],
        collective=7, copies=100,
    )

    def columns(values):
        return lax.dynamic_slice_in_dim(values, h * 256, 256, 1).astype(F32)

    block_out = columns(hidden_in) + columns(summed) + out_share.astype(F32)
    input_grads = columns(cotangent) + columns(d_sum) + in_share.astype(F32)
    down, gateup, mixout, attn, mixer, query, keyval, state_total = widened(x_out, ms_out)
    return (
        block_out,
        input_grads,
        small[0],
        query,
        keyval,
        attn,
        mixer,
        state_total,
        small[4:8, :MW],
        small[2].reshape(KC, 256),
        small[4, MW : 2 * MW],
        small[3, :256],
        jnp.sum(small[6, MW : 2 * MW].reshape(HMH, MP), axis=1),
        small[5, MW : 2 * MW],
        mixout,
        small[1],
        gateup,
        down,
    )


def solution(mesh):
    return jax.shard_map(
        on_device,
        mesh=mesh,
        in_specs=(
            P("seq", None), P("seq", None), P("seq", "head"), P(), P(None, "head"), P(),
            P("head", None), P(None, None, "head"), P(), P(None, "head"), P(), P("head"), P(),
            P("head"), P("head"), P("head", None), P(), P(None, None, "head"), P("head", None),
        ),
        out_specs=(
            P("seq", "head"), P("seq", "head"), P(), P(None, "head"), P(), P("head", None),
            P(None, None, "head"), P(), P(None, "head"), P(), P("head"), P(), P("head"), P("head"),
            P("head", None), P(), P(None, None, "head"), P("head", None),
        ),
        check_vma=False,
    )
```

```python
import functools

import jax
import jax.numpy as jnp
from jax import lax
from jax.experimental import pallas as pl
from jax.experimental.pallas import tpu as pltpu
from jax.sharding import PartitionSpec as P

D = 1024
FF = 2048
AH = 8
KVH = 2
HD = 64
MAMBA_HEADS = 24
MP = 64
NS = 128
KC = 4
EPSILON = 1e-05
SEQ = 32
HEADS = 4
ROWS = 256
MW = 384
CW = 640
HMH = 6
HIGHEST = lax.Precision.HIGHEST
MESH = pl.DeviceIdType.MESH
F32 = jnp.float32
BF16 = jnp.bfloat16
VMEM_LIMIT = 50 * 1024 * 1024


def nn(a, b):
    return jnp.dot(a, b, preferred_element_type=F32)


def nt(a, b):
    return lax.dot_general(a, b, (((1,), (1,)), ((), ())), preferred_element_type=F32)


def tn(a, b):
    return lax.dot_general(a, b, (((0,), (0,)), ((), ())), preferred_element_type=F32)


def exact(a, b, dims):
    return lax.dot_general(
        a, b, (dims, ((), ())), precision=HIGHEST, preferred_element_type=F32
    )


def sigmoid(v):
    return 1.0 / (1.0 + jnp.exp(-v))


def shape(dims, kind):
    return jax.ShapeDtypeStruct(dims, kind)


def seq_bits(s):
    core, y, z = s % 2, (s // 2) % 4, s // 8
    return {
        "c": core,
        "ya": (y + y // 2) % 2,
        "yb": y // 2,
        "za": (z + z // 2) % 2,
        "zb": z // 2,
        "y4": y,
        "z4": z,
    }


SEQ_PATHS = (
    ("c", "ya", "yb", "z4"),
    ("c", "yb", "ya", "z4"),
    ("c", "za", "zb", "y4"),
    ("c", "zb", "za", "y4"),
)
HEAD_PATHS = (("xa", "xb"), ("xb", "xa"))


def ways(name):
    return 4 if name in ("y4", "z4") else 2


def position(bits, path):
    at = 0
    for name in path:
        at = at * ways(name) + bits[name]
    return at


def sizes(rows, path):
    left = []
    for name in path:
        rows = rows // ways(name)
        left.append(rows)
    return left


def block_position(s, p):
    return position(seq_bits(s), SEQ_PATHS[p])


def head_position(h, p):
    bits = {"xa": (h + h // 2) % 2, "xb": h // 2}
    return position(bits, HEAD_PATHS[p])


class Links:
    def __init__(self, send_sem, recv_sem):
        s, h = lax.axis_index("seq"), lax.axis_index("head")
        self.s, self.h = s, h
        core, y, z = s % 2, (s // 2) % 4, s // 8
        self.bits = seq_bits(s)
        self.bits["xa"] = (h + h // 2) % 2
        self.bits["xb"] = h // 2
        self.partner = {
            "c": (s + 1 - 2 * core, h),
            "ya": (s + 2 * (1 - 2 * (y % 2)), h),
            "yb": (s + 2 * (3 - 2 * y), h),
            "za": (s + 8 * (1 - 2 * (z % 2)), h),
            "zb": (s + 8 * (3 - 2 * z), h),
            "xa": (s, h + 1 - 2 * (h % 2)),
            "xb": (s, 3 - h),
            "y41": (s - 2 * y + 2 * ((y + 1) % 4), h),
            "y42": (s - 2 * y + 2 * ((y + 2) % 4), h),
            "y43": (s - 2 * y + 2 * ((y + 3) % 4), h),
            "z41": ((s + 8) % SEQ, h),
            "z42": ((s + 16) % SEQ, h),
            "z43": ((s + 24) % SEQ, h),
            "x1": (s, (h + 1) % HEADS),
            "x2": (s, (h + 2) % HEADS),
            "x3": (s, (h + 3) % HEADS),
            "next": ((s + 1) % SEQ, h),
            "prev": ((s + SEQ - 1) % SEQ, h),
        }
        self.send_sem, self.recv_sem, self.used = send_sem, recv_sem, 0

    def greet(self, names):
        semaphore = pltpu.get_barrier_semaphore()
        for name in names:
            pl.semaphore_signal(
                semaphore, inc=1, device_id=self.partner[name], device_id_type=MESH
            )

    def met(self, names):
        pl.semaphore_wait(pltpu.get_barrier_semaphore(), len(names))

    def barrier(self, names):
        self.greet(names)
        self.met(names)

    def send(self, src, dst, name):
        k = self.used
        self.used += 1
        assert k < self.send_sem.shape[0]
        copy = pltpu.make_async_remote_copy(
            src_ref=src,
            dst_ref=dst,
            send_sem=self.send_sem.at[k],
            recv_sem=self.recv_sem.at[k],
            device_id=self.partner[name],
            device_id_type=MESH,
        )
        copy.start()
        return copy


DONE = object()
SEQ_NAMES = ("c", "y41", "y42", "y43", "z41", "z42", "z43")
DOUBLING = ("c", "ya", "yb", "za", "zb")


def rows_at(start, count, unit=16):
    return pl.ds(pl.multiple_of(start, unit), count)


class Reduce:
    def __init__(self, links, path, rows, src, src_base, work, recv, out, base):
        self.links, self.path, self.rows = links, path, rows
        self.src, self.src_base = src, src_base
        self.work, self.recv, self.out, self.base = work, recv, out, base
        self.left = sizes(rows, path)
        self.start = 0
        self.copies = []

    def source(self, step):
        return (self.src, self.src_base) if step == 0 else (self.work, self.base)

    def landing(self, step):
        return self.base + self.rows - (self.rows if step == 0 else self.left[step - 1])

    def begin(self, step):
        name, size = self.path[step], self.left[step]
        ref, at = self.source(step)
        landing = self.landing(step)
        self.copies = []
        for k in range(1, ways(name)):
            away = (self.links.bits[name] + k) % ways(name)
            to = name if ways(name) == 2 else name + str(k)
            self.copies.append(
                self.links.send(
                    ref.at[rows_at(at + self.start + away * size, size)],
                    self.recv.at[pl.ds(landing + (k - 1) * size, size)],
                    to,
                )
            )

    def finish(self, step):
        name, size = self.path[step], self.left[step]
        keep = self.start + self.links.bits[name] * size
        ref, at = self.source(step)
        landing = self.landing(step)
        last = step == len(self.path) - 1
        target = self.out if last and self.out is not None else self.work
        for copy in self.copies:
            copy.wait()
        chunk = 32 if size % 32 == 0 else 16

        def add(i, carry):
            total = ref[rows_at(at + keep + i * chunk, chunk)].astype(F32)
            for k in range(ways(name) - 1):
                total += self.recv[rows_at(landing + k * size + i * chunk, chunk)].astype(F32)
            target[rows_at(self.base + keep + i * chunk, chunk)] = total.astype(BF16)
            return carry

        lax.fori_loop(0, size // chunk, add, 0)
        self.start = keep

    def send_back(self, step, columns=None):
        name, size = self.path[step], self.left[step]
        at = rows_at(self.base + self.start, size, min(size, 16))
        ref = self.out.at[at] if columns is None else self.out.at[at, pl.ds(0, columns)]
        self.copies = [
            self.links.send(ref, ref, name if ways(name) == 2 else name + str(k))
            for k in range(1, ways(name))
        ]

    def wait_back(self, step):
        name, size = self.path[step], self.left[step]
        for copy in self.copies:
            copy.wait()
        self.start = self.start - self.links.bits[name] * size


def reduce_steps(jobs):
    for job in jobs:
        job.begin(0)
    for step in range(max(len(job.path) for job in jobs)):
        yield
        for job in jobs:
            if step < len(job.path):
                job.finish(step)
                if step + 1 < len(job.path):
                    job.begin(step + 1)


def gather_steps(jobs, columns=None):
    columns = columns or [None] * len(jobs)
    for job, width in zip(jobs, columns):
        job.send_back(len(job.path) - 1, width)
    for step in range(max(len(job.path) for job in jobs) - 1, -1, -1):
        yield
        for job, width in zip(jobs, columns):
            if step < len(job.path):
                job.wait_back(step)
                if step:
                    job.send_back(step - 1, width)


def finish(*runs):
    runs = list(runs)
    while runs:
        for run in list(runs):
            if next(run, DONE) is DONE:
                runs.remove(run)


def advance(*runs):
    for run in runs:
        next(run, DONE)


def reduce_all(jobs):
    finish(reduce_steps(jobs))


def gather_all(jobs, columns=None):
    finish(gather_steps(jobs, columns))


def call(body, outs, args, scratch=(), collective=None, smem=0, copies=0, cost=None):
    vm = pl.BlockSpec(memory_space=pltpu.VMEM)
    scratch = list(scratch)
    if copies:
        scratch += [pltpu.SemaphoreType.DMA((copies,)), pltpu.SemaphoreType.DMA((copies,))]
    if collective is None:
        params = pltpu.CompilerParams(vmem_limit_bytes=VMEM_LIMIT)
    else:
        params = pltpu.CompilerParams(
            vmem_limit_bytes=VMEM_LIMIT, collective_id=collective, has_side_effects=True
        )
    in_specs = [pl.BlockSpec(memory_space=pltpu.SMEM)] * smem + [vm] * (len(args) - smem)
    return pl.pallas_call(
        body,
        out_shape=tuple(outs),
        in_specs=in_specs,
        out_specs=tuple(vm for _ in outs),
        scratch_shapes=scratch,
        compiler_params=params,
    )(*args)


class Gather:
    def __init__(self, links, path, piece, out, base):
        self.links, self.path, self.out, self.base = links, path, out, base
        self.start = position(links.bits, path) * piece
        self.left = sizes(piece * SEQ, path)
        self.copies = []

    send_back = Reduce.send_back
    wait_back = Reduce.wait_back


def gather_rows(links, src, out, paths=SEQ_PATHS):
    piece = src.shape[0] // len(paths)
    jobs = []
    for p, path in enumerate(paths):
        job = Gather(links, path, piece, out, p * piece * SEQ)
        own = rows_at(job.base + job.start, piece, 8 if piece == 8 else 16)
        out[own] = src[pl.ds(p * piece, piece)]
        jobs.append(job)
    return jobs


def own_rows(job, count):
    return job.work[rows_at(job.base + job.start, count)]


def head_spread():
    lane = lax.broadcasted_iota(jnp.int32, (HMH, MW), 1)
    row = lax.broadcasted_iota(jnp.int32, (HMH, MW), 0)
    return jnp.where((lane >= row * MP) & (lane < row * MP + MP), 1.0, 0.0)


def widen(values):
    return exact(values, head_spread(), ((1,), (0,)))


def decay_terms(decay_ref, cum_ref):
    cum_x = widen(cum_ref[...])
    step_x = -widen(decay_ref[...])
    enter_x = jnp.exp(cum_x)
    tail_x = jnp.exp(cum_x[ROWS - 1 : ROWS, :] - cum_x)
    return step_x, enter_x, tail_x


def of_channels(mixer, state, c):
    return (mixer, pl.ds(128 * c, 128)) if c < 3 else (state, pl.ds(128 * (c - 3), 128))


def conv_forward(ext, taps_m, taps_s, bias_m, bias_s, pre, post):
    for c in range(5):
        lanes = pl.ds(128 * c, 128)
        taps, own = of_channels(taps_m, taps_s, c)
        bias, own = of_channels(bias_m, bias_s, c)
        total = bias[:, own] + taps[pl.ds(0, 1), own] * ext[pl.ds(13, ROWS), lanes]
        for k in range(1, KC):
            total = total + taps[pl.ds(k, 1), own] * ext[pl.ds(13 + k, ROWS), lanes]
        pre[:, lanes] = total
        post[:, lanes] = (total * sigmoid(total)).astype(BF16)


def chain(s, gathered, logs, total, forward):
    total[...] = jnp.zeros_like(total)

    def hop(i, run):
        j = s - 1 - i if forward else s + 1 + i
        weight = jnp.exp(run)
        for seg in range(12):
            p, off = seg // 3, (seg % 3) * 32
            at = rows_at(p * 3072 + block_position(j, p) * 96 + off, 32)
            h = seg // 2
            total[pl.ds(32 * seg, 32)] += weight[h : h + 1, :] * gathered[at].astype(F32)
        return run + logs[rows_at(block_position(j, 0) * 8, 8, 8)]

    lax.fori_loop(0, s if forward else SEQ - 1 - s, hop, jnp.zeros((8, 128), F32))


def lower_mask():
    t = lax.broadcasted_iota(jnp.int32, (ROWS, ROWS), 0)
    u = lax.broadcasted_iota(jnp.int32, (ROWS, ROWS), 1)
    return u <= t


def decay_of(cum, cum_t, h, mask):
    diff = cum[:, h : h + 1] - cum_t[h : h + 1, :]
    return jnp.exp(jnp.where(mask, diff, -1e30))


def row_sums(values):
    return exact(jnp.ones((8, values.shape[1]), F32), values, ((1,), (1,)))


def column_of(rows):
    return exact(rows, jnp.full((8, 128), 0.125, F32), ((0,), (0,)))[:, 0:1]


def ssd_forward(post, step_x, enter_x, cum_ref, cumt_ref, skip, gz, state, ssd, mixed, squares):
    mixer_in = post[:, pl.ds(0, MW)].astype(F32)
    scaled = (mixer_in * step_x).astype(BF16)
    b, c = post[:, pl.ds(MW, NS)], post[:, pl.ds(MW + NS, NS)]
    gram = nt(c, b)
    mask = lower_mask()
    cum, cum_t = cum_ref[...], cumt_ref[...]
    left = lax.broadcasted_iota(jnp.int32, (ROWS, 128), 1) < MP
    carried = enter_x * nt(c, state[...]) + widen(skip[...]) * mixer_in
    for pair in range(3):
        lanes = slice(128 * pair, 128 * pair + 128)
        first = nn((gram * decay_of(cum, cum_t, 2 * pair, mask)).astype(BF16), scaled[:, lanes])
        second = nn((gram * decay_of(cum, cum_t, 2 * pair + 1, mask)).astype(BF16), scaled[:, lanes])
        ssd[:, pl.ds(128 * pair, 128)] = jnp.where(left, first, second) + carried[:, lanes]
    z = gz[...]
    m = ssd[...] * (z * sigmoid(z))
    mixed[...] = m
    squares[...] = row_sums(m * m)


def load_block(kv_all, j):
    return jnp.concatenate(
        [kv_all[rows_at(2048 * p + block_position(j, p) * 64, 64)] for p in range(4)], axis=0
    )


def causal(block):
    key = lax.broadcasted_iota(jnp.int32, block.shape, 0)
    query = lax.broadcasted_iota(jnp.int32, block.shape, 1)
    query = jnp.where(query >= ROWS, query - ROWS, query)
    return jnp.where(key <= query, block, -1e30)


def stacked_queries(q):
    q = q.astype(F32) * (HD ** -0.5)
    left = lax.broadcasted_iota(jnp.int32, (ROWS, 128), 1) < HD
    first = jnp.where(left, q, 0.0)
    second = jnp.where(left, pltpu.roll(q, HD, 1), 0.0)
    return jnp.concatenate([first, second], axis=0).astype(BF16)


FORWARD_NAMES = SEQ_NAMES + ("next", "prev", "x1", "x2", "x3")


def forward_kernel(
    x_ref, gain, wq, kvw, wm, ws, taps_m, taps_s, bias_m, bias_s, decay, skip, mgain, wmo, wao,
    cum_ref, cumt_ref, normed, q, kv_all, logs_all, gz, ext, pre, post, attended, attended_f, totals, ssd, mixed,
    squares, state, gated, summed,
    kv, logs, x_edge, edge_normed, local, states, chained, qp, acc, own_squares, slots, proj, part, work,
    recv, send_sem, recv_sem,
):
    links = Links(send_sem, recv_sem)
    s = links.s
    links.greet(FORWARD_NAMES)

    def normalise(rows):
        x = rows.astype(F32)
        r1 = lax.rsqrt(jnp.mean(x * x, axis=1, keepdims=True) + EPSILON)
        return (x * r1 * gain[...]).astype(BF16)

    n = normalise(x_ref[...])
    normed[...] = n
    left = lax.broadcasted_iota(jnp.int32, (ROWS, 128), 1) < HD
    key_cols, value_cols = nn(n, kvw[0]), nn(n, kvw[1])
    key_cols = jnp.where(links.h < 2, key_cols, pltpu.roll(key_cols, HD, 1))
    value_cols = jnp.where(links.h < 2, pltpu.roll(value_cols, HD, 1), value_cols)
    kv[...] = jnp.where(left, key_cols, value_cols).astype(BF16)
    q[...] = nn(n, wq[...]).astype(BF16)
    sums = exact(decay[...], jnp.ones((ROWS, 128), F32), ((0,), (0,)))
    logs[...] = jnp.concatenate([sums, jnp.zeros((8 - HMH, 128), F32)], axis=0)
    key_jobs = gather_rows(links, kv, kv_all) + gather_rows(links, logs, logs_all, SEQ_PATHS[:1])
    links.met(FORWARD_NAMES)
    edge_copy = links.send(x_ref.at[pl.ds(ROWS - 16, 16)], x_edge, "next")
    keys = gather_steps(key_jobs)
    advance(keys)
    gz[...] = nn(normed[...], wm[0])
    lower = jnp.where(lower_mask(), 1.0, 0.0)
    cum_ref[...] = exact(lower, decay[...], ((1,), (0,)))
    cumt_ref[...] = exact(decay[...], lower, ((0,), (1,)))
    advance(keys)
    ext[pl.ds(16, ROWS), pl.ds(0, MW)] = nn(normed[...], wm[1])
    ext[pl.ds(16, ROWS), pl.ds(MW, 256)] = nn(normed[...], ws[...])
    edge_copy.wait()
    advance(keys)
    keep = jnp.where(s > 0, 1.0, 0.0)
    edge_normed[...] = normalise(x_edge[...])
    ext[pl.ds(0, 16), pl.ds(0, MW)] = nn(edge_normed[...], wm[1]) * keep
    ext[pl.ds(0, 16), pl.ds(MW, 256)] = nn(edge_normed[...], ws[...]) * keep
    conv_forward(ext, taps_m, taps_s, bias_m, bias_s, pre, post)
    advance(keys)
    step_x, enter_x, tail_x = decay_terms(decay, cum_ref)
    tail_in = (post[:, pl.ds(0, MW)].astype(F32) * step_x * tail_x).astype(BF16)
    local[...] = tn(tail_in, post[:, pl.ds(MW, NS)]).astype(BF16)
    entering = gather_steps(gather_rows(links, local, states))
    advance(entering, keys)

    qp[...] = stacked_queries(q[...])
    scores = causal(nt(kv[...], qp[...]))
    high = jnp.max(scores, axis=0, keepdims=True)
    weights = jnp.exp(scores - high)
    acc[...] = tn(kv[...], weights.astype(BF16))
    advance(entering)
    finish(keys)

    def merge(blocks, running):
        high, total = running
        scores = [nt(block, qp[...]) for block in blocks]
        new = high
        for block in scores:
            new = jnp.maximum(new, jnp.max(block, axis=0, keepdims=True))
        fade = jnp.exp(high - new)
        weights = [jnp.exp(block - new) for block in scores]
        total = total * fade
        gained = acc[...] * fade
        for block, weight in zip(blocks, weights):
            total = total + jnp.sum(weight, axis=0, keepdims=True)
            gained = gained + tn(block, weight.astype(BF16))
        acc[...] = gained
        return new, total

    def hop(i, running):
        return merge([load_block(kv_all, 2 * i), load_block(kv_all, 2 * i + 1)], running)

    def last_hop(i, running):
        return merge([load_block(kv_all, s - 1)], running)

    running = (high, jnp.sum(weights, axis=0, keepdims=True))
    hops = s // 2
    for turn in range(4):
        running = lax.fori_loop((hops * turn) // 4, (hops * (turn + 1)) // 4, hop, running)
        advance(entering)
    running = lax.fori_loop(0, s % 2, last_hop, running)
    high, total = running
    out = acc[pl.ds(HD, HD)] / total
    out = jnp.concatenate([out[:, :ROWS], out[:, ROWS:]], axis=0).T
    attended_f[...] = out
    attended[...] = out.astype(BF16)
    totals[...] = jnp.broadcast_to(high + jnp.log(total), totals.shape)
    finish(entering)

    chain(s, states, logs_all, chained, True)
    state[...] = chained[...].astype(BF16)
    ssd_forward(post, step_x, enter_x, cum_ref, cumt_ref, skip, gz, state, ssd, mixed, own_squares)
    slots[links.h] = own_squares[...]
    copies = [links.send(own_squares, slots.at[links.h], name) for name in ("x1", "x2", "x3")]
    for c in range(2):
        lanes = pl.ds(512 * c, 512)
        proj[:, lanes] = nn(attended[...], wao[:, lanes])
    for copy in copies:
        copy.wait()
    squares[...] = (slots[0] + slots[1]) + (slots[2] + slots[3])
    scale = lax.rsqrt(column_of(squares[...]) / (MAMBA_HEADS * MP) + EPSILON)
    gated[...] = (mixed[...] * scale * mgain[...]).astype(BF16)
    for c in range(2):
        lanes = pl.ds(512 * c, 512)
        part[:, lanes] = (proj[:, lanes] + nn(gated[...], wmo[:, lanes])).astype(BF16)
    jobs = [
        Reduce(links, path, 128, part, 128 * p, work, recv, summed, 128 * p)
        for p, path in enumerate(HEAD_PATHS)
    ]
    reduce_all(jobs)
    gather_all(jobs)


def put_wide(wide, values):
    for j in range(HEADS):
        for p in range(2):
            at = 512 * p + int(head_position(j, p)) * 128
            wide[pl.ds(at, 128)] = values[128 * p : 128 * p + 128, 256 * j : 256 * j + 256].astype(BF16)


MIDDLE_NAMES = SEQ_NAMES + ("x1", "x2", "x3")


def middle_kernel(
    x_ref, summed, cot_ref, gain, gu, dw, gated, attended, wmo, wao, mixed, squares, mgain, gz, ssd,
    post, decay, cum_ref, cumt_ref, state, q, kv_all, attended_f, totals, logs_all,
    d_sum, share, x_out, xb_piece, second_part, mixgain, d_z, d_ssd, skip_part, d_scaled, d_bc, leaving, d_q, pairs,
    sn, out_acc, d_acc, back, wide, xf, xb, work, recv, wide_work, wide_recv, x_work, x_recv,
    xb_work, xb_recv,
    d_att, d_gated, own_inner, slots, local, grads, chained, qp, dop, acc, send_sem, recv_sem,
):
    links = Links(send_sem, recv_sem)
    s = links.s
    links.greet(MIDDLE_NAMES)

    residual = x_ref[...].astype(F32) + summed[...].astype(F32)
    r2 = lax.rsqrt(jnp.mean(residual * residual, axis=1, keepdims=True) + EPSILON)
    sn[...] = (residual * r2 * gain[...]).astype(BF16)
    out_acc[...] = jnp.zeros_like(out_acc)
    d_acc[...] = jnp.zeros_like(d_acc)

    def part(c, carry):
        cols = pl.ds(pl.multiple_of(c * 256, 256), 256)
        wg, wu, wd = gu[0, :, cols], gu[1, :, cols], dw[cols]
        gate, up = nn(sn[...], wg), nn(sn[...], wu)
        sig = sigmoid(gate)
        act_gate = gate * sig
        act = (act_gate * up).astype(BF16)
        out_acc[...] += nn(act, wd)
        for cb in range(4):
            at = rows_at(1536 * cb + c * 256, 256)
            xf[at] = tn(act, cot_ref[:, pl.ds(256 * cb, 256)]).astype(BF16)
        d_act = nt(cot_ref[...], wd)
        d_gate = (d_act * up * (sig * (1.0 + gate * (1.0 - sig)))).astype(BF16)
        d_up = (d_act * act_gate).astype(BF16)
        xf[rows_at(1536 * c + 512, 1024)] = tn(sn[...], d_gate).astype(BF16)
        xf[rows_at(1536 * c + 3584, 1024)] = tn(sn[...], d_up).astype(BF16)
        d_acc[...] += nt(d_gate, wg) + nt(d_up, wu)
        return carry

    lax.fori_loop(0, 2, part, 0)
    d_second = d_acc[...]
    residual = x_ref[...].astype(F32) + summed[...].astype(F32)
    second_part[...] = jnp.broadcast_to(
        jnp.sum(d_second * residual * r2, axis=0, keepdims=True), second_part.shape
    )
    weighted = d_second * gain[...]
    inner = jnp.sum(weighted * residual, axis=1, keepdims=True)
    back[...] = (r2 * weighted - residual * (r2 * r2 * r2 / D * inner)).astype(BF16)
    links.met(MIDDLE_NAMES)

    sums = [
        Reduce(links, path, 128, back, 128 * p, work, recv, d_sum, 128 * p)
        for p, path in enumerate(HEAD_PATHS)
    ]
    x_jobs = [
        Reduce(links, path, 1536, xf, 1536 * p, x_work, x_recv, x_out, 1536 * p)
        for p, path in enumerate(SEQ_PATHS)
    ]
    summing = reduce_steps(sums)
    first_weights = reduce_steps(x_jobs)
    advance(summing, first_weights)
    put_wide(wide, out_acc[...])
    advance(summing, first_weights, summing)
    back_again = gather_steps(sums)
    advance(back_again, first_weights, back_again, first_weights, back_again)

    low = (cot_ref[...].astype(F32) + d_sum[...].astype(F32)).astype(BF16)
    scale = lax.rsqrt(column_of(squares[...]) / (MAMBA_HEADS * MP) + EPSILON)
    d_gated[...] = nt(low, wmo[...])
    product = d_gated[...] * mixed[...]
    own_inner[...] = row_sums(product * mgain[...])
    slots[links.h] = own_inner[...]
    copies = [links.send(own_inner, slots.at[links.h], name) for name in ("x1", "x2", "x3")]
    mixgain[...] = jnp.broadcast_to(jnp.sum(product * scale, axis=0, keepdims=True), mixgain.shape)
    for cb in range(4):
        lanes = slice(256 * cb, 256 * cb + 256)
        xb[pl.ds(512 * cb, MW)] = tn(gated[...], low[:, lanes]).astype(BF16)
        xb[pl.ds(512 * cb + MW, 128)] = tn(attended[...], low[:, lanes]).astype(BF16)
    d_att[...] = nt(low, wao[...]).astype(BF16)
    finish(first_weights)

    xb_jobs = [
        Reduce(links, path, 512, xb, 512 * p, xb_work, xb_recv, None, 512 * p)
        for p, path in enumerate(SEQ_PATHS)
    ]
    shares = [
        Reduce(links, path, 512, wide, 512 * p, wide_work, wide_recv, None, 512 * p)
        for p, path in enumerate(HEAD_PATHS)
    ]
    others = [gather_steps(x_jobs), reduce_steps(xb_jobs), reduce_steps(shares)]
    advance(*others)
    for copy in copies:
        copy.wait()

    inner_col = column_of((slots[0] + slots[1]) + (slots[2] + slots[3]))
    d_mixed = scale * (d_gated[...] * mgain[...]) - mixed[...] * (
        scale * scale * scale / (MAMBA_HEADS * MP) * inner_col
    )
    z = gz[...]
    sig = sigmoid(z)
    ds = d_mixed * (z * sig)
    d_ssd[...] = ds
    d_z[...] = (d_mixed * ssd[...] * (sig * (1.0 + z * (1.0 - sig)))).astype(BF16)
    step_x, enter_x, _ = decay_terms(decay, cum_ref)
    b, c = post[:, pl.ds(MW, NS)], post[:, pl.ds(MW + NS, NS)]
    entered = (ds * enter_x).astype(BF16)
    local[...] = tn(entered, c).astype(BF16)
    leaving_all = gather_steps(gather_rows(links, local, grads))
    advance(leaving_all)
    mixer_in = post[:, pl.ds(0, MW)].astype(F32)
    skip_part[...] = jnp.broadcast_to(jnp.sum(ds * mixer_in, axis=0, keepdims=True), skip_part.shape)
    scaled = (mixer_in * step_x).astype(BF16)
    gram = nt(c, b)
    mask = lower_mask()
    cum, cum_t = cum_ref[...], cumt_ref[...]
    left = lax.broadcasted_iota(jnp.int32, (ROWS, 128), 1) < MP
    low = ds.astype(BF16)
    d_gram = jnp.zeros((ROWS, ROWS), F32)
    for pair in range(3):
        lanes = slice(128 * pair, 128 * pair + 128)
        halves = []
        for k in range(2):
            decay = decay_of(cum, cum_t, 2 * pair + k, mask)
            here = left if k == 0 else jnp.logical_not(left)
            mine = jnp.where(here, ds[:, lanes], 0.0).astype(BF16)
            halves.append(tn((gram * decay).astype(BF16), low[:, lanes]))
            d_gram = d_gram + decay * nt(mine, scaled[:, lanes])
        d_scaled[:, pl.ds(128 * pair, 128)] = jnp.where(left, halves[0], halves[1])
    d_gram = d_gram.astype(BF16)
    d_bc[:, pl.ds(0, NS)] = tn(d_gram, c)
    d_bc[:, pl.ds(NS, NS)] = nn(d_gram, b) + nn(entered, state[...])

    qp[...] = stacked_queries(q[...])
    d_out = d_att[...].astype(F32)
    dop[...] = jnp.concatenate(
        [jnp.where(left, 0.0, pltpu.roll(d_out, HD, 1)), jnp.where(left, 0.0, d_out)], axis=0
    ).astype(BF16)
    product = (d_out * attended_f[...]).T
    delta = jnp.concatenate(
        [
            jnp.sum(product[:HD], axis=0, keepdims=True),
            jnp.sum(product[HD:], axis=0, keepdims=True),
        ],
        axis=1,
    )
    total = totals[pl.ds(0, 1)]
    pairs[...] = jnp.zeros_like(pairs)

    def block_grads(j, masked):
        block = load_block(kv_all, j)
        scores = nt(block, qp[...])
        if masked:
            scores = causal(scores)
        probs = jnp.exp(scores - total)
        d_probs = nt(block, dop[...])
        d_scores = (probs * (d_probs - delta)).astype(BF16)
        d_pair = (nn(d_scores, qp[...]) + nn(probs.astype(BF16), dop[...])).astype(BF16)
        for p in range(4):
            at = rows_at(2048 * p + block_position(j, p) * 64, 64)
            pairs[at] = d_pair[64 * p : 64 * p + 64]
        return tn(block, d_scores)

    acc[...] = block_grads(s, True)

    def hop(i, carry):
        acc[...] += block_grads(2 * i, False) + block_grads(2 * i + 1, False)
        return carry

    def last_hop(i, carry):
        acc[...] += block_grads(s - 1, False)
        return carry

    hops, turns = s // 2, 5
    for turn in range(turns):
        advance(leaving_all, *others)
        lax.fori_loop((hops * turn) // turns, (hops * (turn + 1)) // turns, hop, 0)
    lax.fori_loop(0, s % 2, last_hop, 0)
    out = acc[pl.ds(0, HD)] * (HD ** -0.5)
    d_q[...] = jnp.concatenate([out[:, :ROWS], out[:, ROWS:]], axis=0).T.astype(BF16)
    finish(leaving_all)
    chain(s, grads, logs_all, chained, False)
    leaving[...] = chained[...].astype(BF16)
    finish(*others)
    for p, job in enumerate(shares):
        share[pl.ds(128 * p, 128)] = own_rows(job, 128)
    for p, job in enumerate(xb_jobs):
        xb_piece[pl.ds(16 * p, 16)] = own_rows(job, 16)


LAST_NAMES = SEQ_NAMES + ("next", "prev", "x1", "x2", "x3")


def last_kernel(
    pairs, leaving, d_ssd, d_scaled, d_bc, skip, decay, cum, post, pre, ext, taps_m, taps_s, d_z, d_q,
    normed, x_ref, gain, wm, ws, wq, kvw, second_part, mixgain, skip_part, xb_piece,
    xb_out, ms_out, kq_out, share, small_out,
    pair_work, pair_recv, d_pre, edge_in, shifted, d_all, acc, kernel_grads, ms, ms_work, ms_recv,
    kq, kq_work, kq_recv, wide, wide_work, wide_recv, ms_slots, kq_slots, small_work, small_recv,
    small_x, send_sem, recv_sem,
):
    links = Links(send_sem, recv_sem)
    s = links.s
    links.greet(LAST_NAMES)
    links.met(LAST_NAMES)
    pair_jobs = [
        Reduce(links, path, 2048, pairs, 2048 * p, pair_work, pair_recv, None, 2048 * p)
        for p, path in enumerate(SEQ_PATHS)
    ]
    pairing = reduce_steps(pair_jobs)
    advance(pairing)
    output_weights = gather_steps(gather_rows(links, xb_piece, xb_out))

    step_x, _, tail_x = decay_terms(decay, cum)
    b = post[:, pl.ds(MW, NS)]
    mixer_in = post[:, pl.ds(0, MW)].astype(F32)
    tail_in = (mixer_in * step_x * tail_x).astype(BF16)
    scaled_grad = d_scaled[...] + tail_x * nt(b, leaving[...])
    d_pre[:, pl.ds(0, MW)] = widen(skip[...]) * d_ssd[...] + scaled_grad * step_x
    d_pre[:, pl.ds(MW, NS)] = d_bc[:, pl.ds(0, NS)] + nn(tail_in, leaving[...])
    d_pre[:, pl.ds(MW + NS, NS)] = d_bc[:, pl.ds(NS, NS)]
    for c in range(5):
        lanes = pl.ds(128 * c, 128)
        v = pre[:, lanes]
        sig = sigmoid(v)
        dp = d_pre[:, lanes] * (sig * (1.0 + v * (1.0 - sig)))
        d_pre[:, lanes] = dp
        rows = [jnp.sum(dp * ext[pl.ds(13 + k, ROWS), lanes], axis=0, keepdims=True) for k in range(KC)]
        rows.append(jnp.sum(dp, axis=0, keepdims=True))
        rows.append(jnp.zeros((3, 128), F32))
        kernel_grads[:, lanes] = jnp.concatenate(rows, axis=0)
    edge_copy = links.send(d_pre.at[pl.ds(0, 8)], edge_in, "prev")
    advance(pairing)
    d_all[:, pl.ds(0, MW)] = d_z[...]
    d_all[:, pl.ds(1024, 128)] = d_q[...]

    def early(i, carry):
        rows = pl.ds(pl.multiple_of(i * 256, 256), 256)
        ms[rows, pl.ds(0, MW)] = tn(normed[:, rows], d_all[:, pl.ds(0, MW)]).astype(BF16)
        kq[rows] = tn(normed[:, rows], d_all[:, pl.ds(1024, 128)]).astype(BF16)
        acc[:, rows] = nt(d_all[:, pl.ds(0, MW)], wm[0, rows]) + nt(d_all[:, pl.ds(1024, 128)], wq[rows])
        return carry

    lax.fori_loop(0, 4, early, 0)
    advance(pairing)
    edge_copy.wait()
    keep = jnp.where(s < SEQ - 1, 1.0, 0.0)
    shifted[pl.ds(0, ROWS)] = d_pre[...]
    shifted[pl.ds(ROWS, 8)] = edge_in[...] * keep
    for c in range(5):
        lanes = pl.ds(128 * c, 128)
        taps, own = of_channels(taps_m, taps_s, c)
        total = taps[pl.ds(0, 1), own] * shifted[pl.ds(3, ROWS), lanes]
        for k in range(1, KC):
            total = total + taps[pl.ds(k, 1), own] * shifted[pl.ds(3 - k, ROWS), lanes]
        to = 640 + 128 * c if c < 3 else 384 + 128 * (c - 3)
        d_all[:, pl.ds(to, 128)] = total.astype(BF16)

    def middle(i, carry):
        rows = pl.ds(pl.multiple_of(i * 256, 256), 256)
        late = pl.ds(pl.multiple_of(i * 256 + 1024, 256), 256)
        mine = normed[:, rows]
        states = tn(mine, d_all[:, pl.ds(MW, 256)]).astype(BF16)
        ms[rows, pl.ds(MW, 128)] = states[:, :128]
        ms[late, pl.ds(MW, 128)] = states[:, 128:]
        ms[late, pl.ds(0, MW)] = tn(mine, d_all[:, pl.ds(640, MW)]).astype(BF16)
        return carry

    lax.fori_loop(0, 4, middle, 0)
    ms_jobs = [
        Reduce(links, path, 512, ms, 512 * p, ms_work, ms_recv, None, 512 * p)
        for p, path in enumerate(SEQ_PATHS)
    ]

    def mixer_weights():
        yield from reduce_steps(ms_jobs)
        for p, job in enumerate(ms_jobs):
            at = rows_at(job.base + job.start, 16)
            ms_slots[links.h, pl.ds(16 * p, 16)] = ms_work[at, pl.ds(MW, 128)]
        slot = ms_slots.at[links.h]
        copies = [links.send(slot, slot, name) for name in ("x1", "x2", "x3")]
        yield
        for copy in copies:
            copy.wait()
        for p, job in enumerate(ms_jobs):
            at = rows_at(job.base + job.start, 16)
            parts = [ms_slots[k, pl.ds(16 * p, 16)].astype(F32) for k in range(HEADS)]
            ms_out[at, pl.ds(0, MW)] = ms_work[at, pl.ds(0, MW)]
            ms_out[at, pl.ds(MW, 128)] = ((parts[0] + parts[1]) + (parts[2] + parts[3])).astype(BF16)
            job.out = ms_out
        yield from gather_steps(ms_jobs)

    mixing = mixer_weights()
    advance(pairing, mixing, output_weights)

    def late_part(i, carry):
        rows = pl.ds(pl.multiple_of(i * 256, 256), 256)
        total = acc[:, rows] + nt(d_all[:, pl.ds(640, MW)], wm[1, rows])
        acc[:, rows] = total + nt(d_all[:, pl.ds(MW, 256)], ws[rows])
        return carry

    lax.fori_loop(0, 4, late_part, 0)
    finish(pairing)
    for p, job in enumerate(pair_jobs):
        d_all[pl.ds(64 * p, 64), pl.ds(1152, 128)] = own_rows(job, 64)
    advance(mixing, output_weights)
    left = lax.broadcasted_iota(jnp.int32, (ROWS, 128), 1) < HD
    d_pair = d_all[:, pl.ds(1152, 128)].astype(F32)
    other = pltpu.roll(d_pair, HD, 1)
    zero = jnp.zeros_like(d_pair)
    low_head = links.h < 2
    d_keys = jnp.where(low_head, jnp.where(left, d_pair, zero), jnp.where(left, zero, other)).astype(BF16)
    d_values = jnp.where(low_head, jnp.where(left, other, zero), jnp.where(left, zero, d_pair)).astype(BF16)

    def pair_part(i, carry):
        rows = pl.ds(pl.multiple_of(i * 256, 256), 256)
        late = pl.ds(pl.multiple_of(i * 256 + 1024, 256), 256)
        pair = d_all[:, pl.ds(1152, 128)]
        kq[late] = tn(normed[:, rows], pair).astype(BF16)
        acc[:, rows] += nt(d_keys, kvw[0, rows]) + nt(d_values, kvw[1, rows])
        return carry

    lax.fori_loop(0, 4, pair_part, 0)
    kq_jobs = [
        Reduce(links, path, 512, kq, 512 * p, kq_work, kq_recv, None, 512 * p)
        for p, path in enumerate(SEQ_PATHS)
    ]

    def head_weights():
        yield from reduce_steps(kq_jobs)
        for p in (2, 3):
            job = kq_jobs[p]
            kq_slots[links.h, pl.ds(16 * (p - 2), 16)] = own_rows(job, 16)
        slot = kq_slots.at[links.h]
        copies = [links.send(slot, slot, name) for name in ("x1", "x2", "x3")]
        yield
        for copy in copies:
            copy.wait()
        for p, job in enumerate(kq_jobs):
            at = rows_at(job.base + job.start, 16)
            job.out = kq_out
            if p < 2:
                kq_out[at, pl.ds(0, 128)] = own_rows(job, 16)
            else:
                parts = [kq_slots[k, pl.ds(16 * (p - 2), 16)].astype(F32) for k in range(HEADS)]
                kq_out[at, pl.ds(0, 128)] = (parts[0] + parts[1]).astype(BF16)
                kq_out[at, pl.ds(128, 128)] = (parts[2] + parts[3]).astype(BF16)
        yield from gather_steps(kq_jobs, [128, 128, None, None])

    heading = head_weights()
    advance(heading)
    x = x_ref[...].astype(F32)
    r1 = lax.rsqrt(jnp.mean(x * x, axis=1, keepdims=True) + EPSILON)
    d_normed = acc[...]
    weighted = d_normed * gain[...]
    inner = jnp.sum(weighted * x, axis=1, keepdims=True)
    put_wide(wide, r1 * weighted - x * (r1 * r1 * r1 / D * inner))
    shares = [
        Reduce(links, path, 512, wide, 512 * p, wide_work, wide_recv, None, 512 * p)
        for p, path in enumerate(HEAD_PATHS)
    ]
    sharing = reduce_steps(shares)
    advance(sharing)
    blank = jnp.zeros((1, 256), F32)
    grads = kernel_grads[...]
    vector_rows = [
        [jnp.sum(d_normed * x * r1, axis=0, keepdims=True)],
        [second_part[pl.ds(0, 1)]],
        [grads[k : k + 1, MW:] for k in range(KC)],
        [grads[KC : KC + 1, MW:], blank, blank, blank],
        [grads[0:1, :MW], grads[KC : KC + 1, :MW], blank],
        [grads[1:2, :MW], mixgain[pl.ds(0, 1)], blank],
        [grads[2:3, :MW], skip_part[pl.ds(0, 1)], blank],
        [grads[3:4, :MW], blank, blank, blank[:, :128]],
    ]
    small_work[0] = jnp.concatenate([jnp.concatenate(row, axis=1) for row in vector_rows], axis=0)

    def vectors():
        for step, name in enumerate(DOUBLING):
            copy = links.send(small_work.at[step], small_recv.at[step], name)
            yield
            copy.wait()
            small_work[step + 1] = small_work[step] + small_recv[step]
        small_x[links.h] = small_work[5]
        copies = [links.send(small_work.at[5], small_x.at[links.h], n) for n in ("x1", "x2", "x3")]
        yield
        for copy in copies:
            copy.wait()
        total = (small_x[0] + small_x[1]) + (small_x[2] + small_x[3])
        row = lax.broadcasted_iota(jnp.int32, (8, 1024), 0)
        small_out[...] = jnp.where(row < 4, total, small_work[5])

    finish(heading, mixing, sharing, vectors(), output_weights)
    for p, job in enumerate(shares):
        share[pl.ds(128 * p, 128)] = own_rows(job, 128)


def widths_kernel(
    h, down0, down1, down2, down3, gate0, gate1, up0, up1, mix0, mix1, mix2, mix3, head, tail, query_in,
    keyval_in, x_ref, summed, out_share, cot, d_sum, in_share, small,
    down, gateup, mixout, attn, mixer, query, keyval, state, block_out, input_grads,
    gain, second, kernel_m, kernel_s, bias_m, bias_s, skip, mgain,
):
    i = pl.program_id(0)
    for cb, block in enumerate((down0, down1, down2, down3)):
        down[:, pl.ds(256 * cb, 256)] = block[...].astype(F32)
    for cb, block in enumerate((gate0, gate1)):
        gateup[0, :, pl.ds(256 * cb, 256)] = block[...].astype(F32)
    for cb, block in enumerate((up0, up1)):
        gateup[1, :, pl.ds(256 * cb, 256)] = block[...].astype(F32)

    @pl.when(i < 3)
    def _():
        for cb, block in enumerate((mix0, mix1, mix2, mix3)):
            mixout[:, pl.ds(256 * cb, 256)] = block[...].astype(F32)

    @pl.when(i == 3)
    def _():
        for cb, block in enumerate((mix0, mix1, mix2, mix3)):
            attn[:, pl.ds(256 * cb, 256)] = block[...].astype(F32)

    mixer[0] = head[:, pl.ds(0, MW)].astype(F32)
    mixer[1] = tail[:, pl.ds(0, MW)].astype(F32)
    state[:, pl.ds(0, 128)] = head[:, pl.ds(MW, 128)].astype(F32)
    state[:, pl.ds(128, 128)] = tail[:, pl.ds(MW, 128)].astype(F32)
    query[...] = query_in[...].astype(F32)
    left = lax.broadcasted_iota(jnp.int32, (256, 128), 1) < HD
    first, second_head = keyval_in[:, pl.ds(0, 128)].astype(F32), keyval_in[:, pl.ds(128, 128)].astype(F32)
    keyval[0] = jnp.where(left, first, pltpu.roll(second_head, HD, 1))
    keyval[1] = jnp.where(left, pltpu.roll(first, HD, 1), second_head)
    block_out[...] = x_ref[...].astype(F32) + summed[...].astype(F32) + out_share[...].astype(F32)
    input_grads[...] = cot[...].astype(F32) + d_sum[...].astype(F32) + in_share[...].astype(F32)

    @pl.when(i == 0)
    def _():
        gain[...] = small[pl.ds(0, 1)]
        second[...] = small[pl.ds(1, 1)]
        kernel_m[...] = small[pl.ds(4, KC), pl.ds(0, MW)]
        for k in range(KC):
            kernel_s[pl.ds(k, 1)] = small[pl.ds(2, 1), pl.ds(256 * k, 256)]
        bias_m[...] = small[pl.ds(4, 1), pl.ds(MW, MW)]
        bias_s[...] = small[pl.ds(3, 1), pl.ds(0, 256)]
        skip[...] = exact(small[pl.ds(6, 1), pl.ds(MW, MW)], head_spread(), ((1,), (1,)))
        mgain[...] = small[pl.ds(5, 1), pl.ds(MW, MW)]


def widened(h, x_out, xb_out, ms_out, kq_out, x_ref, summed, out_share, cot, d_sum, in_share, small):
    def rows(count, width, offset=0):
        return pl.BlockSpec((count, width), lambda i, h: (i + offset, 0))

    def halves(count, width):
        return pl.BlockSpec((2, count, width), lambda i, h: (0, i, 0))

    def whole(count, width):
        return pl.BlockSpec((count, width), lambda i, h: (0, 0))

    own = pl.BlockSpec((64, 256), lambda i, h: (i, h[0]))
    grid = pltpu.PrefetchScalarGridSpec(
        num_scalar_prefetch=1,
        grid=(4,),
        in_specs=[rows(128, 256, 12 * cb) for cb in range(4)]
        + [rows(256, 256, 6 * cb + 2) for cb in range(4)]
        + [rows(128, 256, 4 * cb) for cb in range(4)]
        + [rows(256, 512), rows(256, 512, 4), rows(256, 128), rows(256, 256, 4)]
        + [own, own, rows(64, 256), own, own, rows(64, 256), whole(8, D)],
        out_specs=(
            rows(128, D), halves(256, 512),
            pl.BlockSpec((128, D), lambda i, h: (jnp.minimum(i, 2), 0)), whole(128, D),
            halves(256, MW), rows(256, 128), halves(256, 128), rows(256, 256),
            rows(64, 256), rows(64, 256),
            whole(1, D), whole(1, D), whole(KC, MW), whole(KC, 256), whole(1, MW), whole(1, 256),
            whole(1, HMH), whole(1, MW),
        ),
    )
    return pl.pallas_call(
        widths_kernel,
        grid_spec=grid,
        out_shape=(
            shape((512, D), F32), shape((2, D, 512), F32), shape((MW, D), F32), shape((128, D), F32),
            shape((2, D, MW), F32), shape((D, 128), F32), shape((2, D, 128), F32), shape((D, 256), F32),
            shape((ROWS, 256), F32), shape((ROWS, 256), F32),
            shape((1, D), F32), shape((1, D), F32), shape((KC, MW), F32), shape((KC, 256), F32),
            shape((1, MW), F32), shape((1, 256), F32), shape((1, HMH), F32), shape((1, MW), F32),
        ),
        compiler_params=pltpu.CompilerParams(vmem_limit_bytes=VMEM_LIMIT),
    )(
        h, *[x_out] * 8, *[xb_out] * 4, ms_out, ms_out, kq_out, kq_out, x_ref, summed, out_share, cot,
        d_sum, in_share, small,
    )


def on_device(
    hidden_in, cotangent, log_decay, norm_gain, query_weight, keyvalue_weight, attention_output,
    mixer_weight, state_weight, kernel_mixer, kernel_state, bias_mixer, bias_state, skip_gain,
    mixer_gain, mixer_output, second_gain, gate_up, down_weight,
):
    gain1 = norm_gain.reshape(1, D)
    gain2 = second_gain.reshape(1, D)
    mgain = mixer_gain.reshape(1, MW)
    skip = skip_gain.reshape(1, HMH)
    bias_m, bias_s = bias_mixer.reshape(1, MW), bias_state.reshape(1, 256)
    (
        cum, cum_t, normed, q, kv_all, logs_all, gz, ext, pre, post, attended, attended_f, totals, ssd, mixed,
        squares, state, gated, summed,
    ) = call(
        forward_kernel,
        [
            shape((ROWS, HMH), F32), shape((HMH, ROWS), F32),
            shape((ROWS, D), BF16), shape((ROWS, 128), BF16), shape((8192, 128), BF16),
            shape((256, 128), F32), shape((ROWS, MW), F32), shape((ROWS + 16, CW), F32),
            shape((ROWS, CW), F32), shape((ROWS, CW), BF16), shape((ROWS, 128), BF16),
            shape((ROWS, 128), F32), shape((8, 512), F32), shape((ROWS, MW), F32),
            shape((ROWS, MW), F32), shape((8, ROWS), F32), shape((MW, NS), BF16),
            shape((ROWS, MW), BF16), shape((ROWS, D), BF16),
        ],
        (
            hidden_in, gain1, query_weight, keyvalue_weight, mixer_weight, state_weight, kernel_mixer,
            kernel_state, bias_m, bias_s, log_decay, skip, mgain, mixer_output, attention_output,
        ),
        scratch=[
            pltpu.VMEM((ROWS, 128), BF16), pltpu.VMEM((8, 128), F32),
            pltpu.VMEM((16, D), BF16), pltpu.VMEM((16, D), BF16),
            pltpu.VMEM((MW, NS), BF16), pltpu.VMEM((12288, NS), BF16), pltpu.VMEM((MW, NS), F32),
            pltpu.VMEM((512, 128), BF16), pltpu.VMEM((128, 512), F32), pltpu.VMEM((8, ROWS), F32),
            pltpu.VMEM((HEADS, 8, ROWS), F32), pltpu.VMEM((ROWS, D), F32),
            pltpu.VMEM((ROWS, D), BF16), pltpu.VMEM((ROWS, D), BF16), pltpu.VMEM((ROWS, D), BF16),
        ],
        collective=1, copies=80,
    )
    (
        d_sum, out_share, x_out, xb_piece, second_part, mixgain, d_z, d_ssd, skip_part, d_scaled, d_bc, leaving,
        d_q, pairs,
    ) = call(
        middle_kernel,
        [
            shape((ROWS, D), BF16), shape((ROWS, 256), BF16), shape((6144, 256), BF16),
            shape((64, 256), BF16),
            shape((8, D), F32), shape((8, MW), F32), shape((ROWS, MW), BF16), shape((ROWS, MW), F32),
            shape((8, MW), F32), shape((ROWS, MW), F32), shape((ROWS, 256), F32),
            shape((MW, NS), BF16), shape((ROWS, 128), BF16), shape((8192, 128), BF16),
        ],
        (
            hidden_in, summed, cotangent, gain2, gate_up, down_weight, gated, attended, mixer_output,
            attention_output, mixed, squares, mgain, gz, ssd, post, log_decay, cum, cum_t, state, q, kv_all,
            attended_f, totals, logs_all,
        ),
        scratch=[
            pltpu.VMEM((ROWS, D), BF16), pltpu.VMEM((ROWS, D), F32), pltpu.VMEM((ROWS, D), F32),
            pltpu.VMEM((ROWS, D), BF16), pltpu.VMEM((1024, 256), BF16), pltpu.VMEM((6144, 256), BF16),
            pltpu.VMEM((2048, 256), BF16), pltpu.VMEM((ROWS, D), BF16), pltpu.VMEM((ROWS, D), BF16),
            pltpu.VMEM((1024, 256), BF16), pltpu.VMEM((1024, 256), BF16),
            pltpu.VMEM((6144, 256), BF16), pltpu.VMEM((6144, 256), BF16),
            pltpu.VMEM((2048, 256), BF16), pltpu.VMEM((2048, 256), BF16),
            pltpu.VMEM((ROWS, 128), BF16), pltpu.VMEM((ROWS, MW), F32), pltpu.VMEM((8, ROWS), F32),
            pltpu.VMEM((HEADS, 8, ROWS), F32), pltpu.VMEM((MW, NS), BF16),
            pltpu.VMEM((12288, NS), BF16), pltpu.VMEM((MW, NS), F32), pltpu.VMEM((512, 128), BF16),
            pltpu.VMEM((512, 128), BF16), pltpu.VMEM((128, 512), F32),
        ],
        collective=2, copies=150,
    )
    xb_out, ms_out, kq_out, in_share, small = call(
        last_kernel,
        [
            shape((2048, 256), BF16), shape((2048, 512), BF16), shape((2048, 256), BF16),
            shape((ROWS, 256), BF16),
            shape((8, D), F32),
        ],
        (
            pairs, leaving, d_ssd, d_scaled, d_bc, skip, log_decay, cum, post, pre, ext, kernel_mixer,
            kernel_state, d_z, d_q, normed, hidden_in, gain1, mixer_weight, state_weight, query_weight,
            keyvalue_weight, second_part, mixgain, skip_part, xb_piece,
        ),
        scratch=[
            pltpu.VMEM((8192, 128), BF16), pltpu.VMEM((8192, 128), BF16), pltpu.VMEM((ROWS, CW), F32),
            pltpu.VMEM((8, CW), F32), pltpu.VMEM((ROWS + 8, CW), F32), pltpu.VMEM((ROWS, 1280), BF16),
            pltpu.VMEM((ROWS, D), F32), pltpu.VMEM((8, CW), F32),
            pltpu.VMEM((2048, 512), BF16), pltpu.VMEM((2048, 512), BF16), pltpu.VMEM((2048, 512), BF16),
            pltpu.VMEM((2048, 128), BF16), pltpu.VMEM((2048, 128), BF16), pltpu.VMEM((2048, 128), BF16),
            pltpu.VMEM((1024, 256), BF16), pltpu.VMEM((1024, 256), BF16), pltpu.VMEM((1024, 256), BF16),
            pltpu.VMEM((HEADS, 64, 128), BF16), pltpu.VMEM((HEADS, 32, 128), BF16),
            pltpu.VMEM((6, 8, D), F32), pltpu.VMEM((5, 8, D), F32), pltpu.VMEM((HEADS, 8, D), F32),
        ],
        collective=3, copies=190,
    )

    h = lax.axis_index("head").astype(jnp.int32).reshape(1)
    (
        down, gateup, mixout, attn, mixer, query, keyval, state_grads, block_out, input_grads,
        gain_grads, second_grads, mixkernel, statekernel, mixbias, statebias, skip_grads, mixgain_grads,
    ) = widened(
        h, x_out, xb_out, ms_out, kq_out, hidden_in, summed, out_share, cotangent, d_sum, in_share, small
    )
    return (
        block_out,
        input_grads,
        gain_grads.reshape(D),
        query,
        keyval,
        attn,
        mixer,
        state_grads,
        mixkernel,
        statekernel,
        mixbias.reshape(MW),
        statebias.reshape(256),
        skip_grads.reshape(HMH),
        mixgain_grads.reshape(MW),
        mixout,
        second_grads.reshape(D),
        gateup,
        down,
    )


def solution(mesh):
    return jax.shard_map(
        on_device,
        mesh=mesh,
        in_specs=(
            P("seq", None), P("seq", None), P("seq", "head"), P(), P(None, "head"), P(),
            P("head", None), P(None, None, "head"), P(), P(None, "head"), P(), P("head"), P(),
            P("head"), P("head"), P("head", None), P(), P(None, None, "head"), P("head", None),
        ),
        out_specs=(
            P("seq", "head"), P("seq", "head"), P(), P(None, "head"), P(), P("head", None),
            P(None, None, "head"), P(), P(None, "head"), P(), P("head"), P(), P("head"), P("head"),
            P("head", None), P(), P(None, None, "head"), P("head", None),
        ),
        check_vma=False,
    )
```

```python
import functools

import jax
import jax.numpy as jnp
from jax import lax
from jax.experimental import pallas as pl
from jax.experimental.pallas import tpu as pltpu
from jax.sharding import PartitionSpec as P

D = 1024
FF = 2048
AH = 8
KVH = 2
HD = 64
MAMBA_HEADS = 24
MP = 64
NS = 128
KC = 4
EPSILON = 1e-05
SEQ = 32
HEADS = 4
ROWS = 256
MW = 384
CW = 640
HMH = 6
HIGHEST = lax.Precision.HIGHEST
MESH = pl.DeviceIdType.MESH
F32 = jnp.float32
BF16 = jnp.bfloat16
VMEM_LIMIT = 50 * 1024 * 1024


def nn(a, b):
    return jnp.dot(a, b, preferred_element_type=F32)


def nt(a, b):
    return lax.dot_general(a, b, (((1,), (1,)), ((), ())), preferred_element_type=F32)


def tn(a, b):
    return lax.dot_general(a, b, (((0,), (0,)), ((), ())), preferred_element_type=F32)


def exact(a, b, dims):
    return lax.dot_general(
        a, b, (dims, ((), ())), precision=HIGHEST, preferred_element_type=F32
    )


def sigmoid(v):
    return 1.0 / (1.0 + jnp.exp(-v))


def shape(dims, kind):
    return jax.ShapeDtypeStruct(dims, kind)


def seq_bits(s):
    core, y, z = s % 2, (s // 2) % 4, s // 8
    return {
        "c": core,
        "ya": (y + y // 2) % 2,
        "yb": y // 2,
        "za": (z + z // 2) % 2,
        "zb": z // 2,
        "y4": y,
        "z4": z,
    }


SEQ_PATHS = (
    ("c", "ya", "yb", "z4"),
    ("c", "yb", "ya", "z4"),
    ("c", "za", "zb", "y4"),
    ("c", "zb", "za", "y4"),
)
LOG_PATH = ("c", "y4", "z4")
SHORT_PATHS = (("c", "y4", "z4"), ("c", "z4", "y4"))
HEAD_PATHS = (("xa", "xb"), ("xb", "xa"))


def ways(name):
    return 4 if name in ("y4", "z4") else 2


def position(bits, path):
    at = 0
    for name in path:
        at = at * ways(name) + bits[name]
    return at


def sizes(rows, path):
    left = []
    for name in path:
        rows = rows // ways(name)
        left.append(rows)
    return left


def block_position(s, p):
    return position(seq_bits(s), SEQ_PATHS[p])


def head_position(h, p):
    bits = {"xa": (h + h // 2) % 2, "xb": h // 2}
    return position(bits, HEAD_PATHS[p])


class Links:
    def __init__(self, send_sem, recv_sem):
        s, h = lax.axis_index("seq"), lax.axis_index("head")
        self.s, self.h = s, h
        core, y, z = s % 2, (s // 2) % 4, s // 8
        self.bits = seq_bits(s)
        self.bits["xa"] = (h + h // 2) % 2
        self.bits["xb"] = h // 2
        self.partner = {
            "c": (s + 1 - 2 * core, h),
            "ya": (s + 2 * (1 - 2 * (y % 2)), h),
            "yb": (s + 2 * (3 - 2 * y), h),
            "za": (s + 8 * (1 - 2 * (z % 2)), h),
            "zb": (s + 8 * (3 - 2 * z), h),
            "xa": (s, h + 1 - 2 * (h % 2)),
            "xb": (s, 3 - h),
            "y41": (s - 2 * y + 2 * ((y + 1) % 4), h),
            "y42": (s - 2 * y + 2 * ((y + 2) % 4), h),
            "y43": (s - 2 * y + 2 * ((y + 3) % 4), h),
            "z41": ((s + 8) % SEQ, h),
            "z42": ((s + 16) % SEQ, h),
            "z43": ((s + 24) % SEQ, h),
            "x1": (s, (h + 1) % HEADS),
            "x2": (s, (h + 2) % HEADS),
            "x3": (s, (h + 3) % HEADS),
            "next": ((s + 1) % SEQ, h),
            "prev": ((s + SEQ - 1) % SEQ, h),
        }
        self.send_sem, self.recv_sem, self.used = send_sem, recv_sem, 0

    def greet(self, names):
        semaphore = pltpu.get_barrier_semaphore()
        for name in names:
            pl.semaphore_signal(
                semaphore, inc=1, device_id=self.partner[name], device_id_type=MESH
            )

    def met(self, names):
        pl.semaphore_wait(pltpu.get_barrier_semaphore(), len(names))

    def barrier(self, names):
        self.greet(names)
        self.met(names)

    def send(self, src, dst, name):
        k = self.used
        self.used += 1
        assert k < self.send_sem.shape[0]
        copy = pltpu.make_async_remote_copy(
            src_ref=src,
            dst_ref=dst,
            send_sem=self.send_sem.at[k],
            recv_sem=self.recv_sem.at[k],
            device_id=self.partner[name],
            device_id_type=MESH,
        )
        copy.start()
        return copy


DONE = object()
SEQ_NAMES = ("c", "y41", "y42", "y43", "z41", "z42", "z43")


def rows_at(start, count, unit=16):
    return pl.ds(pl.multiple_of(start, unit), count)


class Reduce:
    def __init__(self, links, path, rows, src, src_base, work, recv, out, base):
        self.links, self.path, self.rows = links, path, rows
        self.src, self.src_base = src, src_base
        self.work, self.recv, self.out, self.base = work, recv, out, base
        self.left = sizes(rows, path)
        self.start = 0
        self.copies = []

    def source(self, step):
        return (self.src, self.src_base) if step == 0 else (self.work, self.base)

    def landing(self, step):
        return self.base + self.rows - (self.rows if step == 0 else self.left[step - 1])

    def begin(self, step):
        name, size = self.path[step], self.left[step]
        ref, at = self.source(step)
        landing = self.landing(step)
        self.copies = []
        for k in range(1, ways(name)):
            away = (self.links.bits[name] + k) % ways(name)
            to = name if ways(name) == 2 else name + str(k)
            self.copies.append(
                self.links.send(
                    ref.at[rows_at(at + self.start + away * size, size)],
                    self.recv.at[pl.ds(landing + (k - 1) * size, size)],
                    to,
                )
            )

    def finish(self, step):
        name, size = self.path[step], self.left[step]
        keep = self.start + self.links.bits[name] * size
        ref, at = self.source(step)
        landing = self.landing(step)
        last = step == len(self.path) - 1
        target = self.out if last and self.out is not None else self.work
        for copy in self.copies:
            copy.wait()
        chunk = 32 if size % 32 == 0 else 16

        def add(i, carry):
            total = ref[rows_at(at + keep + i * chunk, chunk)].astype(F32)
            for k in range(ways(name) - 1):
                total += self.recv[rows_at(landing + k * size + i * chunk, chunk)].astype(F32)
            target[rows_at(self.base + keep + i * chunk, chunk)] = total.astype(BF16)
            return carry

        lax.fori_loop(0, size // chunk, add, 0)
        self.start = keep

    def send_back(self, step, columns=None):
        name, size = self.path[step], self.left[step]
        at = rows_at(self.base + self.start, size, min(size, 16))
        ref = self.out.at[at] if columns is None else self.out.at[at, pl.ds(0, columns)]
        self.copies = [
            self.links.send(ref, ref, name if ways(name) == 2 else name + str(k))
            for k in range(1, ways(name))
        ]

    def wait_back(self, step):
        name, size = self.path[step], self.left[step]
        for copy in self.copies:
            copy.wait()
        self.start = self.start - self.links.bits[name] * size


def reduce_steps(jobs):
    for job in jobs:
        job.begin(0)
    for step in range(max(len(job.path) for job in jobs)):
        yield
        for job in jobs:
            if step < len(job.path):
                job.finish(step)
                if step + 1 < len(job.path):
                    job.begin(step + 1)


def gather_steps(jobs, columns=None):
    columns = columns or [None] * len(jobs)
    for job, width in zip(jobs, columns):
        job.send_back(len(job.path) - 1, width)
    for step in range(max(len(job.path) for job in jobs) - 1, -1, -1):
        yield
        for job, width in zip(jobs, columns):
            if step < len(job.path):
                job.wait_back(step)
                if step:
                    job.send_back(step - 1, width)


def finish(*runs):
    runs = list(runs)
    while runs:
        for run in list(runs):
            if next(run, DONE) is DONE:
                runs.remove(run)


def advance(*runs):
    for run in runs:
        next(run, DONE)


def reduce_all(jobs):
    finish(reduce_steps(jobs))


def gather_all(jobs, columns=None):
    finish(gather_steps(jobs, columns))


def call(body, outs, args, scratch=(), collective=None, smem=0, copies=0, cost=None):
    vm = pl.BlockSpec(memory_space=pltpu.VMEM)
    scratch = list(scratch)
    if copies:
        scratch += [pltpu.SemaphoreType.DMA((copies,)), pltpu.SemaphoreType.DMA((copies,))]
    if collective is None:
        params = pltpu.CompilerParams(vmem_limit_bytes=VMEM_LIMIT)
    else:
        params = pltpu.CompilerParams(
            vmem_limit_bytes=VMEM_LIMIT, collective_id=collective, has_side_effects=True
        )
    in_specs = [pl.BlockSpec(memory_space=pltpu.SMEM)] * smem + [vm] * (len(args) - smem)
    return pl.pallas_call(
        body,
        out_shape=tuple(outs),
        in_specs=in_specs,
        out_specs=tuple(vm for _ in outs),
        scratch_shapes=scratch,
        compiler_params=params,
    )(*args)


class Gather:
    def __init__(self, links, path, piece, out, base):
        self.links, self.path, self.out, self.base = links, path, out, base
        self.start = position(links.bits, path) * piece
        self.left = sizes(piece * SEQ, path)
        self.copies = []

    send_back = Reduce.send_back
    wait_back = Reduce.wait_back


def gather_rows(links, src, out, paths=SEQ_PATHS):
    piece = src.shape[0] // len(paths)
    jobs = []
    for p, path in enumerate(paths):
        job = Gather(links, path, piece, out, p * piece * SEQ)
        own = rows_at(job.base + job.start, piece, 8 if piece == 8 else 16)
        out[own] = src[pl.ds(p * piece, piece)]
        jobs.append(job)
    return jobs


def own_rows(job, count):
    return job.work[rows_at(job.base + job.start, count)]


def head_spread():
    lane = lax.broadcasted_iota(jnp.int32, (HMH, MW), 1)
    row = lax.broadcasted_iota(jnp.int32, (HMH, MW), 0)
    return jnp.where((lane >= row * MP) & (lane < row * MP + MP), 1.0, 0.0)


def widen(values):
    return exact(values, head_spread(), ((1,), (0,)))


def decay_terms(decay_ref, cum_ref):
    cum_x = widen(cum_ref[...])
    step_x = -widen(decay_ref[...])
    enter_x = jnp.exp(cum_x)
    tail_x = jnp.exp(cum_x[ROWS - 1 : ROWS, :] - cum_x)
    return step_x, enter_x, tail_x


def of_channels(mixer, state, c):
    return (mixer, pl.ds(128 * c, 128)) if c < 3 else (state, pl.ds(128 * (c - 3), 128))


def conv_forward(ext, taps_m, taps_s, bias_m, bias_s, pre, post):
    for c in range(5):
        lanes = pl.ds(128 * c, 128)
        taps, own = of_channels(taps_m, taps_s, c)
        bias, own = of_channels(bias_m, bias_s, c)
        offset = bias[own].reshape(1, 128) if c < 3 else bias[:, own]
        total = offset + taps[pl.ds(0, 1), own] * ext[pl.ds(13, ROWS), lanes]
        for k in range(1, KC):
            total = total + taps[pl.ds(k, 1), own] * ext[pl.ds(13 + k, ROWS), lanes]
        pre[:, lanes] = total
        post[:, lanes] = (total * sigmoid(total)).astype(BF16)


def scan_steps(links, local, logs, sibling, row_slots, plane_slots, halves, result, forward):
    s, core, y, z = links.s, links.bits["c"], links.bits["y4"], links.bits["z4"]
    turn = range(4) if forward else range(3, -1, -1)
    copy = links.send(local, sibling, "c")
    yield

    def log_of(j):
        return logs[rows_at(position(seq_bits(j), LOG_PATH) * 8, 8, 8)]

    def of_half(tile, k):
        return jnp.where(core == 0, tile[k : k + 1], tile[HMH // 2 + k : HMH // 2 + k + 1])

    first = core == (0 if forward else 1)
    other = s + 1 - 2 * core
    own_weight = jnp.where(first, jnp.exp(log_of(other)), 1.0)
    other_weight = jnp.where(first, 1.0, jnp.exp(log_of(s)))
    row_logs = [log_of(8 * z + 2 * k) + log_of(8 * z + 2 * k + 1) for k in range(4)]
    plane_logs = []
    for k in range(4):
        total = log_of(8 * k)
        for j in range(1, 8):
            total = total + log_of(8 * k + j)
        plane_logs.append(total)

    def exclusive(slots, tiles, at, k):
        rows = pl.ds(64 * k, 64)
        total = jnp.zeros((64, NS), F32)
        before = total
        for j in turn:
            before = jnp.where(at == j, total, before)
            total = of_half(jnp.exp(tiles[j]), k) * total + slots[j, rows].astype(F32)
        return before, total

    copy.wait()
    for k in range(3):
        rows = rows_at(192 * core + 64 * k, 64)
        total = of_half(own_weight, k) * local[rows].astype(F32)
        total = total + of_half(other_weight, k) * sibling[rows].astype(F32)
        row_slots[y, pl.ds(64 * k, 64)] = total.astype(BF16)
    slot = row_slots.at[y]
    copies = [links.send(slot, slot, name) for name in ("y41", "y42", "y43")]
    yield
    for copy in copies:
        copy.wait()
    within = []
    for k in range(3):
        before, total = exclusive(row_slots, row_logs, y, k)
        within.append(before)
        plane_slots[z, pl.ds(64 * k, 64)] = total.astype(BF16)
    slot = plane_slots.at[z]
    copies = [links.send(slot, slot, name) for name in ("z41", "z42", "z43")]
    ahead = jnp.zeros((8, 128), F32)
    passed = ahead
    for j in turn:
        passed = jnp.where(y == j, ahead, passed)
        ahead = ahead + row_logs[j]
    yield
    for copy in copies:
        copy.wait()
    for k in range(3):
        before, _ = exclusive(plane_slots, plane_logs, z, k)
        total = of_half(jnp.exp(passed), k) * before + within[k]
        halves[rows_at(192 * core + 64 * k, 64)] = total.astype(BF16)
    mine = halves.at[rows_at(192 * core, 192)]
    copy = links.send(mine, mine, "c")
    yield
    copy.wait()
    fade = jnp.exp(log_of(other))
    for k in range(HMH):
        rows = pl.ds(64 * k, 64)
        chip = halves[rows].astype(F32)
        later = fade[k : k + 1] * chip + sibling[rows].astype(F32)
        result[rows] = jnp.where(first, chip, later).astype(BF16)


def lower_mask():
    t = lax.broadcasted_iota(jnp.int32, (ROWS, ROWS), 0)
    u = lax.broadcasted_iota(jnp.int32, (ROWS, ROWS), 1)
    return u <= t


def decay_of(cum, cum_t, h, mask):
    diff = cum[:, h : h + 1] - cum_t[h : h + 1, :]
    return jnp.exp(jnp.where(mask, diff, -1e30))


def row_sums(values):
    return exact(jnp.ones((8, values.shape[1]), F32), values, ((1,), (1,)))


def column_of(rows):
    return exact(rows, jnp.full((8, 128), 0.125, F32), ((0,), (0,)))[:, 0:1]


def ssd_forward(post, step_x, enter_x, cum_ref, cumt_ref, skip, gz, state, ssd, mixed, squares):
    mixer_in = post[:, pl.ds(0, MW)].astype(F32)
    scaled = (mixer_in * step_x).astype(BF16)
    b, c = post[:, pl.ds(MW, NS)], post[:, pl.ds(MW + NS, NS)]
    gram = nt(c, b)
    mask = lower_mask()
    cum, cum_t = cum_ref[...], cumt_ref[...]
    left = lax.broadcasted_iota(jnp.int32, (ROWS, 128), 1) < MP
    carried = enter_x * nt(c, state[...]) + widen(skip[...]) * mixer_in
    for pair in range(3):
        lanes = slice(128 * pair, 128 * pair + 128)
        first = nn((gram * decay_of(cum, cum_t, 2 * pair, mask)).astype(BF16), scaled[:, lanes])
        second = nn((gram * decay_of(cum, cum_t, 2 * pair + 1, mask)).astype(BF16), scaled[:, lanes])
        ssd[:, pl.ds(128 * pair, 128)] = jnp.where(left, first, second) + carried[:, lanes]
    z = gz[...]
    m = ssd[...] * (z * sigmoid(z))
    mixed[...] = m
    squares[...] = row_sums(m * m)


def load_block(kv_all, j):
    return jnp.concatenate(
        [kv_all[rows_at(2048 * p + block_position(j, p) * 64, 64)] for p in range(4)], axis=0
    )


def causal(block):
    key = lax.broadcasted_iota(jnp.int32, block.shape, 0)
    query = lax.broadcasted_iota(jnp.int32, block.shape, 1)
    query = jnp.where(query >= ROWS, query - ROWS, query)
    return jnp.where(key <= query, block, -1e30)


def stacked_queries(q):
    q = q.astype(F32) * (HD ** -0.5)
    left = lax.broadcasted_iota(jnp.int32, (ROWS, 128), 1) < HD
    first = jnp.where(left, q, 0.0)
    second = jnp.where(left, pltpu.roll(q, HD, 1), 0.0)
    return jnp.concatenate([first, second], axis=0).astype(BF16)


FORWARD_NAMES = SEQ_NAMES + ("next", "prev", "x1", "x2", "x3")


def forward_kernel(
    x_ref, gain, wq, kvw, wm, ws, taps_m, taps_s, bias_m, bias_s, decay, skip, mgain, wmo, wao,
    cum_ref, cumt_ref, normed, q, kv_all, logs_all, gz, ext, pre, post, attended, attended_f, totals, ssd, mixed,
    squares, state, gated, summed,
    kv, logs, x_edge, edge_normed, local, sibling, row_slots, plane_slots, halves, qp, acc, own_squares, slots, proj, part, work,
    recv, send_sem, recv_sem,
):
    links = Links(send_sem, recv_sem)
    s = links.s
    links.greet(FORWARD_NAMES)

    def normalise(rows):
        x = rows.astype(F32)
        r1 = lax.rsqrt(jnp.mean(x * x, axis=1, keepdims=True) + EPSILON)
        return (x * r1 * gain[...]).astype(BF16)

    n = normalise(x_ref[...])
    normed[...] = n
    left = lax.broadcasted_iota(jnp.int32, (ROWS, 128), 1) < HD
    key_cols, value_cols = nn(n, kvw[0]), nn(n, kvw[1])
    key_cols = jnp.where(links.h < 2, key_cols, pltpu.roll(key_cols, HD, 1))
    value_cols = jnp.where(links.h < 2, pltpu.roll(value_cols, HD, 1), value_cols)
    kv[...] = jnp.where(left, key_cols, value_cols).astype(BF16)
    q[...] = nn(n, wq[...]).astype(BF16)
    sums = exact(decay[...], jnp.ones((ROWS, 128), F32), ((0,), (0,)))
    logs[...] = jnp.concatenate([sums, jnp.zeros((8 - HMH, 128), F32)], axis=0)
    key_jobs = gather_rows(links, kv, kv_all)
    log_jobs = gather_rows(links, logs, logs_all, (LOG_PATH,))
    links.met(FORWARD_NAMES)
    edge_copy = links.send(x_ref.at[pl.ds(ROWS - 16, 16)], x_edge, "next")
    keys, every_log = gather_steps(key_jobs), gather_steps(log_jobs)
    advance(keys, every_log)
    gz[...] = nn(normed[...], wm[0])
    lower = jnp.where(lower_mask(), 1.0, 0.0)
    cum_ref[...] = exact(lower, decay[...], ((1,), (0,)))
    cumt_ref[...] = exact(decay[...], lower, ((0,), (1,)))
    advance(keys, every_log)
    ext[pl.ds(16, ROWS), pl.ds(0, MW)] = nn(normed[...], wm[1])
    ext[pl.ds(16, ROWS), pl.ds(MW, 256)] = nn(normed[...], ws[...])
    edge_copy.wait()
    advance(keys, every_log)
    keep = jnp.where(s > 0, 1.0, 0.0)
    edge_normed[...] = normalise(x_edge[...])
    ext[pl.ds(0, 16), pl.ds(0, MW)] = nn(edge_normed[...], wm[1]) * keep
    ext[pl.ds(0, 16), pl.ds(MW, 256)] = nn(edge_normed[...], ws[...]) * keep
    conv_forward(ext, taps_m, taps_s, bias_m, bias_s, pre, post)
    advance(keys)
    finish(every_log)
    step_x, enter_x, tail_x = decay_terms(decay, cum_ref)
    tail_in = (post[:, pl.ds(0, MW)].astype(F32) * step_x * tail_x).astype(BF16)
    local[...] = tn(tail_in, post[:, pl.ds(MW, NS)]).astype(BF16)
    entering = scan_steps(
        links, local, logs_all, sibling, row_slots, plane_slots, halves, state, True
    )
    advance(entering)

    qp[...] = stacked_queries(q[...])
    scores = causal(nt(kv[...], qp[...]))
    high = jnp.max(scores, axis=0, keepdims=True)
    weights = jnp.exp(scores - high)
    acc[...] = tn(kv[...], weights.astype(BF16))
    advance(entering)
    finish(keys)

    def merge(blocks, running):
        high, total = running
        scores = [nt(block, qp[...]) for block in blocks]
        new = high
        for block in scores:
            new = jnp.maximum(new, jnp.max(block, axis=0, keepdims=True))
        fade = jnp.exp(high - new)
        weights = [jnp.exp(block - new) for block in scores]
        total = total * fade
        gained = acc[...] * fade
        for block, weight in zip(blocks, weights):
            total = total + jnp.sum(weight, axis=0, keepdims=True)
            gained = gained + tn(block, weight.astype(BF16))
        acc[...] = gained
        return new, total

    def hop(i, running):
        return merge([load_block(kv_all, 2 * i), load_block(kv_all, 2 * i + 1)], running)

    def last_hop(i, running):
        return merge([load_block(kv_all, s - 1)], running)

    running = (high, jnp.sum(weights, axis=0, keepdims=True))
    hops = s // 2
    for turn in range(4):
        if turn == 3:
            finish(entering)
            ssd_forward(
                post, step_x, enter_x, cum_ref, cumt_ref, skip, gz, state, ssd, mixed, own_squares
            )
            slots[links.h] = own_squares[...]
            square_copies = [
                links.send(own_squares, slots.at[links.h], name) for name in ("x1", "x2", "x3")
            ]
        running = lax.fori_loop((hops * turn) // 4, (hops * (turn + 1)) // 4, hop, running)
        advance(entering)
    running = lax.fori_loop(0, s % 2, last_hop, running)
    high, total = running
    out = acc[pl.ds(HD, HD)] / total
    out = jnp.concatenate([out[:, :ROWS], out[:, ROWS:]], axis=0).T
    attended_f[...] = out
    attended[...] = out.astype(BF16)
    totals[...] = jnp.broadcast_to(high + jnp.log(total), totals.shape)
    for c in range(2):
        lanes = pl.ds(512 * c, 512)
        proj[:, lanes] = nn(attended[...], wao[:, lanes])
    for copy in square_copies:
        copy.wait()
    squares[...] = (slots[0] + slots[1]) + (slots[2] + slots[3])
    scale = lax.rsqrt(column_of(squares[...]) / (MAMBA_HEADS * MP) + EPSILON)
    gated[...] = (mixed[...] * scale * mgain[...].reshape(1, MW)).astype(BF16)
    for c in range(2):
        lanes = pl.ds(512 * c, 512)
        part[:, lanes] = (proj[:, lanes] + nn(gated[...], wmo[:, lanes])).astype(BF16)
    jobs = [
        Reduce(links, path, 64, part, 64 * p, work, recv, summed, 64 * p)
        for p, path in enumerate(HEAD_PATHS * 2)
    ]
    reduce_all(jobs)
    gather_all(jobs)


def put_wide(wide, values):
    for j in range(HEADS):
        for p in range(2):
            at = 512 * p + int(head_position(j, p)) * 128
            wide[pl.ds(at, 128)] = values[128 * p : 128 * p + 128, 256 * j : 256 * j + 256].astype(BF16)


MIDDLE_NAMES = SEQ_NAMES + ("x1", "x2", "x3")


def middle_kernel(
    x_ref, summed, cot_ref, gain, gu, dw, gated, attended, wmo, wao, mixed, squares, mgain, gz, ssd,
    post, decay, cum_ref, cumt_ref, state, q, kv_all, attended_f, totals, logs_all,
    d_sum, share, x_piece, xb_piece, second_part, mixgain, d_z, d_ssd, skip_part, d_scaled, d_bc, leaving, d_q, pairs,
    sn, out_acc, d_acc, back, wide, xf, xb, work, recv, wide_work, wide_recv, x_work, x_recv,
    xb_work, xb_recv,
    d_att, d_gated, own_inner, slots, local, sibling, row_slots, plane_slots, halves, qp, dop, acc, send_sem, recv_sem,
):
    links = Links(send_sem, recv_sem)
    s = links.s
    links.greet(MIDDLE_NAMES)

    residual = x_ref[...].astype(F32) + summed[...].astype(F32)
    r2 = lax.rsqrt(jnp.mean(residual * residual, axis=1, keepdims=True) + EPSILON)
    sn[...] = (residual * r2 * gain[...]).astype(BF16)
    out_acc[...] = jnp.zeros_like(out_acc)
    d_acc[...] = jnp.zeros_like(d_acc)

    def part(c, carry):
        cols = pl.ds(pl.multiple_of(c * 256, 256), 256)
        wg, wu, wd = gu[0, :, cols], gu[1, :, cols], dw[cols]
        gate, up = nn(sn[...], wg), nn(sn[...], wu)
        sig = sigmoid(gate)
        act_gate = gate * sig
        act = (act_gate * up).astype(BF16)
        out_acc[...] += nn(act, wd)
        for cb in range(4):
            at = rows_at(1536 * cb + c * 256, 256)
            xf[at] = tn(act, cot_ref[:, pl.ds(256 * cb, 256)]).astype(BF16)
        d_act = nt(cot_ref[...], wd)
        d_gate = (d_act * up * (sig * (1.0 + gate * (1.0 - sig)))).astype(BF16)
        d_up = (d_act * act_gate).astype(BF16)
        xf[rows_at(1536 * c + 512, 1024)] = tn(sn[...], d_gate).astype(BF16)
        xf[rows_at(1536 * c + 3584, 1024)] = tn(sn[...], d_up).astype(BF16)
        d_acc[...] += nt(d_gate, wg) + nt(d_up, wu)
        return carry

    lax.fori_loop(0, 2, part, 0)
    d_second = d_acc[...]
    residual = x_ref[...].astype(F32) + summed[...].astype(F32)
    second_part[...] = jnp.broadcast_to(
        jnp.sum(d_second * residual * r2, axis=0, keepdims=True), second_part.shape
    )
    weighted = d_second * gain[...]
    inner = jnp.sum(weighted * residual, axis=1, keepdims=True)
    back[...] = (r2 * weighted - residual * (r2 * r2 * r2 / D * inner)).astype(BF16)
    links.met(MIDDLE_NAMES)

    sums = [
        Reduce(links, path, 64, back, 64 * p, work, recv, d_sum, 64 * p)
        for p, path in enumerate(HEAD_PATHS * 2)
    ]
    x_jobs = [
        Reduce(links, path, 1536, xf, 1536 * p, x_work, x_recv, None, 1536 * p)
        for p, path in enumerate(SEQ_PATHS)
    ]
    summing = reduce_steps(sums)
    first_weights = reduce_steps(x_jobs)
    advance(summing, first_weights)
    put_wide(wide, out_acc[...])
    advance(summing, first_weights, summing)
    back_again = gather_steps(sums)
    advance(back_again, back_again, first_weights, back_again)

    low = (cot_ref[...].astype(F32) + d_sum[...].astype(F32)).astype(BF16)
    scale = lax.rsqrt(column_of(squares[...]) / (MAMBA_HEADS * MP) + EPSILON)
    d_gated[...] = nt(low, wmo[...])
    product = d_gated[...] * mixed[...]
    own_inner[...] = row_sums(product * mgain[...].reshape(1, MW))
    slots[links.h] = own_inner[...]
    copies = [links.send(own_inner, slots.at[links.h], name) for name in ("x1", "x2", "x3")]
    mixgain[...] = jnp.broadcast_to(jnp.sum(product * scale, axis=0, keepdims=True), mixgain.shape)
    for cb in range(4):
        lanes = slice(256 * cb, 256 * cb + 256)
        xb[pl.ds(512 * cb, MW)] = tn(gated[...], low[:, lanes]).astype(BF16)
        xb[pl.ds(512 * cb + MW, 128)] = tn(attended[...], low[:, lanes]).astype(BF16)
    d_att[...] = nt(low, wao[...]).astype(BF16)

    xb_jobs = [
        Reduce(links, path, 512, xb, 512 * p, xb_work, xb_recv, None, 512 * p)
        for p, path in enumerate(SEQ_PATHS)
    ]
    shares = [
        Reduce(links, path, 512, wide, 512 * p, wide_work, wide_recv, None, 512 * p)
        for p, path in enumerate(HEAD_PATHS)
    ]
    others = [first_weights, reduce_steps(xb_jobs), reduce_steps(shares)]
    advance(*others)
    for copy in copies:
        copy.wait()

    inner_col = column_of((slots[0] + slots[1]) + (slots[2] + slots[3]))
    d_mixed = scale * (d_gated[...] * mgain[...].reshape(1, MW)) - mixed[...] * (
        scale * scale * scale / (MAMBA_HEADS * MP) * inner_col
    )
    z = gz[...]
    sig = sigmoid(z)
    ds = d_mixed * (z * sig)
    d_ssd[...] = ds
    d_z[...] = (d_mixed * ssd[...] * (sig * (1.0 + z * (1.0 - sig)))).astype(BF16)
    step_x, enter_x, _ = decay_terms(decay, cum_ref)
    b, c = post[:, pl.ds(MW, NS)], post[:, pl.ds(MW + NS, NS)]
    entered = (ds * enter_x).astype(BF16)
    local[...] = tn(entered, c).astype(BF16)
    leaving_all = scan_steps(
        links, local, logs_all, sibling, row_slots, plane_slots, halves, leaving, False
    )
    advance(leaving_all)
    mixer_in = post[:, pl.ds(0, MW)].astype(F32)
    skip_part[...] = jnp.broadcast_to(jnp.sum(ds * mixer_in, axis=0, keepdims=True), skip_part.shape)
    scaled = (mixer_in * step_x).astype(BF16)
    gram = nt(c, b)
    mask = lower_mask()
    cum, cum_t = cum_ref[...], cumt_ref[...]
    left = lax.broadcasted_iota(jnp.int32, (ROWS, 128), 1) < MP
    low = ds.astype(BF16)
    d_gram = jnp.zeros((ROWS, ROWS), F32)
    for pair in range(3):
        lanes = slice(128 * pair, 128 * pair + 128)
        halves = []
        for k in range(2):
            decay = decay_of(cum, cum_t, 2 * pair + k, mask)
            here = left if k == 0 else jnp.logical_not(left)
            mine = jnp.where(here, ds[:, lanes], 0.0).astype(BF16)
            halves.append(tn((gram * decay).astype(BF16), low[:, lanes]))
            d_gram = d_gram + decay * nt(mine, scaled[:, lanes])
        d_scaled[:, pl.ds(128 * pair, 128)] = jnp.where(left, halves[0], halves[1])
    d_gram = d_gram.astype(BF16)
    d_bc[:, pl.ds(0, NS)] = tn(d_gram, c)
    d_bc[:, pl.ds(NS, NS)] = nn(d_gram, b) + nn(entered, state[...])

    qp[...] = stacked_queries(q[...])
    d_out = d_att[...].astype(F32)
    dop[...] = jnp.concatenate(
        [jnp.where(left, 0.0, pltpu.roll(d_out, HD, 1)), jnp.where(left, 0.0, d_out)], axis=0
    ).astype(BF16)
    product = (d_out * attended_f[...]).T
    delta = jnp.concatenate(
        [
            jnp.sum(product[:HD], axis=0, keepdims=True),
            jnp.sum(product[HD:], axis=0, keepdims=True),
        ],
        axis=1,
    )
    total = totals[pl.ds(0, 1)]
    pairs[...] = jnp.zeros_like(pairs)

    def block_grads(j, masked):
        block = load_block(kv_all, j)
        scores = nt(block, qp[...])
        if masked:
            scores = causal(scores)
        probs = jnp.exp(scores - total)
        d_probs = nt(block, dop[...])
        d_scores = (probs * (d_probs - delta)).astype(BF16)
        d_pair = (nn(d_scores, qp[...]) + nn(probs.astype(BF16), dop[...])).astype(BF16)
        for p in range(4):
            at = rows_at(2048 * p + block_position(j, p) * 64, 64)
            pairs[at] = d_pair[64 * p : 64 * p + 64]
        return tn(block, d_scores)

    acc[...] = block_grads(s, True)

    def hop(i, carry):
        acc[...] += block_grads(2 * i, False) + block_grads(2 * i + 1, False)
        return carry

    def last_hop(i, carry):
        acc[...] += block_grads(s - 1, False)
        return carry

    hops, turns = s // 2, 5
    for turn in range(turns):
        advance(leaving_all, *others)
        lax.fori_loop((hops * turn) // turns, (hops * (turn + 1)) // turns, hop, 0)
    lax.fori_loop(0, s % 2, last_hop, 0)
    out = acc[pl.ds(0, HD)] * (HD ** -0.5)
    d_q[...] = jnp.concatenate([out[:, :ROWS], out[:, ROWS:]], axis=0).T.astype(BF16)
    finish(leaving_all)
    finish(*others)
    for p, job in enumerate(shares):
        share[pl.ds(128 * p, 128)] = own_rows(job, 128)
    for p, job in enumerate(xb_jobs):
        xb_piece[pl.ds(16 * p, 16)] = own_rows(job, 16)
    for p, job in enumerate(x_jobs):
        x_piece[pl.ds(48 * p, 48)] = own_rows(job, 48)


LAST_NAMES = SEQ_NAMES + ("next", "prev", "x1", "x2", "x3")


def last_kernel(
    pairs, leaving, d_ssd, d_scaled, d_bc, skip, decay, cum, post, pre, ext, taps_m, taps_s, d_z, d_q,
    normed, x_ref, gain, wm, ws, wq, kvw, second_part, mixgain, skip_part, x_piece, xb_piece,
    x_out, xb_out, zq_out, mix_out, st_out, kv_out, share, small_out,
    pair_work, pair_recv, d_pre, edge_in, shifted, d_all, acc, kernel_grads,
    zq, zq_work, zq_recv, mix, mix_work, mix_recv, st, st_work, st_recv, kv, kv_work, kv_recv,
    wide, wide_work, wide_recv, st_slots, kv_slots, small_work, small_slots, send_sem, recv_sem,
):
    links = Links(send_sem, recv_sem)
    s = links.s
    links.greet(LAST_NAMES)
    links.met(LAST_NAMES)

    def reduces(paths, rows, src, work, recv):
        return [
            Reduce(links, path, rows, src, rows * k, work, recv, None, rows * k)
            for k, path in enumerate(paths)
        ]

    pair_jobs = reduces(SEQ_PATHS, 2048, pairs, pair_work, pair_recv)
    pairing = reduce_steps(pair_jobs)
    advance(pairing)
    feed_weights = gather_steps(gather_rows(links, x_piece, x_out))
    output_weights = gather_steps(gather_rows(links, xb_piece, xb_out))

    step_x, _, tail_x = decay_terms(decay, cum)
    b = post[:, pl.ds(MW, NS)]
    mixer_in = post[:, pl.ds(0, MW)].astype(F32)
    tail_in = (mixer_in * step_x * tail_x).astype(BF16)
    scaled_grad = d_scaled[...] + tail_x * nt(b, leaving[...])
    d_pre[:, pl.ds(0, MW)] = widen(skip[...]) * d_ssd[...] + scaled_grad * step_x
    d_pre[:, pl.ds(MW, NS)] = d_bc[:, pl.ds(0, NS)] + nn(tail_in, leaving[...])
    d_pre[:, pl.ds(MW + NS, NS)] = d_bc[:, pl.ds(NS, NS)]
    for c in range(5):
        lanes = pl.ds(128 * c, 128)
        v = pre[:, lanes]
        sig = sigmoid(v)
        dp = d_pre[:, lanes] * (sig * (1.0 + v * (1.0 - sig)))
        d_pre[:, lanes] = dp
    edge_copy = links.send(d_pre.at[pl.ds(0, 8)], edge_in, "prev")
    advance(pairing, feed_weights)
    for c in range(5):
        lanes = pl.ds(128 * c, 128)
        dp = d_pre[:, lanes]
        rows = [jnp.sum(dp * ext[pl.ds(13 + k, ROWS), lanes], axis=0, keepdims=True) for k in range(KC)]
        rows.append(jnp.sum(dp, axis=0, keepdims=True))
        rows.append(jnp.zeros((3, 128), F32))
        kernel_grads[:, lanes] = jnp.concatenate(rows, axis=0)
    d_all[:, pl.ds(0, MW)] = d_z[...]
    d_all[:, pl.ds(MW, 128)] = d_q[...]

    def early(i, carry):
        rows = pl.ds(pl.multiple_of(i * 256, 256), 256)
        block = tn(normed[:, rows], d_all[:, pl.ds(0, 512)]).astype(BF16)
        for k in range(4):
            zq[rows_at(1024 * k + i * 256, 256)] = block[:, 128 * k : 128 * k + 128]
        acc[:, rows] = nt(d_all[:, pl.ds(0, MW)], wm[0, rows]) + nt(d_all[:, pl.ds(MW, 128)], wq[rows])
        return carry

    lax.fori_loop(0, 4, early, 0)
    zq_jobs = reduces(SHORT_PATHS, 2048, zq, zq_work, zq_recv)

    def gate_weights():
        yield from reduce_steps(zq_jobs)
        for job in zq_jobs:
            at = rows_at(job.base + job.start, 64)
            zq_out[at] = zq_work[at]
            job.out = zq_out
        yield from gather_steps(zq_jobs)

    zq_weights = gate_weights()
    advance(zq_weights, pairing, feed_weights, output_weights)
    edge_copy.wait()
    keep = jnp.where(s < SEQ - 1, 1.0, 0.0)
    shifted[pl.ds(0, ROWS)] = d_pre[...]
    shifted[pl.ds(ROWS, 8)] = edge_in[...] * keep
    for c in range(5):
        lanes = pl.ds(128 * c, 128)
        taps, own = of_channels(taps_m, taps_s, c)
        total = taps[pl.ds(0, 1), own] * shifted[pl.ds(3, ROWS), lanes]
        for k in range(1, KC):
            total = total + taps[pl.ds(k, 1), own] * shifted[pl.ds(3 - k, ROWS), lanes]
        d_all[:, pl.ds(512 + 128 * c, 128)] = total.astype(BF16)

    def middle(i, carry):
        rows = pl.ds(pl.multiple_of(i * 256, 256), 256)
        block = tn(normed[:, rows], d_all[:, pl.ds(512, CW)]).astype(BF16)
        mix[rows] = block[:, :MW]
        st[rows] = block[:, MW:]
        return carry

    lax.fori_loop(0, 4, middle, 0)
    mix_jobs = reduces(SHORT_PATHS, 512, mix, mix_work, mix_recv)
    st_jobs = reduces(SHORT_PATHS, 512, st, st_work, st_recv)

    def mixer_weights():
        yield from reduce_steps(mix_jobs + st_jobs)
        for k, job in enumerate(st_jobs):
            st_slots[links.h, pl.ds(16 * k, 16)] = own_rows(job, 16)
        slot = st_slots.at[links.h]
        copies = [links.send(slot, slot, name) for name in ("x1", "x2", "x3")]
        for job in mix_jobs:
            at = rows_at(job.base + job.start, 16)
            mix_out[at] = mix_work[at]
            job.out = mix_out
        yield
        for copy in copies:
            copy.wait()
        for k, job in enumerate(st_jobs):
            at = rows_at(job.base + job.start, 16)
            parts = [st_slots[j, pl.ds(16 * k, 16)].astype(F32) for j in range(HEADS)]
            st_out[at] = ((parts[0] + parts[1]) + (parts[2] + parts[3])).astype(BF16)
            job.out = st_out
        yield from gather_steps(mix_jobs + st_jobs)

    mixing = mixer_weights()
    advance(mixing, pairing)

    def late_part(i, carry):
        rows = pl.ds(pl.multiple_of(i * 256, 256), 256)
        total = acc[:, rows] + nt(d_all[:, pl.ds(512, MW)], wm[1, rows])
        acc[:, rows] = total + nt(d_all[:, pl.ds(512 + MW, 256)], ws[rows])
        return carry

    lax.fori_loop(0, 4, late_part, 0)
    advance(zq_weights, feed_weights, output_weights)
    finish(pairing)
    for p, job in enumerate(pair_jobs):
        d_all[pl.ds(64 * p, 64), pl.ds(1152, 128)] = own_rows(job, 64)
    left = lax.broadcasted_iota(jnp.int32, (ROWS, 128), 1) < HD
    d_pair = d_all[:, pl.ds(1152, 128)].astype(F32)
    other = pltpu.roll(d_pair, HD, 1)
    zero = jnp.zeros_like(d_pair)
    low_head = links.h < 2
    d_keys = jnp.where(low_head, jnp.where(left, d_pair, zero), jnp.where(left, zero, other)).astype(BF16)
    d_values = jnp.where(low_head, jnp.where(left, other, zero), jnp.where(left, zero, d_pair)).astype(BF16)

    def pair_part(i, carry):
        rows = pl.ds(pl.multiple_of(i * 256, 256), 256)
        kv[rows] = tn(normed[:, rows], d_all[:, pl.ds(1152, 128)]).astype(BF16)
        acc[:, rows] += nt(d_keys, kvw[0, rows]) + nt(d_values, kvw[1, rows])
        return carry

    lax.fori_loop(0, 4, pair_part, 0)
    kv_jobs = reduces(SHORT_PATHS, 512, kv, kv_work, kv_recv)

    def head_weights():
        yield from reduce_steps(kv_jobs)
        for k, job in enumerate(kv_jobs):
            kv_slots[links.h, pl.ds(16 * k, 16)] = own_rows(job, 16)
        slot = kv_slots.at[links.h]
        copies = [links.send(slot, slot, name) for name in ("x1", "x2", "x3")]
        yield
        for copy in copies:
            copy.wait()
        for k, job in enumerate(kv_jobs):
            at = rows_at(job.base + job.start, 16)
            parts = [kv_slots[j, pl.ds(16 * k, 16)].astype(F32) for j in range(HEADS)]
            kv_out[at, pl.ds(0, 128)] = (parts[0] + parts[1]).astype(BF16)
            kv_out[at, pl.ds(128, 128)] = (parts[2] + parts[3]).astype(BF16)
            job.out = kv_out
        yield from gather_steps(kv_jobs)

    heading = head_weights()
    advance(heading)
    x = x_ref[...].astype(F32)
    r1 = lax.rsqrt(jnp.mean(x * x, axis=1, keepdims=True) + EPSILON)
    d_normed = acc[...]
    blank = jnp.zeros((1, 256), F32)
    grads = kernel_grads[...]
    vector_rows = [
        [jnp.sum(d_normed * x * r1, axis=0, keepdims=True)],
        [second_part[pl.ds(0, 1)]],
        [grads[k : k + 1, MW:] for k in range(KC)],
        [grads[KC : KC + 1, MW:], blank, blank, blank],
        [grads[0:1, :MW], grads[KC : KC + 1, :MW], blank],
        [grads[1:2, :MW], mixgain[pl.ds(0, 1)], blank],
        [grads[2:3, :MW], skip_part[pl.ds(0, 1)], blank],
        [grads[3:4, :MW], blank, blank, blank[:, :128]],
    ]
    small_work[0] = jnp.concatenate([jnp.concatenate(row, axis=1) for row in vector_rows], axis=0)

    def vectors():
        at = 0
        for names, me in (
            (("c",), links.bits["c"]),
            (("y41", "y42", "y43"), links.bits["y4"]),
            (("z41", "z42", "z43"), links.bits["z4"]),
            (("x1", "x2", "x3"), links.h),
        ):
            step, count = at, len(names) + 1
            slots = small_slots.at[pl.ds(4 * step, 4)]
            slots[me] = small_work[step]
            copies = [links.send(small_work.at[step], slots.at[me], name) for name in names]
            yield
            for copy in copies:
                copy.wait()
            total = slots[0] + slots[1]
            if count == 4:
                total = total + (slots[2] + slots[3])
            small_work[step + 1] = total
            at += 1
        row = lax.broadcasted_iota(jnp.int32, (8, 1024), 0)
        small_out[...] = jnp.where(row < 4, small_work[4], small_work[3])

    adding = vectors()
    advance(adding)
    weighted = d_normed * gain[...]
    inner = jnp.sum(weighted * x, axis=1, keepdims=True)
    put_wide(wide, r1 * weighted - x * (r1 * r1 * r1 / D * inner))
    shares = [
        Reduce(links, path, 512, wide, 512 * p, wide_work, wide_recv, None, 512 * p)
        for p, path in enumerate(HEAD_PATHS)
    ]
    sharing = reduce_steps(shares)
    advance(sharing)
    finish(heading, adding, mixing, sharing, zq_weights, feed_weights, output_weights)
    for p, job in enumerate(shares):
        share[pl.ds(128 * p, 128)] = own_rows(job, 128)


def widths_kernel(
    h, down0, down1, down2, down3, gate0, gate1, up0, up1, mix0, mix1, mix2, mix3, z0, z1, z2, query_in,
    raw_in, state_in, keyval_in, x_ref, summed, out_share, cot, d_sum, in_share, small,
    down, gateup, mixout, attn, mixer, query, keyval, state, block_out, input_grads,
    gain, second, kernel_m, kernel_s, bias_m, bias_s, skip, mgain,
):
    i = pl.program_id(0)
    for cb, block in enumerate((down0, down1, down2, down3)):
        down[:, pl.ds(256 * cb, 256)] = block[...].astype(F32)
    for cb, block in enumerate((gate0, gate1)):
        gateup[0, :, pl.ds(256 * cb, 256)] = block[...].astype(F32)
    for cb, block in enumerate((up0, up1)):
        gateup[1, :, pl.ds(256 * cb, 256)] = block[...].astype(F32)

    @pl.when(i < 3)
    def _():
        for cb, block in enumerate((mix0, mix1, mix2, mix3)):
            mixout[:, pl.ds(256 * cb, 256)] = block[...].astype(F32)

    @pl.when(i == 3)
    def _():
        for cb, block in enumerate((mix0, mix1, mix2, mix3)):
            attn[:, pl.ds(256 * cb, 256)] = block[...].astype(F32)

    for k, block in enumerate((z0, z1, z2)):
        mixer[0, :, pl.ds(128 * k, 128)] = block[...].astype(F32)
    mixer[1] = raw_in[...].astype(F32)
    state[...] = state_in[...].astype(F32)
    query[...] = query_in[...].astype(F32)
    left = lax.broadcasted_iota(jnp.int32, (256, 128), 1) < HD
    first, second_head = keyval_in[:, pl.ds(0, 128)].astype(F32), keyval_in[:, pl.ds(128, 128)].astype(F32)
    keyval[0] = jnp.where(left, first, pltpu.roll(second_head, HD, 1))
    keyval[1] = jnp.where(left, pltpu.roll(first, HD, 1), second_head)
    block_out[...] = x_ref[...].astype(F32) + summed[...].astype(F32) + out_share[...].astype(F32)
    input_grads[...] = cot[...].astype(F32) + d_sum[...].astype(F32) + in_share[...].astype(F32)

    @pl.when(i == 0)
    def _():
        gain[...] = small[pl.ds(0, 1)]
        second[...] = small[pl.ds(1, 1)]
        kernel_m[...] = small[pl.ds(4, KC), pl.ds(0, MW)]
        for k in range(KC):
            kernel_s[pl.ds(k, 1)] = small[pl.ds(2, 1), pl.ds(256 * k, 256)]
        bias_m[...] = small[4, pl.ds(MW, MW)]
        bias_s[...] = small[pl.ds(3, 1), pl.ds(0, 256)]
        skip[...] = exact(small[pl.ds(6, 1), pl.ds(MW, MW)], head_spread(), ((1,), (1,)))
        mgain[...] = small[5, pl.ds(MW, MW)]


def widened(h, x_out, xb_out, zq_out, mix_out, st_out, kv_out, x_ref, summed, out_share, cot, d_sum, in_share, small):
    def rows(count, width, offset=0):
        return pl.BlockSpec((count, width), lambda i, h: (i + offset, 0))

    def halves(count, width):
        return pl.BlockSpec((2, count, width), lambda i, h: (0, i, 0))

    def whole(count, width):
        return pl.BlockSpec((count, width), lambda i, h: (0, 0))

    def line(width):
        return pl.BlockSpec((width,), lambda i, h: (0,))

    own = pl.BlockSpec((64, 256), lambda i, h: (i, h[0]))
    grid = pltpu.PrefetchScalarGridSpec(
        num_scalar_prefetch=1,
        grid=(4,),
        in_specs=[rows(128, 256, 12 * cb) for cb in range(4)]
        + [rows(256, 256, 6 * cb + 2) for cb in range(4)]
        + [rows(128, 256, 4 * cb) for cb in range(4)]
        + [rows(256, 128, 4 * k) for k in range(4)]
        + [rows(256, MW), rows(256, 256), rows(256, 256)]
        + [own, own, rows(64, 256), own, own, rows(64, 256), whole(8, D)],
        out_specs=(
            rows(128, D), halves(256, 512),
            pl.BlockSpec((128, D), lambda i, h: (jnp.minimum(i, 2), 0)), whole(128, D),
            halves(256, MW), rows(256, 128), halves(256, 128), rows(256, 256),
            rows(64, 256), rows(64, 256),
            whole(1, D), whole(1, D), whole(KC, MW), whole(KC, 256), line(MW), whole(1, 256),
            whole(1, HMH), line(MW),
        ),
    )
    return pl.pallas_call(
        widths_kernel,
        grid_spec=grid,
        out_shape=(
            shape((512, D), F32), shape((2, D, 512), F32), shape((MW, D), F32), shape((128, D), F32),
            shape((2, D, MW), F32), shape((D, 128), F32), shape((2, D, 128), F32), shape((D, 256), F32),
            shape((ROWS, 256), F32), shape((ROWS, 256), F32),
            shape((1, D), F32), shape((1, D), F32), shape((KC, MW), F32), shape((KC, 256), F32),
            shape((MW,), F32), shape((1, 256), F32), shape((1, HMH), F32), shape((MW,), F32),
        ),
        compiler_params=pltpu.CompilerParams(vmem_limit_bytes=VMEM_LIMIT),
    )(
        h, *[x_out] * 8, *[xb_out] * 4, *[zq_out] * 4, mix_out, st_out, kv_out, x_ref, summed, out_share, cot,
        d_sum, in_share, small,
    )


SCAN_SCRATCH = (
    pltpu.VMEM((MW, NS), BF16), pltpu.VMEM((MW, NS), BF16), pltpu.VMEM((4, MW // 2, NS), BF16),
    pltpu.VMEM((4, MW // 2, NS), BF16), pltpu.VMEM((MW, NS), BF16),
)


def on_device(
    hidden_in, cotangent, log_decay, norm_gain, query_weight, keyvalue_weight, attention_output,
    mixer_weight, state_weight, kernel_mixer, kernel_state, bias_mixer, bias_state, skip_gain,
    mixer_gain, mixer_output, second_gain, gate_up, down_weight,
):
    gain1 = norm_gain.reshape(1, D)
    gain2 = second_gain.reshape(1, D)
    mgain = mixer_gain
    skip = skip_gain.reshape(1, HMH)
    bias_m, bias_s = bias_mixer, bias_state.reshape(1, 256)
    (
        cum, cum_t, normed, q, kv_all, logs_all, gz, ext, pre, post, attended, attended_f, totals, ssd, mixed,
        squares, state, gated, summed,
    ) = call(
        forward_kernel,
        [
            shape((ROWS, HMH), F32), shape((HMH, ROWS), F32),
            shape((ROWS, D), BF16), shape((ROWS, 128), BF16), shape((8192, 128), BF16),
            shape((256, 128), F32), shape((ROWS, MW), F32), shape((ROWS + 16, CW), F32),
            shape((ROWS, CW), F32), shape((ROWS, CW), BF16), shape((ROWS, 128), BF16),
            shape((ROWS, 128), F32), shape((8, 512), F32), shape((ROWS, MW), F32),
            shape((ROWS, MW), F32), shape((8, ROWS), F32), shape((MW, NS), BF16),
            shape((ROWS, MW), BF16), shape((ROWS, D), BF16),
        ],
        (
            hidden_in, gain1, query_weight, keyvalue_weight, mixer_weight, state_weight, kernel_mixer,
            kernel_state, bias_m, bias_s, log_decay, skip, mgain, mixer_output, attention_output,
        ),
        scratch=[
            pltpu.VMEM((ROWS, 128), BF16), pltpu.VMEM((8, 128), F32),
            pltpu.VMEM((16, D), BF16), pltpu.VMEM((16, D), BF16),
            *SCAN_SCRATCH,
            pltpu.VMEM((512, 128), BF16), pltpu.VMEM((128, 512), F32), pltpu.VMEM((8, ROWS), F32),
            pltpu.VMEM((HEADS, 8, ROWS), F32), pltpu.VMEM((ROWS, D), F32),
            pltpu.VMEM((ROWS, D), BF16), pltpu.VMEM((ROWS, D), BF16), pltpu.VMEM((ROWS, D), BF16),
        ],
        collective=1, copies=80,
    )
    (
        d_sum, out_share, x_piece, xb_piece, second_part, mixgain, d_z, d_ssd, skip_part, d_scaled, d_bc, leaving,
        d_q, pairs,
    ) = call(
        middle_kernel,
        [
            shape((ROWS, D), BF16), shape((ROWS, 256), BF16), shape((192, 256), BF16),
            shape((64, 256), BF16),
            shape((8, D), F32), shape((8, MW), F32), shape((ROWS, MW), BF16), shape((ROWS, MW), F32),
            shape((8, MW), F32), shape((ROWS, MW), F32), shape((ROWS, 256), F32),
            shape((MW, NS), BF16), shape((ROWS, 128), BF16), shape((8192, 128), BF16),
        ],
        (
            hidden_in, summed, cotangent, gain2, gate_up, down_weight, gated, attended, mixer_output,
            attention_output, mixed, squares, mgain, gz, ssd, post, log_decay, cum, cum_t, state, q, kv_all,
            attended_f, totals, logs_all,
        ),
        scratch=[
            pltpu.VMEM((ROWS, D), BF16), pltpu.VMEM((ROWS, D), F32), pltpu.VMEM((ROWS, D), F32),
            pltpu.VMEM((ROWS, D), BF16), pltpu.VMEM((1024, 256), BF16), pltpu.VMEM((6144, 256), BF16),
            pltpu.VMEM((2048, 256), BF16), pltpu.VMEM((ROWS, D), BF16), pltpu.VMEM((ROWS, D), BF16),
            pltpu.VMEM((1024, 256), BF16), pltpu.VMEM((1024, 256), BF16),
            pltpu.VMEM((6144, 256), BF16), pltpu.VMEM((6144, 256), BF16),
            pltpu.VMEM((2048, 256), BF16), pltpu.VMEM((2048, 256), BF16),
            pltpu.VMEM((ROWS, 128), BF16), pltpu.VMEM((ROWS, MW), F32), pltpu.VMEM((8, ROWS), F32),
            pltpu.VMEM((HEADS, 8, ROWS), F32), pltpu.VMEM((MW, NS), BF16),
            *SCAN_SCRATCH[1:], pltpu.VMEM((512, 128), BF16),
            pltpu.VMEM((512, 128), BF16), pltpu.VMEM((128, 512), F32),
        ],
        collective=2, copies=150,
    )
    x_out, xb_out, zq_out, mix_out, st_out, kv_out, in_share, small = call(
        last_kernel,
        [
            shape((6144, 256), BF16), shape((2048, 256), BF16), shape((4096, 128), BF16),
            shape((D, MW), BF16), shape((D, 256), BF16), shape((D, 256), BF16),
            shape((ROWS, 256), BF16), shape((8, D), F32),
        ],
        (
            pairs, leaving, d_ssd, d_scaled, d_bc, skip, log_decay, cum, post, pre, ext, kernel_mixer,
            kernel_state, d_z, d_q, normed, hidden_in, gain1, mixer_weight, state_weight, query_weight,
            keyvalue_weight, second_part, mixgain, skip_part, x_piece, xb_piece,
        ),
        scratch=[
            pltpu.VMEM((8192, 128), BF16), pltpu.VMEM((8192, 128), BF16), pltpu.VMEM((ROWS, CW), F32),
            pltpu.VMEM((8, CW), F32), pltpu.VMEM((ROWS + 8, CW), F32), pltpu.VMEM((ROWS, 1280), BF16),
            pltpu.VMEM((ROWS, D), F32), pltpu.VMEM((8, CW), F32),
            *[pltpu.VMEM((4096, 128), BF16)] * 3, *[pltpu.VMEM((D, MW), BF16)] * 3,
            *[pltpu.VMEM((D, 256), BF16)] * 3, *[pltpu.VMEM((D, 128), BF16)] * 3,
            *[pltpu.VMEM((D, 256), BF16)] * 3,
            pltpu.VMEM((HEADS, 32, 256), BF16), pltpu.VMEM((HEADS, 32, 128), BF16),
            pltpu.VMEM((5, 8, D), F32), pltpu.VMEM((16, 8, D), F32),
        ],
        collective=3, copies=230,
    )
    h = lax.axis_index("head").astype(jnp.int32).reshape(1)
    (
        down, gateup, mixout, attn, mixer, query, keyval, state_grads, block_out, input_grads,
        gain_grads, second_grads, mixkernel, statekernel, mixbias, statebias, skip_grads, mixgain_grads,
    ) = widened(
        h, x_out, xb_out, zq_out, mix_out, st_out, kv_out, hidden_in, summed, out_share, cotangent,
        d_sum, in_share, small,
    )
    return (
        block_out,
        input_grads,
        gain_grads.reshape(D),
        query,
        keyval,
        attn,
        mixer,
        state_grads,
        mixkernel,
        statekernel,
        mixbias,
        statebias.reshape(256),
        skip_grads.reshape(HMH),
        mixgain_grads,
        mixout,
        second_grads.reshape(D),
        gateup,
        down,
    )


def solution(mesh):
    return jax.shard_map(
        on_device,
        mesh=mesh,
        in_specs=(
            P("seq", None), P("seq", None), P("seq", "head"), P(), P(None, "head"), P(),
            P("head", None), P(None, None, "head"), P(), P(None, "head"), P(), P("head"), P(),
            P("head"), P("head"), P("head", None), P(), P(None, None, "head"), P("head", None),
        ),
        out_specs=(
            P("seq", "head"), P("seq", "head"), P(), P(None, "head"), P(), P("head", None),
            P(None, None, "head"), P(), P(None, "head"), P(), P("head"), P(), P("head"), P("head"),
            P("head", None), P(), P(None, None, "head"), P("head", None),
        ),
        check_vma=False,
    )
```

```python
import functools

import jax
import jax.numpy as jnp
from jax import lax
from jax.experimental import pallas as pl
from jax.experimental.pallas import tpu as pltpu
from jax.sharding import PartitionSpec as P

D = 1024
FF = 2048
AH = 8
KVH = 2
HD = 64
MAMBA_HEADS = 24
MP = 64
NS = 128
KC = 4
EPSILON = 1e-05
SEQ = 32
HEADS = 4
ROWS = 256
MW = 384
CW = 640
HMH = 6
HIGHEST = lax.Precision.HIGHEST
MESH = pl.DeviceIdType.MESH
F32 = jnp.float32
BF16 = jnp.bfloat16
VMEM_LIMIT = 50 * 1024 * 1024


def nn(a, b):
    return jnp.dot(a, b, preferred_element_type=F32)


def nt(a, b):
    return lax.dot_general(a, b, (((1,), (1,)), ((), ())), preferred_element_type=F32)


def tn(a, b):
    return lax.dot_general(a, b, (((0,), (0,)), ((), ())), preferred_element_type=F32)


def exact(a, b, dims):
    return lax.dot_general(
        a, b, (dims, ((), ())), precision=HIGHEST, preferred_element_type=F32
    )


def sigmoid(v):
    return 1.0 / (1.0 + jnp.exp(-v))


def shape(dims, kind):
    return jax.ShapeDtypeStruct(dims, kind)


def seq_bits(s):
    core, y, z = s % 2, (s // 2) % 4, s // 8
    return {
        "c": core,
        "ya": (y + y // 2) % 2,
        "yb": y // 2,
        "za": (z + z // 2) % 2,
        "zb": z // 2,
        "y4": y,
        "z4": z,
    }


SEQ_PATHS = (
    ("c", "ya", "yb", "z4"),
    ("c", "yb", "ya", "z4"),
    ("c", "za", "zb", "y4"),
    ("c", "zb", "za", "y4"),
)
LOG_PATH = ("c", "y4", "z4")
SHORT_PATHS = (("c", "y4", "z4"), ("c", "z4", "y4"))
HEAD_PATHS = (("xa", "xb"), ("xb", "xa"))


def ways(name):
    return 4 if name in ("y4", "z4") else 2


def position(bits, path):
    at = 0
    for name in path:
        at = at * ways(name) + bits[name]
    return at


def sizes(rows, path):
    left = []
    for name in path:
        rows = rows // ways(name)
        left.append(rows)
    return left


def block_position(s, p):
    return position(seq_bits(s), SEQ_PATHS[p])


def head_position(h, p):
    bits = {"xa": (h + h // 2) % 2, "xb": h // 2}
    return position(bits, HEAD_PATHS[p])


class Links:
    def __init__(self, send_sem, recv_sem):
        s, h = lax.axis_index("seq"), lax.axis_index("head")
        self.s, self.h = s, h
        core, y, z = s % 2, (s // 2) % 4, s // 8
        self.bits = seq_bits(s)
        self.bits["xa"] = (h + h // 2) % 2
        self.bits["xb"] = h // 2
        self.partner = {
            "c": (s + 1 - 2 * core, h),
            "ya": (s + 2 * (1 - 2 * (y % 2)), h),
            "yb": (s + 2 * (3 - 2 * y), h),
            "za": (s + 8 * (1 - 2 * (z % 2)), h),
            "zb": (s + 8 * (3 - 2 * z), h),
            "xa": (s, h + 1 - 2 * (h % 2)),
            "xb": (s, 3 - h),
            "y41": (s - 2 * y + 2 * ((y + 1) % 4), h),
            "y42": (s - 2 * y + 2 * ((y + 2) % 4), h),
            "y43": (s - 2 * y + 2 * ((y + 3) % 4), h),
            "z41": ((s + 8) % SEQ, h),
            "z42": ((s + 16) % SEQ, h),
            "z43": ((s + 24) % SEQ, h),
            "x1": (s, (h + 1) % HEADS),
            "x2": (s, (h + 2) % HEADS),
            "x3": (s, (h + 3) % HEADS),
            "next": ((s + 1) % SEQ, h),
            "prev": ((s + SEQ - 1) % SEQ, h),
        }
        self.send_sem, self.recv_sem, self.used = send_sem, recv_sem, 0

    def greet(self, names):
        semaphore = pltpu.get_barrier_semaphore()
        for name in names:
            pl.semaphore_signal(
                semaphore, inc=1, device_id=self.partner[name], device_id_type=MESH
            )

    def met(self, names):
        pl.semaphore_wait(pltpu.get_barrier_semaphore(), len(names))

    def barrier(self, names):
        self.greet(names)
        self.met(names)

    def send(self, src, dst, name):
        k = self.used
        self.used += 1
        assert k < self.send_sem.shape[0]
        copy = pltpu.make_async_remote_copy(
            src_ref=src,
            dst_ref=dst,
            send_sem=self.send_sem.at[k],
            recv_sem=self.recv_sem.at[k],
            device_id=self.partner[name],
            device_id_type=MESH,
        )
        copy.start()
        return copy


DONE = object()
SEQ_NAMES = ("c", "y41", "y42", "y43", "z41", "z42", "z43")


def rows_at(start, count, unit=16):
    return pl.ds(pl.multiple_of(start, unit), count)


class Reduce:
    def __init__(self, links, path, rows, src, src_base, work, recv, out, base):
        self.links, self.path, self.rows = links, path, rows
        self.src, self.src_base = src, src_base
        self.work, self.recv, self.out, self.base = work, recv, out, base
        self.left = sizes(rows, path)
        self.start = 0
        self.copies = []

    def source(self, step):
        return (self.src, self.src_base) if step == 0 else (self.work, self.base)

    def landing(self, step):
        return self.base + self.rows - (self.rows if step == 0 else self.left[step - 1])

    def begin(self, step):
        name, size = self.path[step], self.left[step]
        ref, at = self.source(step)
        landing = self.landing(step)
        self.copies = []
        for k in range(1, ways(name)):
            away = (self.links.bits[name] + k) % ways(name)
            to = name if ways(name) == 2 else name + str(k)
            self.copies.append(
                self.links.send(
                    ref.at[rows_at(at + self.start + away * size, size)],
                    self.recv.at[pl.ds(landing + (k - 1) * size, size)],
                    to,
                )
            )

    def finish(self, step):
        name, size = self.path[step], self.left[step]
        keep = self.start + self.links.bits[name] * size
        ref, at = self.source(step)
        landing = self.landing(step)
        last = step == len(self.path) - 1
        target = self.out if last and self.out is not None else self.work
        for copy in self.copies:
            copy.wait()
        chunk = 32 if size % 32 == 0 else 16

        def add(i, carry):
            total = ref[rows_at(at + keep + i * chunk, chunk)].astype(F32)
            for k in range(ways(name) - 1):
                total += self.recv[rows_at(landing + k * size + i * chunk, chunk)].astype(F32)
            target[rows_at(self.base + keep + i * chunk, chunk)] = total.astype(BF16)
            return carry

        lax.fori_loop(0, size // chunk, add, 0)
        self.start = keep

    def send_back(self, step, columns=None):
        name, size = self.path[step], self.left[step]
        at = rows_at(self.base + self.start, size, min(size, 16))
        ref = self.out.at[at] if columns is None else self.out.at[at, pl.ds(0, columns)]
        self.copies = [
            self.links.send(ref, ref, name if ways(name) == 2 else name + str(k))
            for k in range(1, ways(name))
        ]

    def wait_back(self, step):
        name, size = self.path[step], self.left[step]
        for copy in self.copies:
            copy.wait()
        self.start = self.start - self.links.bits[name] * size


def reduce_steps(jobs):
    for job in jobs:
        job.begin(0)
    for step in range(max(len(job.path) for job in jobs)):
        yield
        for job in jobs:
            if step < len(job.path):
                job.finish(step)
                if step + 1 < len(job.path):
                    job.begin(step + 1)


def gather_steps(jobs, columns=None):
    columns = columns or [None] * len(jobs)
    for job, width in zip(jobs, columns):
        job.send_back(len(job.path) - 1, width)
    for step in range(max(len(job.path) for job in jobs) - 1, -1, -1):
        yield
        for job, width in zip(jobs, columns):
            if step < len(job.path):
                job.wait_back(step)
                if step:
                    job.send_back(step - 1, width)


def finish(*runs):
    runs = list(runs)
    while runs:
        for run in list(runs):
            if next(run, DONE) is DONE:
                runs.remove(run)


def advance(*runs):
    for run in runs:
        next(run, DONE)


def reduce_all(jobs):
    finish(reduce_steps(jobs))


def gather_all(jobs, columns=None):
    finish(gather_steps(jobs, columns))


def call(body, outs, args, scratch=(), collective=None, smem=0, copies=0, limit=VMEM_LIMIT):
    vm = pl.BlockSpec(memory_space=pltpu.VMEM)
    scratch = list(scratch)
    if copies:
        scratch += [pltpu.SemaphoreType.DMA((copies,)), pltpu.SemaphoreType.DMA((copies,))]
    if collective is None:
        params = pltpu.CompilerParams(vmem_limit_bytes=VMEM_LIMIT)
    else:
        params = pltpu.CompilerParams(
            vmem_limit_bytes=limit, collective_id=collective, has_side_effects=True
        )
    in_specs = [pl.BlockSpec(memory_space=pltpu.SMEM)] * smem + [vm] * (len(args) - smem)
    return pl.pallas_call(
        body,
        out_shape=tuple(outs),
        in_specs=in_specs,
        out_specs=tuple(vm for _ in outs),
        scratch_shapes=scratch,
        compiler_params=params,
    )(*args)


class Gather:
    def __init__(self, links, path, piece, out, base):
        self.links, self.path, self.out, self.base = links, path, out, base
        self.start = position(links.bits, path) * piece
        self.left = sizes(piece * SEQ, path)
        self.copies = []

    send_back = Reduce.send_back
    wait_back = Reduce.wait_back


def gather_rows(links, src, out, paths=SEQ_PATHS):
    piece = src.shape[0] // len(paths)
    jobs = []
    for p, path in enumerate(paths):
        job = Gather(links, path, piece, out, p * piece * SEQ)
        own = rows_at(job.base + job.start, piece, 8 if piece == 8 else 16)
        out[own] = src[pl.ds(p * piece, piece)]
        jobs.append(job)
    return jobs


def own_rows(job, count):
    return job.work[rows_at(job.base + job.start, count)]


def head_spread():
    lane = lax.broadcasted_iota(jnp.int32, (HMH, MW), 1)
    row = lax.broadcasted_iota(jnp.int32, (HMH, MW), 0)
    return jnp.where((lane >= row * MP) & (lane < row * MP + MP), 1.0, 0.0)


def widen(values):
    return exact(values, head_spread(), ((1,), (0,)))


def decay_terms(decay_ref, cum_ref):
    cum_x = widen(cum_ref[...])
    step_x = -widen(decay_ref[...])
    enter_x = jnp.exp(cum_x)
    tail_x = jnp.exp(cum_x[ROWS - 1 : ROWS, :] - cum_x)
    return step_x, enter_x, tail_x


def of_channels(mixer, state, c):
    return (mixer, pl.ds(128 * c, 128)) if c < 3 else (state, pl.ds(128 * (c - 3), 128))


def conv_forward(ext, taps_m, taps_s, bias_m, bias_s, pre, post):
    for c in range(5):
        lanes = pl.ds(128 * c, 128)
        taps, own = of_channels(taps_m, taps_s, c)
        bias, own = of_channels(bias_m, bias_s, c)
        offset = bias[own].reshape(1, 128) if c < 3 else bias[:, own]
        total = offset + taps[pl.ds(0, 1), own] * ext[pl.ds(13, ROWS), lanes]
        for k in range(1, KC):
            total = total + taps[pl.ds(k, 1), own] * ext[pl.ds(13 + k, ROWS), lanes]
        pre[:, lanes] = total
        post[:, lanes] = (total * sigmoid(total)).astype(BF16)


def scan_steps(links, local, logs, sibling, row_slots, plane_slots, halves, result, forward):
    s, core, y, z = links.s, links.bits["c"], links.bits["y4"], links.bits["z4"]
    turn = range(4) if forward else range(3, -1, -1)
    copy = links.send(local, sibling, "c")
    yield

    def log_of(j):
        return logs[rows_at(position(seq_bits(j), LOG_PATH) * 8, 8, 8)]

    def of_half(tile, k):
        return jnp.where(core == 0, tile[k : k + 1], tile[HMH // 2 + k : HMH // 2 + k + 1])

    first = core == (0 if forward else 1)
    other = s + 1 - 2 * core
    own_weight = jnp.where(first, jnp.exp(log_of(other)), 1.0)
    other_weight = jnp.where(first, 1.0, jnp.exp(log_of(s)))
    row_logs = [log_of(8 * z + 2 * k) + log_of(8 * z + 2 * k + 1) for k in range(4)]
    plane_logs = []
    for k in range(4):
        total = log_of(8 * k)
        for j in range(1, 8):
            total = total + log_of(8 * k + j)
        plane_logs.append(total)

    def exclusive(slots, tiles, at, k):
        rows = pl.ds(64 * k, 64)
        total = jnp.zeros((64, NS), F32)
        before = total
        for j in turn:
            before = jnp.where(at == j, total, before)
            total = of_half(jnp.exp(tiles[j]), k) * total + slots[j, rows].astype(F32)
        return before, total

    copy.wait()
    for k in range(3):
        rows = rows_at(192 * core + 64 * k, 64)
        total = of_half(own_weight, k) * local[rows].astype(F32)
        total = total + of_half(other_weight, k) * sibling[rows].astype(F32)
        row_slots[y, pl.ds(64 * k, 64)] = total.astype(BF16)
    slot = row_slots.at[y]
    copies = [links.send(slot, slot, name) for name in ("y41", "y42", "y43")]
    yield
    for copy in copies:
        copy.wait()
    within = []
    for k in range(3):
        before, total = exclusive(row_slots, row_logs, y, k)
        within.append(before)
        plane_slots[z, pl.ds(64 * k, 64)] = total.astype(BF16)
    slot = plane_slots.at[z]
    copies = [links.send(slot, slot, name) for name in ("z41", "z42", "z43")]
    ahead = jnp.zeros((8, 128), F32)
    passed = ahead
    for j in turn:
        passed = jnp.where(y == j, ahead, passed)
        ahead = ahead + row_logs[j]
    yield
    for copy in copies:
        copy.wait()
    for k in range(3):
        before, _ = exclusive(plane_slots, plane_logs, z, k)
        total = of_half(jnp.exp(passed), k) * before + within[k]
        halves[rows_at(192 * core + 64 * k, 64)] = total.astype(BF16)
    mine = halves.at[rows_at(192 * core, 192)]
    copy = links.send(mine, mine, "c")
    yield
    copy.wait()
    fade = jnp.exp(log_of(other))
    for k in range(HMH):
        rows = pl.ds(64 * k, 64)
        chip = halves[rows].astype(F32)
        later = fade[k : k + 1] * chip + sibling[rows].astype(F32)
        result[rows] = jnp.where(first, chip, later).astype(BF16)


def lower_mask():
    t = lax.broadcasted_iota(jnp.int32, (ROWS, ROWS), 0)
    u = lax.broadcasted_iota(jnp.int32, (ROWS, ROWS), 1)
    return u <= t


def decay_of(cum, cum_t, h, mask):
    diff = cum[:, h : h + 1] - cum_t[h : h + 1, :]
    return jnp.exp(jnp.where(mask, diff, -1e30))


def row_sums(values):
    return exact(jnp.ones((8, values.shape[1]), F32), values, ((1,), (1,)))


def column_of(rows):
    return exact(rows, jnp.full((8, 128), 0.125, F32), ((0,), (0,)))[:, 0:1]


def ssd_forward(post, step_x, enter_x, cum_ref, cumt_ref, skip, gz, state, ssd, mixed, squares):
    mixer_in = post[:, pl.ds(0, MW)].astype(F32)
    scaled = (mixer_in * step_x).astype(BF16)
    b, c = post[:, pl.ds(MW, NS)], post[:, pl.ds(MW + NS, NS)]
    gram = nt(c, b)
    mask = lower_mask()
    cum, cum_t = cum_ref[...], cumt_ref[...]
    left = lax.broadcasted_iota(jnp.int32, (ROWS, 128), 1) < MP
    carried = enter_x * nt(c, state[...]) + widen(skip[...]) * mixer_in
    for pair in range(3):
        lanes = slice(128 * pair, 128 * pair + 128)
        first = nn((gram * decay_of(cum, cum_t, 2 * pair, mask)).astype(BF16), scaled[:, lanes])
        second = nn((gram * decay_of(cum, cum_t, 2 * pair + 1, mask)).astype(BF16), scaled[:, lanes])
        ssd[:, pl.ds(128 * pair, 128)] = jnp.where(left, first, second) + carried[:, lanes]
    z = gz[...]
    m = ssd[...] * (z * sigmoid(z))
    mixed[...] = m
    squares[...] = row_sums(m * m)


def load_block(kv_all, j):
    return jnp.concatenate(
        [kv_all[rows_at(2048 * p + block_position(j, p) * 64, 64)] for p in range(4)], axis=0
    )


def causal(block):
    key = lax.broadcasted_iota(jnp.int32, block.shape, 0)
    query = lax.broadcasted_iota(jnp.int32, block.shape, 1)
    query = jnp.where(query >= ROWS, query - ROWS, query)
    return jnp.where(key <= query, block, -1e30)


def stacked_queries(q):
    q = q.astype(F32) * (HD ** -0.5)
    left = lax.broadcasted_iota(jnp.int32, (ROWS, 128), 1) < HD
    first = jnp.where(left, q, 0.0)
    second = jnp.where(left, pltpu.roll(q, HD, 1), 0.0)
    return jnp.concatenate([first, second], axis=0).astype(BF16)


FORWARD_NAMES = SEQ_NAMES + ("next", "prev", "x1", "x2", "x3")


def forward_kernel(
    x_ref, gain, wq, kvw, wm, ws, taps_m, taps_s, bias_m, bias_s, decay, skip, mgain, wmo, wao,
    cum_ref, cumt_ref, normed, q, kv_all, logs_all, gz, ext, pre, post, attended, attended_f, totals, ssd, mixed,
    squares, state, gated, summed,
    kv, logs, x_edge, edge_normed, local, sibling, row_slots, plane_slots, halves, qp, acc, own_squares, slots, proj, part, work,
    recv, send_sem, recv_sem,
):
    links = Links(send_sem, recv_sem)
    s = links.s
    links.greet(FORWARD_NAMES)

    def normalise(rows):
        x = rows.astype(F32)
        r1 = lax.rsqrt(jnp.mean(x * x, axis=1, keepdims=True) + EPSILON)
        return (x * r1 * gain[...]).astype(BF16)

    n = normalise(x_ref[...])
    normed[...] = n
    left = lax.broadcasted_iota(jnp.int32, (ROWS, 128), 1) < HD
    key_cols, value_cols = nn(n, kvw[0]), nn(n, kvw[1])
    key_cols = jnp.where(links.h < 2, key_cols, pltpu.roll(key_cols, HD, 1))
    value_cols = jnp.where(links.h < 2, pltpu.roll(value_cols, HD, 1), value_cols)
    kv[...] = jnp.where(left, key_cols, value_cols).astype(BF16)
    q[...] = nn(n, wq[...]).astype(BF16)
    sums = exact(decay[...], jnp.ones((ROWS, 128), F32), ((0,), (0,)))
    logs[...] = jnp.concatenate([sums, jnp.zeros((8 - HMH, 128), F32)], axis=0)
    key_jobs = gather_rows(links, kv, kv_all)
    log_jobs = gather_rows(links, logs, logs_all, (LOG_PATH,))
    links.met(FORWARD_NAMES)
    edge_copy = links.send(x_ref.at[pl.ds(ROWS - 16, 16)], x_edge, "next")
    keys, every_log = gather_steps(key_jobs), gather_steps(log_jobs)
    advance(keys, every_log)
    gz[...] = nn(normed[...], wm[0])
    lower = jnp.where(lower_mask(), 1.0, 0.0)
    cum_ref[...] = exact(lower, decay[...], ((1,), (0,)))
    cumt_ref[...] = exact(decay[...], lower, ((0,), (1,)))
    advance(keys, every_log)
    ext[pl.ds(16, ROWS), pl.ds(0, MW)] = nn(normed[...], wm[1])
    ext[pl.ds(16, ROWS), pl.ds(MW, 256)] = nn(normed[...], ws[...])
    edge_copy.wait()
    advance(keys, every_log)
    keep = jnp.where(s > 0, 1.0, 0.0)
    edge_normed[...] = normalise(x_edge[...])
    ext[pl.ds(0, 16), pl.ds(0, MW)] = nn(edge_normed[...], wm[1]) * keep
    ext[pl.ds(0, 16), pl.ds(MW, 256)] = nn(edge_normed[...], ws[...]) * keep
    conv_forward(ext, taps_m, taps_s, bias_m, bias_s, pre, post)
    advance(keys)
    finish(every_log)
    step_x, enter_x, tail_x = decay_terms(decay, cum_ref)
    tail_in = (post[:, pl.ds(0, MW)].astype(F32) * step_x * tail_x).astype(BF16)
    local[...] = tn(tail_in, post[:, pl.ds(MW, NS)]).astype(BF16)
    entering = scan_steps(
        links, local, logs_all, sibling, row_slots, plane_slots, halves, state, True
    )
    advance(entering)

    qp[...] = stacked_queries(q[...])
    scores = causal(nt(kv[...], qp[...]))
    high = jnp.max(scores, axis=0, keepdims=True)
    weights = jnp.exp(scores - high)
    acc[...] = tn(kv[...], weights.astype(BF16))
    advance(entering)
    finish(keys)

    def merge(blocks, running):
        high, total = running
        scores = [nt(block, qp[...]) for block in blocks]
        new = high
        for block in scores:
            new = jnp.maximum(new, jnp.max(block, axis=0, keepdims=True))
        fade = jnp.exp(high - new)
        weights = [jnp.exp(block - new) for block in scores]
        total = total * fade
        gained = acc[...] * fade
        for block, weight in zip(blocks, weights):
            total = total + jnp.sum(weight, axis=0, keepdims=True)
            gained = gained + tn(block, weight.astype(BF16))
        acc[...] = gained
        return new, total

    def hop(i, running):
        return merge([load_block(kv_all, 2 * i), load_block(kv_all, 2 * i + 1)], running)

    def last_hop(i, running):
        return merge([load_block(kv_all, s - 1)], running)

    running = (high, jnp.sum(weights, axis=0, keepdims=True))
    hops = s // 2
    for turn in range(4):
        if turn == 3:
            finish(entering)
            ssd_forward(
                post, step_x, enter_x, cum_ref, cumt_ref, skip, gz, state, ssd, mixed, own_squares
            )
            slots[links.h] = own_squares[...]
            square_copies = [
                links.send(own_squares, slots.at[links.h], name) for name in ("x1", "x2", "x3")
            ]
        running = lax.fori_loop((hops * turn) // 4, (hops * (turn + 1)) // 4, hop, running)
        advance(entering)
    running = lax.fori_loop(0, s % 2, last_hop, running)
    high, total = running
    out = acc[pl.ds(HD, HD)] / total
    out = jnp.concatenate([out[:, :ROWS], out[:, ROWS:]], axis=0).T
    attended_f[...] = out
    attended[...] = out.astype(BF16)
    totals[...] = jnp.broadcast_to(high + jnp.log(total), totals.shape)
    for c in range(2):
        lanes = pl.ds(512 * c, 512)
        proj[:, lanes] = nn(attended[...], wao[:, lanes])
    for copy in square_copies:
        copy.wait()
    squares[...] = (slots[0] + slots[1]) + (slots[2] + slots[3])
    scale = lax.rsqrt(column_of(squares[...]) / (MAMBA_HEADS * MP) + EPSILON)
    gated[...] = (mixed[...] * scale * mgain[...].reshape(1, MW)).astype(BF16)
    for c in range(2):
        lanes = pl.ds(512 * c, 512)
        part[:, lanes] = (proj[:, lanes] + nn(gated[...], wmo[:, lanes])).astype(BF16)
    jobs = [
        Reduce(links, path, 64, part, 64 * p, work, recv, summed, 64 * p)
        for p, path in enumerate(HEAD_PATHS * 2)
    ]
    reduce_all(jobs)
    gather_all(jobs)


def put_wide(wide, values):
    for j in range(HEADS):
        for p in range(2):
            at = 512 * p + int(head_position(j, p)) * 128
            wide[pl.ds(at, 128)] = values[128 * p : 128 * p + 128, 256 * j : 256 * j + 256].astype(BF16)


MIDDLE_NAMES = SEQ_NAMES + ("x1", "x2", "x3")


def middle_kernel(
    x_ref, summed, cot_ref, gain, gu, dw, gated, attended, wmo, wao, mixed, squares, mgain, gz, ssd,
    post, decay, cum_ref, cumt_ref, state, q, kv_all, attended_f, totals, logs_all,
    d_sum, share, x_piece, xb_piece, second_part, mixgain, d_z, d_ssd, skip_part, d_scaled, d_bc, leaving, d_q, pairs,
    sn, out_acc, d_acc, back, wide, xf, xb, work, recv, wide_work, wide_recv, x_work, x_recv,
    xb_work, xb_recv,
    d_att, d_gated, own_inner, slots, local, sibling, row_slots, plane_slots, halves, qp, dop, acc, send_sem, recv_sem,
):
    links = Links(send_sem, recv_sem)
    s = links.s
    links.greet(MIDDLE_NAMES)

    residual = x_ref[...].astype(F32) + summed[...].astype(F32)
    r2 = lax.rsqrt(jnp.mean(residual * residual, axis=1, keepdims=True) + EPSILON)
    sn[...] = (residual * r2 * gain[...]).astype(BF16)
    out_acc[...] = jnp.zeros_like(out_acc)
    d_acc[...] = jnp.zeros_like(d_acc)

    def part(c, carry):
        cols = pl.ds(pl.multiple_of(c * 256, 256), 256)
        wg, wu, wd = gu[0, :, cols], gu[1, :, cols], dw[cols]
        gate, up = nn(sn[...], wg), nn(sn[...], wu)
        sig = sigmoid(gate)
        act_gate = gate * sig
        act = (act_gate * up).astype(BF16)
        out_acc[...] += nn(act, wd)
        for cb in range(4):
            at = rows_at(1536 * cb + c * 256, 256)
            xf[at] = tn(act, cot_ref[:, pl.ds(256 * cb, 256)]).astype(BF16)
        d_act = nt(cot_ref[...], wd)
        d_gate = (d_act * up * (sig * (1.0 + gate * (1.0 - sig)))).astype(BF16)
        d_up = (d_act * act_gate).astype(BF16)
        xf[rows_at(1536 * c + 512, 1024)] = tn(sn[...], d_gate).astype(BF16)
        xf[rows_at(1536 * c + 3584, 1024)] = tn(sn[...], d_up).astype(BF16)
        d_acc[...] += nt(d_gate, wg) + nt(d_up, wu)
        return carry

    lax.fori_loop(0, 2, part, 0)
    d_second = d_acc[...]
    residual = x_ref[...].astype(F32) + summed[...].astype(F32)
    second_part[...] = jnp.broadcast_to(
        jnp.sum(d_second * residual * r2, axis=0, keepdims=True), second_part.shape
    )
    weighted = d_second * gain[...]
    inner = jnp.sum(weighted * residual, axis=1, keepdims=True)
    back[...] = (r2 * weighted - residual * (r2 * r2 * r2 / D * inner)).astype(BF16)
    links.met(MIDDLE_NAMES)

    sums = [
        Reduce(links, path, 64, back, 64 * p, work, recv, d_sum, 64 * p)
        for p, path in enumerate(HEAD_PATHS * 2)
    ]
    x_jobs = [
        Reduce(links, path, 1536, xf, 1536 * p, x_work, x_recv, None, 1536 * p)
        for p, path in enumerate(SEQ_PATHS)
    ]
    summing = reduce_steps(sums)
    first_weights = reduce_steps(x_jobs)
    advance(summing, first_weights)
    put_wide(wide, out_acc[...])
    advance(summing, first_weights, summing)
    back_again = gather_steps(sums)
    advance(back_again, back_again, first_weights, back_again)

    low = (cot_ref[...].astype(F32) + d_sum[...].astype(F32)).astype(BF16)
    scale = lax.rsqrt(column_of(squares[...]) / (MAMBA_HEADS * MP) + EPSILON)
    d_gated[...] = nt(low, wmo[...])
    product = d_gated[...] * mixed[...]
    own_inner[...] = row_sums(product * mgain[...].reshape(1, MW))
    slots[links.h] = own_inner[...]
    copies = [links.send(own_inner, slots.at[links.h], name) for name in ("x1", "x2", "x3")]
    mixgain[...] = jnp.broadcast_to(jnp.sum(product * scale, axis=0, keepdims=True), mixgain.shape)
    for cb in range(4):
        lanes = slice(256 * cb, 256 * cb + 256)
        xb[pl.ds(512 * cb, MW)] = tn(gated[...], low[:, lanes]).astype(BF16)
        xb[pl.ds(512 * cb + MW, 128)] = tn(attended[...], low[:, lanes]).astype(BF16)
    d_att[...] = nt(low, wao[...]).astype(BF16)

    xb_jobs = [
        Reduce(links, path, 512, xb, 512 * p, xb_work, xb_recv, None, 512 * p)
        for p, path in enumerate(SEQ_PATHS)
    ]
    shares = [
        Reduce(links, path, 512, wide, 512 * p, wide_work, wide_recv, None, 512 * p)
        for p, path in enumerate(HEAD_PATHS)
    ]
    others = [first_weights, reduce_steps(xb_jobs), reduce_steps(shares)]
    advance(*others)
    for copy in copies:
        copy.wait()

    inner_col = column_of((slots[0] + slots[1]) + (slots[2] + slots[3]))
    d_mixed = scale * (d_gated[...] * mgain[...].reshape(1, MW)) - mixed[...] * (
        scale * scale * scale / (MAMBA_HEADS * MP) * inner_col
    )
    z = gz[...]
    sig = sigmoid(z)
    ds = d_mixed * (z * sig)
    d_ssd[...] = ds
    d_z[...] = (d_mixed * ssd[...] * (sig * (1.0 + z * (1.0 - sig)))).astype(BF16)
    step_x, enter_x, _ = decay_terms(decay, cum_ref)
    b, c = post[:, pl.ds(MW, NS)], post[:, pl.ds(MW + NS, NS)]
    entered = (ds * enter_x).astype(BF16)
    local[...] = tn(entered, c).astype(BF16)
    leaving_all = scan_steps(
        links, local, logs_all, sibling, row_slots, plane_slots, halves, leaving, False
    )
    advance(leaving_all)
    mixer_in = post[:, pl.ds(0, MW)].astype(F32)
    skip_part[...] = jnp.broadcast_to(jnp.sum(ds * mixer_in, axis=0, keepdims=True), skip_part.shape)
    scaled = (mixer_in * step_x).astype(BF16)
    gram = nt(c, b)
    mask = lower_mask()
    cum, cum_t = cum_ref[...], cumt_ref[...]
    left = lax.broadcasted_iota(jnp.int32, (ROWS, 128), 1) < MP
    low = ds.astype(BF16)
    d_gram = jnp.zeros((ROWS, ROWS), F32)
    for pair in range(3):
        lanes = slice(128 * pair, 128 * pair + 128)
        halves = []
        for k in range(2):
            decay = decay_of(cum, cum_t, 2 * pair + k, mask)
            here = left if k == 0 else jnp.logical_not(left)
            mine = jnp.where(here, ds[:, lanes], 0.0).astype(BF16)
            halves.append(tn((gram * decay).astype(BF16), low[:, lanes]))
            d_gram = d_gram + decay * nt(mine, scaled[:, lanes])
        d_scaled[:, pl.ds(128 * pair, 128)] = jnp.where(left, halves[0], halves[1])
    d_gram = d_gram.astype(BF16)
    d_bc[:, pl.ds(0, NS)] = tn(d_gram, c)
    d_bc[:, pl.ds(NS, NS)] = nn(d_gram, b) + nn(entered, state[...])

    qp[...] = stacked_queries(q[...])
    d_out = d_att[...].astype(F32)
    dop[...] = jnp.concatenate(
        [jnp.where(left, 0.0, pltpu.roll(d_out, HD, 1)), jnp.where(left, 0.0, d_out)], axis=0
    ).astype(BF16)
    product = (d_out * attended_f[...]).T
    delta = jnp.concatenate(
        [
            jnp.sum(product[:HD], axis=0, keepdims=True),
            jnp.sum(product[HD:], axis=0, keepdims=True),
        ],
        axis=1,
    )
    total = totals[pl.ds(0, 1)]
    pairs[...] = jnp.zeros_like(pairs)

    def block_grads(j, masked):
        block = load_block(kv_all, j)
        scores = nt(block, qp[...])
        if masked:
            scores = causal(scores)
        probs = jnp.exp(scores - total)
        d_probs = nt(block, dop[...])
        d_scores = (probs * (d_probs - delta)).astype(BF16)
        d_pair = (nn(d_scores, qp[...]) + nn(probs.astype(BF16), dop[...])).astype(BF16)
        for p in range(4):
            at = rows_at(2048 * p + block_position(j, p) * 64, 64)
            pairs[at] = d_pair[64 * p : 64 * p + 64]
        return tn(block, d_scores)

    acc[...] = block_grads(s, True)

    def hop(i, carry):
        acc[...] += block_grads(2 * i, False) + block_grads(2 * i + 1, False)
        return carry

    def last_hop(i, carry):
        acc[...] += block_grads(s - 1, False)
        return carry

    hops, turns = s // 2, 5
    for turn in range(turns):
        advance(leaving_all, *others)
        lax.fori_loop((hops * turn) // turns, (hops * (turn + 1)) // turns, hop, 0)
    lax.fori_loop(0, s % 2, last_hop, 0)
    out = acc[pl.ds(0, HD)] * (HD ** -0.5)
    d_q[...] = jnp.concatenate([out[:, :ROWS], out[:, ROWS:]], axis=0).T.astype(BF16)
    finish(leaving_all)
    finish(*others)
    for p, job in enumerate(shares):
        share[pl.ds(128 * p, 128)] = own_rows(job, 128)
    for p, job in enumerate(xb_jobs):
        xb_piece[pl.ds(16 * p, 16)] = own_rows(job, 16)
    for p, job in enumerate(x_jobs):
        x_piece[pl.ds(48 * p, 48)] = own_rows(job, 48)


LAST_NAMES = SEQ_NAMES + ("next", "prev", "x1", "x2", "x3")


def last_kernel(
    pairs, leaving, d_ssd, d_scaled, d_bc, skip, decay, cum, post, pre, ext, taps_m, taps_s, d_z, d_q,
    normed, x_ref, gain, wm, ws, wq, kvw, second_part, mixgain, skip_part, x_piece, xb_piece,
    x_out, xb_out, zq_out, mix_out, st_out, kv_out, share, small_out,
    pair_work, pair_recv, d_pre, edge_in, shifted, d_all, acc, kernel_grads,
    zq, zq_work, zq_recv, mix, mix_work, mix_recv, st, st_work, st_recv, kv, kv_work, kv_recv,
    wide, wide_work, wide_recv, st_slots, kv_slots, small_work, small_slots, send_sem, recv_sem,
):
    links = Links(send_sem, recv_sem)
    s = links.s
    links.greet(LAST_NAMES)
    links.met(LAST_NAMES)

    def reduces(paths, rows, src, work, recv):
        return [
            Reduce(links, path, rows, src, rows * k, work, recv, None, rows * k)
            for k, path in enumerate(paths)
        ]

    pair_jobs = reduces(SEQ_PATHS, 2048, pairs, pair_work, pair_recv)
    pairing = reduce_steps(pair_jobs)
    advance(pairing)
    feed_weights = gather_steps(gather_rows(links, x_piece, x_out))
    output_weights = gather_steps(gather_rows(links, xb_piece, xb_out))

    step_x, _, tail_x = decay_terms(decay, cum)
    b = post[:, pl.ds(MW, NS)]
    mixer_in = post[:, pl.ds(0, MW)].astype(F32)
    tail_in = (mixer_in * step_x * tail_x).astype(BF16)
    scaled_grad = d_scaled[...] + tail_x * nt(b, leaving[...])
    d_pre[:, pl.ds(0, MW)] = widen(skip[...]) * d_ssd[...] + scaled_grad * step_x
    d_pre[:, pl.ds(MW, NS)] = d_bc[:, pl.ds(0, NS)] + nn(tail_in, leaving[...])
    d_pre[:, pl.ds(MW + NS, NS)] = d_bc[:, pl.ds(NS, NS)]
    for c in range(5):
        lanes = pl.ds(128 * c, 128)
        v = pre[:, lanes]
        sig = sigmoid(v)
        dp = d_pre[:, lanes] * (sig * (1.0 + v * (1.0 - sig)))
        d_pre[:, lanes] = dp
    edge_copy = links.send(d_pre.at[pl.ds(0, 8)], edge_in, "prev")
    advance(pairing, feed_weights)
    for c in range(5):
        lanes = pl.ds(128 * c, 128)
        dp = d_pre[:, lanes]
        rows = [jnp.sum(dp * ext[pl.ds(13 + k, ROWS), lanes], axis=0, keepdims=True) for k in range(KC)]
        rows.append(jnp.sum(dp, axis=0, keepdims=True))
        rows.append(jnp.zeros((3, 128), F32))
        kernel_grads[:, lanes] = jnp.concatenate(rows, axis=0)
    d_all[:, pl.ds(0, MW)] = d_z[...]
    d_all[:, pl.ds(MW, 128)] = d_q[...]

    def early(i, carry):
        rows = pl.ds(pl.multiple_of(i * 256, 256), 256)
        block = tn(normed[:, rows], d_all[:, pl.ds(0, 512)]).astype(BF16)
        for k in range(4):
            zq[rows_at(1024 * k + i * 256, 256)] = block[:, 128 * k : 128 * k + 128]
        acc[:, rows] = nt(d_all[:, pl.ds(0, MW)], wm[0, rows]) + nt(d_all[:, pl.ds(MW, 128)], wq[rows])
        return carry

    lax.fori_loop(0, 4, early, 0)
    zq_jobs = reduces(SHORT_PATHS, 2048, zq, zq_work, zq_recv)

    def gate_weights():
        yield from reduce_steps(zq_jobs)
        for job in zq_jobs:
            at = rows_at(job.base + job.start, 64)
            zq_out[at] = zq_work[at]
            job.out = zq_out
        yield from gather_steps(zq_jobs)

    zq_weights = gate_weights()
    advance(zq_weights, pairing, feed_weights, output_weights)
    edge_copy.wait()
    keep = jnp.where(s < SEQ - 1, 1.0, 0.0)
    shifted[pl.ds(0, ROWS)] = d_pre[...]
    shifted[pl.ds(ROWS, 8)] = edge_in[...] * keep
    for c in range(5):
        lanes = pl.ds(128 * c, 128)
        taps, own = of_channels(taps_m, taps_s, c)
        total = taps[pl.ds(0, 1), own] * shifted[pl.ds(3, ROWS), lanes]
        for k in range(1, KC):
            total = total + taps[pl.ds(k, 1), own] * shifted[pl.ds(3 - k, ROWS), lanes]
        d_all[:, pl.ds(512 + 128 * c, 128)] = total.astype(BF16)

    def middle(i, carry):
        rows = pl.ds(pl.multiple_of(i * 256, 256), 256)
        block = tn(normed[:, rows], d_all[:, pl.ds(512, CW)]).astype(BF16)
        mix[rows] = block[:, :MW]
        st[rows] = block[:, MW:]
        return carry

    lax.fori_loop(0, 4, middle, 0)
    mix_jobs = reduces(SHORT_PATHS, 512, mix, mix_work, mix_recv)
    st_jobs = reduces(SHORT_PATHS, 512, st, st_work, st_recv)

    def mixer_weights():
        yield from reduce_steps(mix_jobs + st_jobs)
        for k, job in enumerate(st_jobs):
            st_slots[links.h, pl.ds(16 * k, 16)] = own_rows(job, 16)
        slot = st_slots.at[links.h]
        copies = [links.send(slot, slot, name) for name in ("x1", "x2", "x3")]
        for job in mix_jobs:
            at = rows_at(job.base + job.start, 16)
            mix_out[at] = mix_work[at]
            job.out = mix_out
        yield
        for copy in copies:
            copy.wait()
        for k, job in enumerate(st_jobs):
            at = rows_at(job.base + job.start, 16)
            parts = [st_slots[j, pl.ds(16 * k, 16)].astype(F32) for j in range(HEADS)]
            st_out[at] = ((parts[0] + parts[1]) + (parts[2] + parts[3])).astype(BF16)
            job.out = st_out
        yield from gather_steps(mix_jobs + st_jobs)

    mixing = mixer_weights()
    advance(mixing, pairing)

    def late_part(i, carry):
        rows = pl.ds(pl.multiple_of(i * 256, 256), 256)
        total = acc[:, rows] + nt(d_all[:, pl.ds(512, MW)], wm[1, rows])
        acc[:, rows] = total + nt(d_all[:, pl.ds(512 + MW, 256)], ws[rows])
        return carry

    lax.fori_loop(0, 4, late_part, 0)
    advance(zq_weights, feed_weights, output_weights)
    finish(pairing)
    for p, job in enumerate(pair_jobs):
        d_all[pl.ds(64 * p, 64), pl.ds(1152, 128)] = own_rows(job, 64)
    left = lax.broadcasted_iota(jnp.int32, (ROWS, 128), 1) < HD
    d_pair = d_all[:, pl.ds(1152, 128)].astype(F32)
    other = pltpu.roll(d_pair, HD, 1)
    zero = jnp.zeros_like(d_pair)
    low_head = links.h < 2
    d_keys = jnp.where(low_head, jnp.where(left, d_pair, zero), jnp.where(left, zero, other)).astype(BF16)
    d_values = jnp.where(low_head, jnp.where(left, other, zero), jnp.where(left, zero, d_pair)).astype(BF16)

    def pair_part(i, carry):
        rows = pl.ds(pl.multiple_of(i * 256, 256), 256)
        kv[rows] = tn(normed[:, rows], d_all[:, pl.ds(1152, 128)]).astype(BF16)
        acc[:, rows] += nt(d_keys, kvw[0, rows]) + nt(d_values, kvw[1, rows])
        return carry

    lax.fori_loop(0, 4, pair_part, 0)
    kv_jobs = reduces(SHORT_PATHS, 512, kv, kv_work, kv_recv)

    def head_weights():
        yield from reduce_steps(kv_jobs)
        for k, job in enumerate(kv_jobs):
            kv_slots[links.h, pl.ds(16 * k, 16)] = own_rows(job, 16)
        slot = kv_slots.at[links.h]
        copies = [links.send(slot, slot, name) for name in ("x1", "x2", "x3")]
        yield
        for copy in copies:
            copy.wait()
        for k, job in enumerate(kv_jobs):
            at = rows_at(job.base + job.start, 16)
            parts = [kv_slots[j, pl.ds(16 * k, 16)].astype(F32) for j in range(HEADS)]
            kv_out[at, pl.ds(0, 128)] = (parts[0] + parts[1]).astype(BF16)
            kv_out[at, pl.ds(128, 128)] = (parts[2] + parts[3]).astype(BF16)
            job.out = kv_out
        yield from gather_steps(kv_jobs)

    heading = head_weights()
    advance(heading)
    x = x_ref[...].astype(F32)
    r1 = lax.rsqrt(jnp.mean(x * x, axis=1, keepdims=True) + EPSILON)
    d_normed = acc[...]
    blank = jnp.zeros((1, 256), F32)
    grads = kernel_grads[...]
    vector_rows = [
        [jnp.sum(d_normed * x * r1, axis=0, keepdims=True)],
        [second_part[pl.ds(0, 1)]],
        [grads[k : k + 1, MW:] for k in range(KC)],
        [grads[KC : KC + 1, MW:], blank, blank, blank],
        [grads[0:1, :MW], grads[KC : KC + 1, :MW], blank],
        [grads[1:2, :MW], mixgain[pl.ds(0, 1)], blank],
        [grads[2:3, :MW], skip_part[pl.ds(0, 1)], blank],
        [grads[3:4, :MW], blank, blank, blank[:, :128]],
    ]
    small_work[0] = jnp.concatenate([jnp.concatenate(row, axis=1) for row in vector_rows], axis=0)

    def vectors():
        at = 0
        for names, me in (
            (("c",), links.bits["c"]),
            (("y41", "y42", "y43"), links.bits["y4"]),
            (("z41", "z42", "z43"), links.bits["z4"]),
            (("x1", "x2", "x3"), links.h),
        ):
            step, count = at, len(names) + 1
            slots = small_slots.at[pl.ds(4 * step, 4)]
            slots[me] = small_work[step]
            copies = [links.send(small_work.at[step], slots.at[me], name) for name in names]
            yield
            for copy in copies:
                copy.wait()
            total = slots[0] + slots[1]
            if count == 4:
                total = total + (slots[2] + slots[3])
            small_work[step + 1] = total
            at += 1
        row = lax.broadcasted_iota(jnp.int32, (8, 1024), 0)
        small_out[...] = jnp.where(row < 4, small_work[4], small_work[3])

    adding = vectors()
    advance(adding)
    weighted = d_normed * gain[...]
    inner = jnp.sum(weighted * x, axis=1, keepdims=True)
    put_wide(wide, r1 * weighted - x * (r1 * r1 * r1 / D * inner))
    shares = [
        Reduce(links, path, 512, wide, 512 * p, wide_work, wide_recv, None, 512 * p)
        for p, path in enumerate(HEAD_PATHS)
    ]
    sharing = reduce_steps(shares)
    advance(sharing)
    finish(heading, adding, mixing, sharing, zq_weights, feed_weights, output_weights)
    for p, job in enumerate(shares):
        share[pl.ds(128 * p, 128)] = own_rows(job, 128)


def widths_kernel(
    h, down0, down1, down2, down3, gate0, gate1, up0, up1, mix0, mix1, mix2, mix3, z0, z1, z2, query_in,
    raw_in, state_in, keyval_in, x_ref, summed, out_share, cot, d_sum, in_share, small,
    down, gateup, mixout, attn, mixer, query, keyval, state, block_out, input_grads,
    gain, second, kernel_m, kernel_s, bias_m, bias_s, skip, mgain,
):
    i = pl.program_id(0)
    for cb, block in enumerate((down0, down1, down2, down3)):
        down[:, pl.ds(256 * cb, 256)] = block[...].astype(F32)
    for cb, block in enumerate((gate0, gate1)):
        gateup[0, :, pl.ds(256 * cb, 256)] = block[...].astype(F32)
    for cb, block in enumerate((up0, up1)):
        gateup[1, :, pl.ds(256 * cb, 256)] = block[...].astype(F32)

    @pl.when(i < 3)
    def _():
        for cb, block in enumerate((mix0, mix1, mix2, mix3)):
            mixout[:, pl.ds(256 * cb, 256)] = block[...].astype(F32)

    @pl.when(i == 3)
    def _():
        for cb, block in enumerate((mix0, mix1, mix2, mix3)):
            attn[:, pl.ds(256 * cb, 256)] = block[...].astype(F32)

    for k, block in enumerate((z0, z1, z2)):
        mixer[0, :, pl.ds(128 * k, 128)] = block[...].astype(F32)
    mixer[1] = raw_in[...].astype(F32)
    state[...] = state_in[...].astype(F32)
    query[...] = query_in[...].astype(F32)
    left = lax.broadcasted_iota(jnp.int32, (256, 128), 1) < HD
    first, second_head = keyval_in[:, pl.ds(0, 128)].astype(F32), keyval_in[:, pl.ds(128, 128)].astype(F32)
    keyval[0] = jnp.where(left, first, pltpu.roll(second_head, HD, 1))
    keyval[1] = jnp.where(left, pltpu.roll(first, HD, 1), second_head)
    block_out[...] = x_ref[...].astype(F32) + summed[...].astype(F32) + out_share[...].astype(F32)
    input_grads[...] = cot[...].astype(F32) + d_sum[...].astype(F32) + in_share[...].astype(F32)

    @pl.when(i == 0)
    def _():
        gain[...] = small[pl.ds(0, 1)]
        second[...] = small[pl.ds(1, 1)]
        kernel_m[...] = small[pl.ds(4, KC), pl.ds(0, MW)]
        for k in range(KC):
            kernel_s[pl.ds(k, 1)] = small[pl.ds(2, 1), pl.ds(256 * k, 256)]
        bias_m[...] = small[4, pl.ds(MW, MW)]
        bias_s[...] = small[pl.ds(3, 1), pl.ds(0, 256)]
        skip[...] = exact(small[pl.ds(6, 1), pl.ds(MW, MW)], head_spread(), ((1,), (1,)))
        mgain[...] = small[5, pl.ds(MW, MW)]


def widened(h, x_out, xb_out, zq_out, mix_out, st_out, kv_out, x_ref, summed, out_share, cot, d_sum, in_share, small):
    def rows(count, width, offset=0):
        return pl.BlockSpec((count, width), lambda i, h: (i + offset, 0))

    def halves(count, width):
        return pl.BlockSpec((2, count, width), lambda i, h: (0, i, 0))

    def whole(count, width):
        return pl.BlockSpec((count, width), lambda i, h: (0, 0))

    def line(width):
        return pl.BlockSpec((width,), lambda i, h: (0,))

    own = pl.BlockSpec((64, 256), lambda i, h: (i, h[0]))
    grid = pltpu.PrefetchScalarGridSpec(
        num_scalar_prefetch=1,
        grid=(4,),
        in_specs=[rows(128, 256, 12 * cb) for cb in range(4)]
        + [rows(256, 256, 6 * cb + 2) for cb in range(4)]
        + [rows(128, 256, 4 * cb) for cb in range(4)]
        + [rows(256, 128, 4 * k) for k in range(4)]
        + [rows(256, MW), rows(256, 256), rows(256, 256)]
        + [own, own, rows(64, 256), own, own, rows(64, 256), whole(8, D)],
        out_specs=(
            rows(128, D), halves(256, 512),
            pl.BlockSpec((128, D), lambda i, h: (jnp.minimum(i, 2), 0)), whole(128, D),
            halves(256, MW), rows(256, 128), halves(256, 128), rows(256, 256),
            rows(64, 256), rows(64, 256),
            whole(1, D), whole(1, D), whole(KC, MW), whole(KC, 256), line(MW), whole(1, 256),
            whole(1, HMH), line(MW),
        ),
    )
    return pl.pallas_call(
        widths_kernel,
        grid_spec=grid,
        out_shape=(
            shape((512, D), F32), shape((2, D, 512), F32), shape((MW, D), F32), shape((128, D), F32),
            shape((2, D, MW), F32), shape((D, 128), F32), shape((2, D, 128), F32), shape((D, 256), F32),
            shape((ROWS, 256), F32), shape((ROWS, 256), F32),
            shape((1, D), F32), shape((1, D), F32), shape((KC, MW), F32), shape((KC, 256), F32),
            shape((MW,), F32), shape((1, 256), F32), shape((1, HMH), F32), shape((MW,), F32),
        ),
        compiler_params=pltpu.CompilerParams(vmem_limit_bytes=VMEM_LIMIT),
    )(
        h, *[x_out] * 8, *[xb_out] * 4, *[zq_out] * 4, mix_out, st_out, kv_out, x_ref, summed, out_share, cot,
        d_sum, in_share, small,
    )


SCAN_SCRATCH = (
    pltpu.VMEM((MW, NS), BF16), pltpu.VMEM((MW, NS), BF16), pltpu.VMEM((4, MW // 2, NS), BF16),
    pltpu.VMEM((4, MW // 2, NS), BF16), pltpu.VMEM((MW, NS), BF16),
)


def on_device(
    hidden_in, cotangent, log_decay, norm_gain, query_weight, keyvalue_weight, attention_output,
    mixer_weight, state_weight, kernel_mixer, kernel_state, bias_mixer, bias_state, skip_gain,
    mixer_gain, mixer_output, second_gain, gate_up, down_weight,
):
    gain1 = norm_gain.reshape(1, D)
    gain2 = second_gain.reshape(1, D)
    mgain = mixer_gain
    skip = skip_gain.reshape(1, HMH)
    bias_m, bias_s = bias_mixer, bias_state.reshape(1, 256)
    (
        cum, cum_t, normed, q, kv_all, logs_all, gz, ext, pre, post, attended, attended_f, totals, ssd, mixed,
        squares, state, gated, summed,
    ) = call(
        forward_kernel,
        [
            shape((ROWS, HMH), F32), shape((HMH, ROWS), F32),
            shape((ROWS, D), BF16), shape((ROWS, 128), BF16), shape((8192, 128), BF16),
            shape((256, 128), F32), shape((ROWS, MW), F32), shape((ROWS + 16, CW), F32),
            shape((ROWS, CW), F32), shape((ROWS, CW), BF16), shape((ROWS, 128), BF16),
            shape((ROWS, 128), F32), shape((8, 512), F32), shape((ROWS, MW), F32),
            shape((ROWS, MW), F32), shape((8, ROWS), F32), shape((MW, NS), BF16),
            shape((ROWS, MW), BF16), shape((ROWS, D), BF16),
        ],
        (
            hidden_in, gain1, query_weight, keyvalue_weight, mixer_weight, state_weight, kernel_mixer,
            kernel_state, bias_m, bias_s, log_decay, skip, mgain, mixer_output, attention_output,
        ),
        scratch=[
            pltpu.VMEM((ROWS, 128), BF16), pltpu.VMEM((8, 128), F32),
            pltpu.VMEM((16, D), BF16), pltpu.VMEM((16, D), BF16),
            *SCAN_SCRATCH,
            pltpu.VMEM((512, 128), BF16), pltpu.VMEM((128, 512), F32), pltpu.VMEM((8, ROWS), F32),
            pltpu.VMEM((HEADS, 8, ROWS), F32), pltpu.VMEM((ROWS, D), F32),
            pltpu.VMEM((ROWS, D), BF16), pltpu.VMEM((ROWS, D), BF16), pltpu.VMEM((ROWS, D), BF16),
        ],
        collective=1, copies=80, limit=60 * 1024 * 1024,
    )
    (
        d_sum, out_share, x_piece, xb_piece, second_part, mixgain, d_z, d_ssd, skip_part, d_scaled, d_bc, leaving,
        d_q, pairs,
    ) = call(
        middle_kernel,
        [
            shape((ROWS, D), BF16), shape((ROWS, 256), BF16), shape((192, 256), BF16),
            shape((64, 256), BF16),
            shape((8, D), F32), shape((8, MW), F32), shape((ROWS, MW), BF16), shape((ROWS, MW), F32),
            shape((8, MW), F32), shape((ROWS, MW), F32), shape((ROWS, 256), F32),
            shape((MW, NS), BF16), shape((ROWS, 128), BF16), shape((8192, 128), BF16),
        ],
        (
            hidden_in, summed, cotangent, gain2, gate_up, down_weight, gated, attended, mixer_output,
            attention_output, mixed, squares, mgain, gz, ssd, post, log_decay, cum, cum_t, state, q, kv_all,
            attended_f, totals, logs_all,
        ),
        scratch=[
            pltpu.VMEM((ROWS, D), BF16), pltpu.VMEM((ROWS, D), F32), pltpu.VMEM((ROWS, D), F32),
            pltpu.VMEM((ROWS, D), BF16), pltpu.VMEM((1024, 256), BF16), pltpu.VMEM((6144, 256), BF16),
            pltpu.VMEM((2048, 256), BF16), pltpu.VMEM((ROWS, D), BF16), pltpu.VMEM((ROWS, D), BF16),
            pltpu.VMEM((1024, 256), BF16), pltpu.VMEM((1024, 256), BF16),
            pltpu.VMEM((6144, 256), BF16), pltpu.VMEM((6144, 256), BF16),
            pltpu.VMEM((2048, 256), BF16), pltpu.VMEM((2048, 256), BF16),
            pltpu.VMEM((ROWS, 128), BF16), pltpu.VMEM((ROWS, MW), F32), pltpu.VMEM((8, ROWS), F32),
            pltpu.VMEM((HEADS, 8, ROWS), F32), pltpu.VMEM((MW, NS), BF16),
            *SCAN_SCRATCH[1:], pltpu.VMEM((512, 128), BF16),
            pltpu.VMEM((512, 128), BF16), pltpu.VMEM((128, 512), F32),
        ],
        collective=2, copies=150,
    )
    x_out, xb_out, zq_out, mix_out, st_out, kv_out, in_share, small = call(
        last_kernel,
        [
            shape((6144, 256), BF16), shape((2048, 256), BF16), shape((4096, 128), BF16),
            shape((D, MW), BF16), shape((D, 256), BF16), shape((D, 256), BF16),
            shape((ROWS, 256), BF16), shape((8, D), F32),
        ],
        (
            pairs, leaving, d_ssd, d_scaled, d_bc, skip, log_decay, cum, post, pre, ext, kernel_mixer,
            kernel_state, d_z, d_q, normed, hidden_in, gain1, mixer_weight, state_weight, query_weight,
            keyvalue_weight, second_part, mixgain, skip_part, x_piece, xb_piece,
        ),
        scratch=[
            pltpu.VMEM((8192, 128), BF16), pltpu.VMEM((8192, 128), BF16), pltpu.VMEM((ROWS, CW), F32),
            pltpu.VMEM((8, CW), F32), pltpu.VMEM((ROWS + 8, CW), F32), pltpu.VMEM((ROWS, 1280), BF16),
            pltpu.VMEM((ROWS, D), F32), pltpu.VMEM((8, CW), F32),
            *[pltpu.VMEM((4096, 128), BF16)] * 3, *[pltpu.VMEM((D, MW), BF16)] * 3,
            *[pltpu.VMEM((D, 256), BF16)] * 3, *[pltpu.VMEM((D, 128), BF16)] * 3,
            *[pltpu.VMEM((D, 256), BF16)] * 3,
            pltpu.VMEM((HEADS, 32, 256), BF16), pltpu.VMEM((HEADS, 32, 128), BF16),
            pltpu.VMEM((5, 8, D), F32), pltpu.VMEM((16, 8, D), F32),
        ],
        collective=3, copies=230,
    )
    h = lax.axis_index("head").astype(jnp.int32).reshape(1)
    (
        down, gateup, mixout, attn, mixer, query, keyval, state_grads, block_out, input_grads,
        gain_grads, second_grads, mixkernel, statekernel, mixbias, statebias, skip_grads, mixgain_grads,
    ) = widened(
        h, x_out, xb_out, zq_out, mix_out, st_out, kv_out, hidden_in, summed, out_share, cotangent,
        d_sum, in_share, small,
    )
    return (
        block_out,
        input_grads,
        gain_grads.reshape(D),
        query,
        keyval,
        attn,
        mixer,
        state_grads,
        mixkernel,
        statekernel,
        mixbias,
        statebias.reshape(256),
        skip_grads.reshape(HMH),
        mixgain_grads,
        mixout,
        second_grads.reshape(D),
        gateup,
        down,
    )


def solution(mesh):
    return jax.shard_map(
        on_device,
        mesh=mesh,
        in_specs=(
            P("seq", None), P("seq", None), P("seq", "head"), P(), P(None, "head"), P(),
            P("head", None), P(None, None, "head"), P(), P(None, "head"), P(), P("head"), P(),
            P("head"), P("head"), P("head", None), P(), P(None, None, "head"), P("head", None),
        ),
        out_specs=(
            P("seq", "head"), P("seq", "head"), P(), P(None, "head"), P(), P("head", None),
            P(None, None, "head"), P(), P(None, "head"), P(), P("head"), P(), P("head"), P("head"),
            P("head", None), P(), P(None, None, "head"), P("head", None),
        ),
        check_vma=False,
    )
```
